32 devices in a mesh: obs: 2 (over core), horiz: 16 (over z, y, x).
Axes of the slice: x: 2, y: 2, z: 4, core: 2. Of those that a mesh axis runs over, the one named last changes fastest.
Arguments:
- control: float32 [128, 16, 4096], P(None, 'obs', 'horiz'), may hold values from -6 to 6
- spread: float32 [128, 16, 4096], P(None, 'obs', 'horiz'), may hold values from 0.3 to 3
- vert_root: float32 [128, 128], replicated, as said below
- wind_lon: float32 [128, 16, 4096], P('horiz', 'obs'), may hold values from -0.45 to 0.45
- wind_lat: float32 [128, 16, 4096], P('horiz', 'obs'), may hold values from -0.45 to 0.45
- obs_dest: int32 [32768, 1], P(('obs', 'horiz')), may hold values from 0 to 15; in each aligned block of 1024 rows (0 to 1023, 1024 to 2047, ...) at most 64 rows name the same one
- obs_cells: int32 [4, 32768], P(None, ('obs', 'horiz')), may hold values from 0 to 262143
- obs_time: int32 [32768], P(('obs', 'horiz')), may hold values from 0 to 4
- obs_value: float32 [32768], P(('obs', 'horiz')), may hold values from -6 to 6
- obs_weight: float32 [4, 32768], P(None, ('obs', 'horiz')), may hold values from 0 to 1
- obs_rinv: float32 [32768], P(('obs', 'horiz')), may hold values from 0.3 to 3
Outputs:
- gradient: float32 [128, 16, 4096], P(None, 'obs', 'horiz')
- departure: float32 [32768], P(('obs', 'horiz'))
The draws below stay inside these ranges and needn't reach their ends.
Inputs may be any that keep to these rules, and one draw needn't show every extreme that they name: `obs_dest`: in the rows of one device at most 64 observations name the same level group, a bound that some block reaches. `obs_cells`: cell index within the owner's block of 128 / 16 levels, 8 rows and 4096 longitudes, flattened in that order. `vert_root`: zero beyond 12 places from the diagonal; diagonal entries from 1 to 1.5.
All inputs are finite; a program needn't handle non-finite values.
Results may differ from the reference program's by a relative error of at most 0.00012.
Values sent between devices are 32-bit elements; how exact they have to be, the bound alone decides.
No kernel may reach another device: no remote copies, remote signals or barrier semaphores. Data moves between devices by JAX's collectives and lax.ppermute only.
A program may use at most 64 MiB of HBM per device.

```python
import math
import jax
import jax.numpy as jnp
import numpy as np
from jax import lax

LEV = 128
CLAT = 8
NLON = 4096
NT = 4
VBAND = 12
NOBS_DEV = 1024
CAP = 64
NLAT = 16
NOBS = 32768
N_HORIZ = 16


def draw_vert_root(key, part):
    first_key, second_key = jax.random.split(jax.random.fold_in(key, 17))
    row_index = jnp.arange(LEV)[:, None]
    col_index = jnp.arange(LEV)[None, :]
    off_band = jax.random.uniform(first_key, (LEV, LEV), jnp.float32, -0.3, 0.3)
    diagonal = jax.random.uniform(second_key, (LEV, LEV), jnp.float32, 1.0, 1.5)
    inside = jnp.abs(row_index - col_index) <= VBAND
    return jnp.where(row_index == col_index, diagonal, jnp.where(inside, off_band, 0.0)).astype(jnp.float32)


def place_ends(values, rng, smallest, high):
    dims = values.shape
    place = [jax.random.randint(jax.random.fold_in(rng, axis), (), 0, dims[axis]) for axis in range(len(dims))]
    values = values.at[tuple(place)].set(smallest)
    longest = dims.index(max(dims))
    place[longest] = (place[longest] + 1) % dims[longest]
    return values.at[tuple(place)].set(high)


def block_scale(stream_key, shape, cuts, least, top_value):
    def one(dim, parts):
        heights = jax.random.uniform(jax.random.fold_in(jax.random.fold_in(stream_key, 6), dim), (parts,), jnp.float32, least / len(cuts), top_value / len(cuts))
        return jnp.repeat(jnp.exp(heights), shape[dim] // parts).reshape((-1,) + (1,) * (len(shape) - dim - 1))

    loudness = one(*cuts[0])
    for cut in cuts[1:]:
        loudness = loudness * one(*cut)
    return loudness


def assign_block(rng, own, number, rows, amount, top, limit, slope):
    ranking = jax.random.permutation(rng, amount)
    crowded, usual = portions_of(amount, rows * top, limit, slope, True), portions_of(amount, rows * top, limit, slope, False)
    places = jnp.arange(amount)

    def named(tallies, rotation):
        used = int((tallies > 0).sum())
        fixed = max(1, used // 4)
        shifted = fixed + (places - fixed + rotation * (used - fixed)) % max(1, amount - fixed)
        return jnp.zeros((amount,), jnp.int32).at[ranking[jnp.where(places < fixed, places, shifted)]].set(jnp.asarray(tallies, jnp.int32))

    tallies = jnp.where(number % 4 == 0, named(crowded, number // 4), named(usual, number - number // 4 - 1))
    mixed = jax.random.permutation(jax.random.fold_in(own, 3), amount)
    donor, receiver = mixed[0:amount // 2 * 2:2], mixed[1:amount // 2 * 2:2]
    margin = jnp.minimum(tallies[donor] - 1, limit - tallies[receiver]) // 2
    margin = jnp.where((donor == ranking[0]) | (receiver == ranking[0]) | (tallies[receiver] == 0), 0, jnp.maximum(margin, 0))
    shifted = jax.random.randint(jax.random.fold_in(own, 4), (amount // 2,), 0, 1 << 20) % (margin + 1)
    tallies = tallies.at[donor].add(-shifted).at[receiver].add(shifted)
    items = jnp.searchsorted(jnp.cumsum(tallies), jnp.arange(rows * top), side="right").astype(jnp.int32)
    grid = items.reshape(top, rows).T
    grid = grid[jax.random.permutation(jax.random.fold_in(own, 1), rows)]
    rotation = jax.random.randint(jax.random.fold_in(own, 2), (rows, 1), 0, top)
    return jnp.take_along_axis(grid, (jnp.arange(top)[None, :] + rotation) % top, axis=1)


def portions_of(number_of, total, most, lean, full):
    portions = [(1 << 20) // math.isqrt(rank ** lean) + 1 for rank in range(1, number_of + 1)]
    largest = most if full else min(most, max(-(-total // number_of), total * portions[0] // sum(portions)))
    least = 1 if total - largest >= number_of - 1 else 0
    holding, spare = [largest] + [least] * (number_of - 1), total - largest - least * (number_of - 1)
    while spare > 0:
        movable = [i for i in range(1, number_of) if holding[i] < largest] or [i for i in range(1, number_of) if holding[i] < most]
        whole, remaining = sum([portions[i] for i in movable]), spare
        for i in movable:
            extra = min(most - holding[i], max(1, remaining * portions[i] // whole), spare)
            holding[i] = holding[i] + extra
            spare = spare - extra
    return np.array(holding)


def normal_values(stream_key, extent, scale, reach, shards=(), kind=jnp.bfloat16):
    factor_of = block_scale(stream_key, extent, shards, -0.22, 0.18) if shards else 1.0
    result = jax.random.normal(stream_key, extent, jnp.float32) * scale * factor_of
    return jnp.minimum(jnp.maximum(result, -reach), reach).astype(kind)


def setup_inputs(seed: int = 0) -> dict:
    splits = jax.random.split(jax.random.key(seed), 12)
    control = normal_values(splits[0], (LEV, NLAT, NLON), 1.0, 6.0, ((1, 2), (2, 16)), jnp.float32)
    spread = jnp.clip(jnp.exp(math.log(3.0) - 2.3025851 * jax.random.uniform(splits[1], (LEV, NLAT, NLON), jnp.float32) ** block_scale(splits[1], (LEV, NLAT, NLON), ((1, 2), (2, 16)), -0.2, 0.2)), 0.3, 3.0)
    vert_root = draw_vert_root(jax.random.fold_in(splits[11], 71), 0)
    wind_lon = jnp.clip(jax.random.uniform(splits[3], (LEV, NLAT, NLON), jnp.float32, -0.45, 0.45) * block_scale(splits[3], (LEV, NLAT, NLON), ((0, 16), (1, 2)), -0.4, 0.0), -0.45, 0.45)
    wind_lat = jnp.clip(jax.random.uniform(splits[4], (LEV, NLAT, NLON), jnp.float32, -0.45, 0.45) * block_scale(splits[4], (LEV, NLAT, NLON), ((0, 16), (1, 2)), -0.4, 0.0), -0.45, 0.45)
    obs_dest_keys = jax.random.split(jax.random.fold_in(splits[5], 1), NOBS // NOBS_DEV)
    obs_dest_turns = jax.random.permutation(jax.random.fold_in(splits[5], 3), NOBS // NOBS_DEV)
    obs_dest = jax.vmap(lambda own, number: assign_block(jax.random.fold_in(splits[5], 2), own, number, NOBS_DEV, N_HORIZ, 1, CAP, 2))(obs_dest_keys, obs_dest_turns).reshape((NOBS, 1))
    obs_cells = place_ends(jax.random.randint(splits[6], (4, NOBS), 0, LEV // N_HORIZ * CLAT * NLON), jax.random.fold_in(splits[6], 1), 0, (LEV // N_HORIZ * CLAT * NLON) - 1).astype(jnp.int32)
    obs_time = place_ends(jax.random.randint(splits[7], (NOBS,), 0, NT + 1), jax.random.fold_in(splits[7], 1), 0, NT).astype(jnp.int32)
    obs_value = normal_values(splits[8], (NOBS,), 1.0, 6.0, ((0, 32),), jnp.float32)
    obs_weight = jnp.clip(1.0 * jax.random.uniform(splits[9], (4, NOBS), jnp.float32) ** block_scale(splits[9], (4, NOBS), ((1, 32),), -0.2, 0.2), 0.0, 1.0)
    obs_rinv = jnp.clip(jnp.exp(math.log(3.0) - 2.3025851 * jax.random.uniform(splits[10], (NOBS,), jnp.float32) ** block_scale(splits[10], (NOBS,), ((0, 32),), -0.2, 0.2)), 0.3, 3.0)
    return dict(control=control, spread=spread, vert_root=vert_root, wind_lon=wind_lon, wind_lat=wind_lat, obs_dest=obs_dest, obs_cells=obs_cells, obs_time=obs_time, obs_value=obs_value, obs_weight=obs_weight, obs_rinv=obs_rinv)


def advance(current, west_cells, east_cells, south_rows, north_rows, wind_u, wind_v):
    up_lon = jnp.maximum(wind_u, 0.0)
    down_lon = jnp.minimum(wind_u, 0.0)
    up_lat = jnp.maximum(wind_v, 0.0)
    down_lat = jnp.minimum(wind_v, 0.0)
    return (current - up_lon * (current - west_cells) - down_lon * (east_cells - current)
            - up_lat * (current - south_rows) - down_lat * (north_rows - current))


def forward_step(current, wind_u, wind_v):
    padded = jnp.pad(current, ((0, 0), (1, 1), (0, 0)))
    return advance(current, jnp.roll(current, 1, axis=2), jnp.roll(current, -1, axis=2),
                   padded[:, :-2], padded[:, 2:], wind_u, wind_v)


def adjoint_terms(adjoint_now, wind_u, wind_v):
    up_lon = jnp.maximum(wind_u, 0.0)
    down_lon = jnp.minimum(wind_u, 0.0)
    up_lat = jnp.maximum(wind_v, 0.0)
    down_lat = jnp.minimum(wind_v, 0.0)
    base = (1.0 - up_lon + down_lon - up_lat + down_lat) * adjoint_now
    base = base + jnp.roll(up_lon * adjoint_now, -1, axis=2) - jnp.roll(down_lon * adjoint_now, 1, axis=2)
    return base, up_lat * adjoint_now, down_lat * adjoint_now


def adjoint_step(adjoint_now, wind_u, wind_v):
    base, plus_flux, minus_flux = adjoint_terms(adjoint_now, wind_u, wind_v)
    plus_pad = jnp.pad(plus_flux, ((0, 0), (1, 1), (0, 0)))
    minus_pad = jnp.pad(minus_flux, ((0, 0), (1, 1), (0, 0)))
    return base + plus_pad[:, 2:] - minus_pad[:, :-2]


def reference(control, spread, vert_root, wind_lon, wind_lat, obs_dest, obs_cells, obs_time, obs_value, obs_weight, obs_rinv):
    levels_all, lat_all, lon_all = control.shape
    increment = spread * jnp.dot(vert_root, control.reshape(levels_all, -1), precision=lax.Precision.HIGHEST,
                                 preferred_element_type=jnp.float32).reshape(control.shape)
    states = [increment]
    current = increment
    for tick_index in range(NT):
        current = forward_step(current, wind_lon, wind_lat)
        states.append(current)
    block_size = levels_all * lat_all * lon_all
    states_flat = jnp.stack(states).reshape(-1)
    level_local = LEV // N_HORIZ
    row_ids = jnp.arange(obs_value.shape[0], dtype=jnp.int32)
    band_ids = row_ids // (NOBS_DEV * N_HORIZ)
    group_ids = obs_dest[:, 0]
    level_ids = group_ids[None, :] * level_local + obs_cells // (CLAT * NLON)
    lat_ids = band_ids[None, :] * CLAT + (obs_cells // NLON) % CLAT
    lon_ids = obs_cells % NLON
    global_ids = (level_ids * lat_all + lat_ids) * lon_all + lon_ids
    where_ids = (obs_time[None, :] * block_size + global_ids).astype(jnp.int32)
    picked = states_flat[where_ids]
    hx = jnp.sum(obs_weight * picked, axis=0)
    departure = obs_rinv * (hx - obs_value)
    forcing = jnp.zeros(((NT + 1) * block_size,), jnp.float32).at[where_ids].add(obs_weight * departure[None, :])
    forcing = forcing.reshape(NT + 1, levels_all, lat_all, lon_all)
    adjoint_now = forcing[NT]
    for tick_index in range(NT - 1, -1, -1):
        adjoint_now = adjoint_step(adjoint_now, wind_lon, wind_lat) + forcing[tick_index]
    weighted = (spread * adjoint_now).reshape(levels_all, -1)
    gradient = control + jnp.dot(vert_root.T, weighted, precision=lax.Precision.HIGHEST,
                                 preferred_element_type=jnp.float32).reshape(control.shape)
    return gradient, departure
```

```python
import functools

import jax
import jax.numpy as jnp
from jax import lax
from jax.experimental import pallas as pl
from jax.experimental.pallas import tpu as pltpu
from jax.sharding import PartitionSpec as P

NT = 4
CAP = 64
ROWS = 8
LANES = 128
FIELDS = 16
F32 = jnp.float32
I32 = jnp.int32
ANY = pl.BlockSpec(memory_space=pl.ANY)
VM = pl.BlockSpec(memory_space=pltpu.VMEM)


def call(body, out_shape, in_specs, out_specs, scratch=(), limit=40, cost=(1e6, 1e6)):
    return pl.pallas_call(
        body,
        out_shape=out_shape,
        in_specs=in_specs,
        out_specs=out_specs,
        scratch_shapes=list(scratch),
        compiler_params=pltpu.CompilerParams(vmem_limit_bytes=limit * 2**20),
        cost_estimate=pl.CostEstimate(
            flops=int(cost[0]), bytes_accessed=int(cost[1]), transcendentals=0
        ),
    )


def exchange(tile_rows, toward):
    count = lax.axis_size("obs")
    if count == 2:
        return lax.ppermute(tile_rows, "obs", [(0, 1), (1, 0)])
    below = lax.ppermute(tile_rows, "obs", [(i, i + 1) for i in range(count - 1)])
    above = lax.ppermute(tile_rows, "obs", [(i + 1, i) for i in range(count - 1)])
    first = (jnp.arange(ROWS) < ROWS // 2)[None, :, None]
    return jnp.where(first, above, below) if toward else jnp.where(first, below, above)


def halo_masks():
    first = (jnp.arange(ROWS) < ROWS // 2)[:, None]
    if lax.axis_size("obs") == 2:
        lower = lax.axis_index("obs") == 0
        front = jnp.where(lower, first, ~first)
        back = ~front
    else:
        front = back = jnp.ones_like(first)
    wide = lambda m: jnp.broadcast_to(m, (ROWS, LANES)).astype(F32)
    return wide(front), wide(back)


def wind_kernel(tiles, u_ref, uh_ref, v_ref, vh_ref, mask_ref, uo_ref, vo_ref, scr):
    levels = u_ref.shape[0]

    def level(l, carry):
        for src, rim, dst in ((u_ref, uh_ref, uo_ref), (v_ref, vh_ref, vo_ref)):
            for c in range(tiles):
                cols = pl.ds(c * LANES, LANES)
                scr[pl.ds(c * 16, 8), :] = src[l, :, cols]
                scr[pl.ds(c * 16 + 8, 8), :] = rim[l, :, cols] * mask_ref[...]
            for c in range(tiles):
                dst[l, pl.ds(c * 16, 8), :] = scr[pl.ds(c * 16, 8, stride=2), :]
                dst[l, pl.ds(c * 16 + 8, 8), :] = scr[pl.ds(c * 16 + 1, 8, stride=2), :]
        return carry

    lax.fori_loop(0, levels, level, 0)


def split3(x):
    a = x.astype(jnp.bfloat16)
    r = x - a.astype(F32)
    b = r.astype(jnp.bfloat16)
    return a, b, (r - b.astype(F32)).astype(jnp.bfloat16)


def bin_kernel(groups, dest_ref, data_ref, out_ref, placed_ref, hit):
    count = dest_ref.shape[0]
    slots = groups * CAP
    width = -(-groups // LANES) * LANES
    below = (
        lax.broadcasted_iota(I32, (LANES, LANES), 0) > lax.broadcasted_iota(I32, (LANES, LANES), 1)
    ).astype(jnp.bfloat16)
    lane = lax.broadcasted_iota(I32, (LANES, width), 1)
    slot_lane = lax.broadcasted_iota(I32, (LANES, slots), 1)
    seen = jnp.zeros((1, width), F32)
    for b in range(count // LANES):
        rows = pl.ds(b * LANES, LANES)
        owner = dest_ref[rows, :]
        mine = (lane == owner).astype(F32)
        before = (
            jnp.dot(below, mine.astype(jnp.bfloat16), preferred_element_type=F32) + seen
        )
        rank = jnp.sum(before * mine, axis=1, keepdims=True)
        seen = seen + jnp.sum(mine, axis=0, keepdims=True)
        placed = owner * CAP + rank.astype(I32)
        placed_ref[rows, :] = placed
        hit[rows, :] = jnp.where(slot_lane == placed, 1.0, 0.0).astype(jnp.bfloat16)
    parts = jnp.concatenate(split3(data_ref[...]), axis=0)
    got = jnp.dot(parts, hit[...], preferred_element_type=F32)
    sums = got[:FIELDS] + got[FIELDS : 2 * FIELDS] + got[2 * FIELDS :]
    for r in range(groups):
        out_ref[r] = sums[:, r * CAP : (r + 1) * CAP]


def hypercube(blocks):
    groups = blocks.shape[0]
    step = 1
    while step < groups:
        pairs = [(i, i ^ step) for i in range(groups)]
        view = blocks.reshape((groups // (2 * step), 2, step) + blocks.shape[1:])
        got = lax.ppermute(view[:, 1], "horiz", pairs)
        blocks = jnp.stack([view[:, 0], got], axis=1).reshape(blocks.shape)
        step *= 2
    return blocks


def prep_kernel(levels, tiles, got_ref, idx_ref, w_ref, vr_ref, scr):
    groups = got_ref.shape[0]
    lon = tiles * LANES
    for r in range(groups):
        part = pl.ds(r * CAP, CAP)
        block = got_ref[r]
        ints = block[0:8].astype(I32)
        cell = ints[0:4]
        time = ints[4:5]
        lev = cell // (ROWS * lon)
        row = (cell // lon) % ROWS
        col = cell % lon
        tile = (time * levels + lev) * tiles + col // LANES
        idx_ref[0:4, part] = tile * 16 + (row % 2) * 8 + row // 2
        idx_ref[4:8, part] = tile * 8 + (row % 2) * 4 + row // 2
        scr[0:4, part] = (col % LANES).astype(F32)
        scr[4:8, part] = jnp.zeros((4, CAP), F32)
        scr[8:16, part] = block[8:16]
    slots = groups * CAP
    lane = lax.broadcasted_iota(I32, (LANES, LANES), 1)
    for b in range(slots // LANES):
        rows = pl.ds(b * LANES, LANES)
        cols = jnp.transpose(scr[:, rows], (1, 0))
        for k in range(4):
            at = cols[:, k : k + 1].astype(I32)
            w_ref[k, rows, :] = jnp.where(lane == at, cols[:, 8 + k : 9 + k], 0.0)
        vr_ref[0, rows, :] = jnp.broadcast_to(cols[:, 12:13], (LANES, LANES))
        vr_ref[1, rows, :] = jnp.broadcast_to(cols[:, 13:14], (LANES, LANES))


def cycle_kernel(
    levels,
    tiles,
    field,
    halo,
    uw_hbm,
    vw_hbm,
    idx_hbm,
    w_hbm,
    vr_hbm,
    front_ref,
    own_out,
    rim_out,
    dep_out,
    uw,
    vw,
    states,
    f0,
    f1,
    f2,
    f3,
    w,
    vr,
    scr,
    picked,
    acc,
    flux,
    idx,
    sems,
    lsems,
):
    forcing = (f0, f1, f2, f3)
    slots = acc.shape[0]
    per = field.shape[2] // LANES
    block = tiles * 16
    loads = [
        pltpu.make_async_copy(idx_hbm, idx, sems.at[0]),
        pltpu.make_async_copy(w_hbm, w, sems.at[1]),
        pltpu.make_async_copy(vr_hbm, vr, sems.at[2]),
    ]

    def wind_loads(l):
        return (
            pltpu.make_async_copy(uw_hbm.at[l], uw.at[l], lsems.at[0, l]),
            pltpu.make_async_copy(vw_hbm.at[l], vw.at[l], lsems.at[1, l]),
        )

    for l in range(levels):
        for copy in wind_loads(l):
            copy.start()
    for copy in loads:
        copy.start()

    lane = lax.broadcasted_iota(I32, (8, LANES), 1)
    first = lane == 0
    last = lane == LANES - 1
    sub = lax.broadcasted_iota(I32, (8, LANES), 0)
    own = sub < 4
    zero = jnp.zeros((8, LANES), F32)
    east_of = lambda x: pltpu.roll(x, LANES - 1, 1)
    west_of = lambda x: pltpu.roll(x, 1, 1)

    def forward(l, carry):
        for copy in wind_loads(l):
            copy.wait()
        start = pl.multiple_of(l * block, block)
        for c in range(tiles):
            j, h = divmod(c, per)
            cols = pl.ds(h * LANES, LANES)
            scr[pl.ds(c * 16, 8), :] = field[j * levels + l, :, cols]
            scr[pl.ds(c * 16 + 8, 8), :] = halo[j * levels + l, :, cols] * front_ref[...]
        for c in range(tiles):
            states[pl.ds(start + c * 16, 8), :] = scr[pl.ds(c * 16, 8, stride=2), :]
            states[pl.ds(start + c * 16 + 8, 8), :] = scr[pl.ds(c * 16 + 1, 8, stride=2), :]
        fstart = pl.multiple_of(l * tiles * 8, tiles * 8)
        fstep = levels * tiles * 8
        for t in range(NT):
            src = pl.multiple_of(start + t * levels * block, block)
            dst = pl.multiple_of(start + (t + 1) * levels * block, block)

            def tile(c):
                c = c % tiles
                return (
                    states[pl.ds(src + c * 16, 8), :],
                    states[pl.ds(src + c * 16 + 8, 8), :],
                )

            q_w, q, q_e = tile(-1), tile(0), tile(1)
            w_w = [west_of(x) for x in q_w]
            w_c = [west_of(x) for x in q]
            e_c = [east_of(x) for x in q]
            for c in range(tiles):
                e_e = [east_of(x) for x in q_e]
                even, odd = q
                souths = (pltpu.roll(odd, 1, 0), even)
                norths = (odd, pltpu.roll(even, 7, 0))
                for side in range(2):
                    here = q[side]
                    at = pl.ds(c * 16 + side * 8, 8)
                    u = uw[l, at, :]
                    v = vw[l, at, :]
                    west = jnp.where(first, w_w[side], w_c[side])
                    east = jnp.where(last, e_e[side], e_c[side])
                    lon = jnp.where(u > 0, west, east)
                    lat = jnp.where(v > 0, souths[side], norths[side])
                    states[pl.ds(dst + c * 16 + side * 8, 8), :] = (
                        here + jnp.abs(u) * (lon - here) + jnp.abs(v) * (lat - here)
                    )
                for f in forcing:
                    f[pl.ds(pl.multiple_of(fstart + t * fstep, 8) + c * 8, 8), :] = zero
                    if t == NT - 1:
                        f[pl.ds(pl.multiple_of(fstart + NT * fstep, 8) + c * 8, 8), :] = zero
                w_w, w_c, e_c = w_c, [west_of(x) for x in q_e], e_e
                q, q_e = q_e, tile(c + 2)
        return carry

    lax.fori_loop(0, levels, forward, 0)

    for copy in loads:
        copy.wait()

    def gather(i, carry):
        base = pl.multiple_of(i * 8, 8)
        for k in range(4):
            for j in range(8):
                r = idx[k, base + j]
                picked[pl.ds(k * 8 + j, 1), :] = states[pl.ds(r, 1), :]
        total = w[0, pl.ds(base, 8), :] * picked[pl.ds(0, 8), :]
        for k in range(1, 4):
            total = total + w[k, pl.ds(base, 8), :] * picked[pl.ds(k * 8, 8), :]
        acc[pl.ds(base, 8), :] = total
        return carry

    lax.fori_loop(0, slots // 8, gather, 0)

    hx = jnp.sum(acc[...], axis=1, keepdims=True)
    dep_out[...] = vr[1] * (hx - vr[0])

    def scatter(i, carry):
        base = pl.multiple_of(i * 8, 8)
        dep = dep_out[pl.ds(base, 8), :]
        for k in range(4):
            flux[pl.ds(k * 8, 8), :] = w[k, pl.ds(base, 8), :] * dep
        for j in range(8):
            for k in range(4):
                r = idx[4 + k, base + j]
                at = pl.ds(r, 1)
                forcing[k][at, :] = forcing[k][at, :] + flux[pl.ds(k * 8 + j, 1), :]
        return carry

    lax.fori_loop(0, slots // 8, scatter, 0)

    def backward(l, carry):
        fstart = pl.multiple_of(l * tiles * 8, tiles * 8)
        fstep = levels * tiles * 8

        def force(t, c):
            at = pl.ds(pl.multiple_of(fstart + t * fstep, 8) + c * 8, 8)
            total = (f0[at, :] + f1[at, :]) + (f2[at, :] + f3[at, :])
            return (jnp.where(own, total, 0.0), jnp.where(own, pltpu.roll(total, 4, 0), 0.0))

        def fluxes(ref, c):
            c = c % tiles
            out = []
            for side in range(2):
                at = pl.ds(c * 16 + side * 8, 8)
                a = ref[at, :]
                u = uw[l, at, :]
                v = vw[l, at, :]
                x = jnp.abs(u) * a
                y = jnp.abs(v) * a
                p = jnp.where(u > 0, x, 0.0)
                s = jnp.where(v > 0, y, 0.0)
                out.append((a - x - y, east_of(p), west_of(x - p), s, y - s))
            return out

        for c in range(tiles):
            even, odd = force(NT, c)
            scr[pl.ds(c * 16, 8), :] = even
            scr[pl.ds(c * 16 + 8, 8), :] = odd
        half = tiles * 16
        for t in range(NT - 1, -1, -1):
            src = scr.at[pl.ds(0 if t % 2 else half, half)]
            dst = scr.at[pl.ds(half if t % 2 else 0, half)]
            before, now = fluxes(src, -1), fluxes(src, 0)
            head = now
            for c in range(tiles):
                after = head if c == tiles - 1 else fluxes(src, c + 1)
                fine = force(t, c)
                (_, _, _, s_e, n_e), (_, _, _, s_o, n_o) = now
                lats = (s_o + pltpu.roll(n_o, 1, 0), pltpu.roll(s_e, 7, 0) + n_e)
                for side in range(2):
                    stay, p, m, _, _ = now[side]
                    value = (
                        stay
                        + jnp.where(last, after[side][1], p)
                        + jnp.where(first, before[side][2], m)
                        + lats[side]
                        + fine[side]
                    )
                    dst[pl.ds(c * 16 + side * 8, 8), :] = value
                before, now = now, after
        for c in range(tiles):
            even = scr[pl.ds(c * 16, 8), :]
            odd = scr[pl.ds(c * 16 + 8, 8), :]
            scr[pl.ds(half + c * 16, 8, stride=2), :] = even
            scr[pl.ds(half + c * 16 + 1, 8, stride=2), :] = odd
        for c in range(tiles):
            j, h = divmod(c, per)
            cols = pl.ds(h * LANES, LANES)
            own_out[j * levels + l, :, cols] = scr[pl.ds(half + c * 16, 8), :]
            rim_out[j * levels + l, :, cols] = scr[pl.ds(half + c * 16 + 8, 8), :]
        return carry

    lax.fori_loop(0, levels, backward, 0)


def per_device(
    control,
    spread,
    vert_root,
    wind_lon,
    wind_lat,
    obs_dest,
    obs_cells,
    obs_time,
    obs_value,
    obs_weight,
    obs_rinv,
):
    levels_all = control.shape[0]
    width = control.shape[2]
    groups = lax.axis_size("horiz")
    levels, _, lon = wind_lon.shape
    tiles = lon // LANES
    slots = groups * CAP
    count = obs_value.shape[0]
    front, back = halo_masks()

    increment = spread * jnp.einsum(
        "lm,mrc->lrc",
        vert_root,
        control,
        precision=lax.Precision.HIGHEST,
        preferred_element_type=F32,
    )
    field = lax.all_to_all(increment, "horiz", split_axis=0, concat_axis=0, tiled=True)

    ring = jax.ShapeDtypeStruct((levels, tiles * 16, LANES), F32)
    uw, vw = call(
        functools.partial(wind_kernel, tiles),
        (ring, ring),
        [VM] * 5,
        (VM, VM),
        [pltpu.VMEM((tiles * 16, LANES), F32)],
        cost=(1e6, 8e6),
    )(wind_lon, exchange(wind_lon, True), wind_lat, exchange(wind_lat, True), front)

    target = obs_dest ^ lax.axis_index("horiz")
    blank = jnp.zeros((1, count), F32)
    data = jnp.concatenate(
        [obs_cells.astype(F32), obs_time[None].astype(F32)]
        + [blank] * 3
        + [obs_weight, obs_value[None], obs_rinv[None]]
        + [blank] * 2,
        axis=0,
    )
    binned, placed = call(
        functools.partial(bin_kernel, groups),
        (
            jax.ShapeDtypeStruct((groups, FIELDS, CAP), F32),
            jax.ShapeDtypeStruct((count, 1), I32),
        ),
        [VM] * 2,
        (VM, VM),
        [pltpu.VMEM((count, slots), jnp.bfloat16)],
        cost=(1e8, 4e6),
    )(target, data)
    got = hypercube(binned)
    idx, weights, pair = call(
        functools.partial(prep_kernel, levels, tiles),
        (
            jax.ShapeDtypeStruct((8, slots), I32),
            jax.ShapeDtypeStruct((4, slots, LANES), F32),
            jax.ShapeDtypeStruct((2, slots, LANES), F32),
        ),
        [VM],
        (VM, VM, VM),
        [pltpu.VMEM((FIELDS, slots), F32)],
        cost=(1e6, 6e6),
    )(got)

    halo = exchange(field, True)
    block = jax.ShapeDtypeStruct((groups * levels, ROWS, width), F32)
    forcing = pltpu.VMEM(((NT + 1) * levels * tiles * 8, LANES), F32)
    adjoint, rim, dep = call(
        functools.partial(cycle_kernel, levels, tiles),
        (block, block, jax.ShapeDtypeStruct((slots, LANES), F32)),
        [VM, VM, ANY, ANY, ANY, ANY, ANY, VM],
        (VM, VM, VM),
        [
            pltpu.VMEM((levels, tiles * 16, LANES), F32),
            pltpu.VMEM((levels, tiles * 16, LANES), F32),
            pltpu.VMEM(((NT + 1) * levels * tiles * 16, LANES), F32),
            forcing,
            forcing,
            forcing,
            forcing,
            pltpu.VMEM((4, slots, LANES), F32),
            pltpu.VMEM((2, slots, LANES), F32),
            pltpu.VMEM((2 * tiles * 16, LANES), F32),
            pltpu.VMEM((32, LANES), F32),
            pltpu.VMEM((slots, LANES), F32),
            pltpu.VMEM((32, LANES), F32),
            pltpu.SMEM((8, slots), I32),
            pltpu.SemaphoreType.DMA((3,)),
            pltpu.SemaphoreType.DMA((2, levels)),
        ],
        limit=56,
        cost=(1e8, 16e6),
    )(field, halo, uw, vw, idx, weights, pair, front)

    total = adjoint + exchange(rim, False) * back[:, :1][None]
    column = lax.all_to_all(total, "horiz", split_axis=0, concat_axis=0, tiled=True)

    back_home = hypercube(dep[:, 0].reshape(groups, CAP)).reshape(1, slots)
    departure = jnp.sum(
        jnp.where(placed == jnp.arange(slots, dtype=I32)[None, :], back_home, 0.0), axis=1
    )

    gradient = control + jnp.einsum(
        "lm,lrc->mrc",
        vert_root,
        spread * column,
        precision=lax.Precision.HIGHEST,
        preferred_element_type=F32,
    )
    return (gradient, departure)


def solution(mesh):
    in_specs = (
        P(None, "obs", "horiz"),
        P(None, "obs", "horiz"),
        P(),
        P("horiz", "obs", None),
        P("horiz", "obs", None),
        P(("obs", "horiz"), None),
        P(None, ("obs", "horiz")),
        P(("obs", "horiz")),
        P(("obs", "horiz")),
        P(None, ("obs", "horiz")),
        P(("obs", "horiz")),
    )
    out_specs = (P(None, "obs", "horiz"), P(("obs", "horiz")))
    return jax.shard_map(
        per_device, mesh=mesh, in_specs=in_specs, out_specs=out_specs, check_vma=False
    )
```

```python
import functools

import jax
import jax.numpy as jnp
from jax import lax
from jax.experimental import pallas as pl
from jax.experimental.pallas import tpu as pltpu
from jax.sharding import PartitionSpec as P

NT = 4
CAP = 64
ROWS = 8
LANES = 128
FIELDS = 16
F32 = jnp.float32
I32 = jnp.int32
ANY = pl.BlockSpec(memory_space=pl.ANY)
VM = pl.BlockSpec(memory_space=pltpu.VMEM)


def call(body, out_shape, in_specs, out_specs, scratch=(), limit=40, cost=(1e6, 1e6), grid=()):
    return pl.pallas_call(
        body,
        out_shape=out_shape,
        grid=grid,
        in_specs=in_specs,
        out_specs=out_specs,
        scratch_shapes=list(scratch),
        compiler_params=pltpu.CompilerParams(vmem_limit_bytes=limit * 2**20),
        cost_estimate=pl.CostEstimate(
            flops=int(cost[0]), bytes_accessed=int(cost[1]), transcendentals=0
        ),
    )


def split2(x):
    a = x.astype(jnp.bfloat16)
    return a, (x - a.astype(F32)).astype(jnp.bfloat16)


def wide_root(root):
    high, low = split2(root)
    return jnp.concatenate([high, high, low], axis=1)


def apply_root(wide, columns):
    high, low = split2(columns)
    return jnp.dot(wide, jnp.concatenate([high, low, high], axis=0), preferred_element_type=F32)


def level_rows(r, levels):
    return pl.ds(r, levels, stride=ROWS)


def start_kernel(
    groups,
    root_hbm,
    control_hbm,
    spread_hbm,
    dest_hbm,
    cells_hbm,
    time_hbm,
    value_hbm,
    weight_hbm,
    rinv_hbm,
    out_hbm,
    placed_ref,
    root,
    control,
    spread,
    dest,
    cells,
    time,
    value,
    weight,
    rinv,
    out,
    data,
    hit,
    small_sems,
    sems,
    out_sems,
):
    levels_all = root.shape[0]
    levels = levels_all // groups
    halves = control.shape[0]
    smalls = [
        pltpu.make_async_copy(a, b, small_sems.at[i])
        for i, (a, b) in enumerate(
            (
                (dest_hbm, dest),
                (cells_hbm, cells),
                (time_hbm, time),
                (value_hbm, value),
                (weight_hbm, weight),
                (rinv_hbm, rinv),
                (root_hbm, root),
            )
        )
    ]
    for copy in smalls:
        copy.start()

    def part(h):
        cols = pl.ds(h * LANES, LANES)
        return (
            pltpu.make_async_copy(control_hbm.at[:, cols], control.at[h], sems.at[0, h]),
            pltpu.make_async_copy(spread_hbm.at[:, cols], spread.at[h], sems.at[1, h]),
        )

    parts = [part(h) for h in range(halves)]
    for i in range(2):
        for h in range(halves):
            parts[h][i].start()
    for copy in smalls:
        copy.wait()
    bin_observations(groups, dest, cells, time, value, weight, rinv, placed_ref, out, data, hit)
    wide = wide_root(root[...])
    block = levels * ROWS
    outs = []
    for h in range(halves):
        parts[h][0].wait()
        results = [apply_root(wide, control[h, level_rows(r, levels_all), :]) for r in range(ROWS)]
        parts[h][1].wait()
        for r in range(ROWS):
            value_r = spread[h, level_rows(r, levels_all), :] * results[r]
            for g in range(groups):
                out[g, pl.ds(h * block + r, levels, stride=ROWS), :] = value_r[
                    g * levels : (g + 1) * levels
                ]
        rows = pl.ds(h * block, block + (ROWS if h == halves - 1 else 0))
        outs.append(
            pltpu.make_async_copy(out.at[:, rows, :], out_hbm.at[:, rows, :], out_sems.at[h])
        )
        outs[-1].start()
    for copy in outs:
        copy.wait()


def end_kernel(groups, root_ref, control_ref, spread_ref, got_ref, placed_ref, out_hbm, dep_ref, control, spread, out, row, sems):
    levels_all = root_ref.shape[0]
    levels = levels_all // groups
    halves = out.shape[0]
    block = levels * ROWS
    wide = wide_root(root_ref[...])
    outs = []
    for h in range(halves):
        cols = pl.ds(h * LANES, LANES)
        control[h] = control_ref[:, cols]
        spread[h] = spread_ref[:, cols]
        for r in range(ROWS):
            at = level_rows(r, levels_all)
            adjoint = jnp.concatenate(
                [
                    got_ref[g, pl.ds(h * block + r, levels, stride=ROWS), :]
                    for g in range(groups)
                ],
                axis=0,
            )
            out[h, at, :] = control[h, at, :] + apply_root(wide, spread[h, at, :] * adjoint)
        outs.append(pltpu.make_async_copy(out.at[h], out_hbm.at[:, cols], sems.at[h]))
        outs[-1].start()
    for r in range(groups):
        row[0:1, r * CAP : (r + 1) * CAP] = got_ref[r, pl.ds(halves * block, 1), 0:CAP]
    lane = lax.broadcasted_iota(I32, (LANES, LANES), 1)
    for b in range(dep_ref.shape[0]):
        placed = to_column(placed_ref[pl.ds(b, 1), :]).astype(I32)
        total = jnp.zeros((LANES, LANES), F32)
        for c in range(groups * CAP // LANES):
            value = row[0:1, c * LANES : (c + 1) * LANES]
            total = total + jnp.where(lane + c * LANES == placed, value, 0.0)
        dep_ref[pl.ds(b, 1), :] = to_row(
            jnp.broadcast_to(jnp.sum(total, axis=1, keepdims=True), (LANES, LANES))
        )
    for copy in outs:
        copy.wait()


def rim_kernel(own_ref, rim_ref, mask_ref, out_ref):
    mask = mask_ref[...]
    rows = rim_ref.shape[1]
    for c in range(rows // ROWS):
        at = pl.ds(c * ROWS, ROWS)
        out_ref[:, at, :] = own_ref[:, at, :] + rim_ref[:, at, :] * mask[None]
    rest = pl.ds(rows, ROWS)
    out_ref[:, rest, :] = own_ref[:, rest, :]


def exchange(tile_rows, toward):
    count = lax.axis_size("obs")
    if count == 2:
        return lax.ppermute(tile_rows, "obs", [(0, 1), (1, 0)])
    below = lax.ppermute(tile_rows, "obs", [(i, i + 1) for i in range(count - 1)])
    above = lax.ppermute(tile_rows, "obs", [(i + 1, i) for i in range(count - 1)])
    first = (jnp.arange(tile_rows.shape[1]) % ROWS < ROWS // 2)[None, :, None]
    return jnp.where(first, above, below) if toward else jnp.where(first, below, above)


def halo_masks():
    first = (jnp.arange(ROWS) < ROWS // 2)[:, None]
    if lax.axis_size("obs") == 2:
        lower = lax.axis_index("obs") == 0
        front = jnp.where(lower, first, ~first)
        back = ~front
    else:
        front = back = jnp.ones_like(first)
    wide = lambda m: jnp.broadcast_to(m, (ROWS, LANES)).astype(F32)
    return wide(front), wide(back)


def wind_kernel(tiles, u_ref, uh_ref, v_ref, vh_ref, mask_ref, uo_ref, vo_ref, scr):
    levels = u_ref.shape[0]

    def level(l, carry):
        for src, rim, dst in ((u_ref, uh_ref, uo_ref), (v_ref, vh_ref, vo_ref)):
            for c in range(tiles):
                cols = pl.ds(c * LANES, LANES)
                scr[pl.ds(c * 16, 8), :] = src[l, :, cols]
                scr[pl.ds(c * 16 + 8, 8), :] = rim[l, :, cols] * mask_ref[...]
            for c in range(tiles):
                dst[l, pl.ds(c * 16, 8), :] = scr[pl.ds(c * 16, 8, stride=2), :]
                dst[l, pl.ds(c * 16 + 8, 8), :] = scr[pl.ds(c * 16 + 1, 8, stride=2), :]
        return carry

    lax.fori_loop(0, levels, level, 0)


def split3(x):
    a = x.astype(jnp.bfloat16)
    r = x - a.astype(F32)
    b = r.astype(jnp.bfloat16)
    return a, b, (r - b.astype(F32)).astype(jnp.bfloat16)


def to_row(wide):
    at = lax.broadcasted_iota(I32, (LANES, LANES), 0) == lax.broadcasted_iota(I32, (LANES, LANES), 1)
    return jnp.sum(jnp.where(at, wide, 0.0), axis=0, keepdims=True)


def to_column(row):
    at = lax.broadcasted_iota(I32, (LANES, LANES), 0) == lax.broadcasted_iota(I32, (LANES, LANES), 1)
    return jnp.sum(jnp.where(at, row, 0.0), axis=1, keepdims=True)


def bin_observations(
    groups, dest_ref, cells_ref, time_ref, value_ref, weight_ref, rinv_ref, placed_ref, out, data, hit
):
    count = dest_ref.shape[1]
    slots = groups * CAP
    width = -(-groups // LANES) * LANES
    below = (
        lax.broadcasted_iota(I32, (LANES, LANES), 0) > lax.broadcasted_iota(I32, (LANES, LANES), 1)
    ).astype(jnp.bfloat16)
    lane = lax.broadcasted_iota(I32, (LANES, width), 1)
    slot_lane = lax.broadcasted_iota(I32, (LANES, slots), 1)
    seen = jnp.zeros((1, width), F32)
    target = dest_ref[...].astype(F32)
    for b in range(count // LANES):
        rows = pl.ds(b * LANES, LANES)
        owner = to_column(target[:, b * LANES : (b + 1) * LANES]).astype(I32)
        mine = (lane == owner).astype(F32)
        before = (
            jnp.dot(below, mine.astype(jnp.bfloat16), preferred_element_type=F32) + seen
        )
        rank = jnp.sum(before * mine, axis=1, keepdims=True)
        seen = seen + jnp.sum(mine, axis=0, keepdims=True)
        placed = owner * CAP + rank.astype(I32)
        placed_ref[pl.ds(b, 1), :] = to_row(
            jnp.broadcast_to(placed.astype(F32), (LANES, LANES))
        )
        hit[rows, :] = jnp.where(slot_lane == placed, 1.0, 0.0).astype(jnp.bfloat16)
    data[0:4, :] = cells_ref[...].astype(F32)
    data[4:5, :] = time_ref[...].astype(F32)
    data[5:8, :] = jnp.zeros((3, count), F32)
    data[8:12, :] = weight_ref[...]
    data[12:13, :] = value_ref[...]
    data[13:14, :] = rinv_ref[...]
    data[14:16, :] = jnp.zeros((2, count), F32)
    parts = jnp.concatenate(split3(data[...]), axis=0)
    got = jnp.dot(parts, hit[...], preferred_element_type=F32)
    sums = got[:FIELDS] + got[FIELDS : 2 * FIELDS] + got[2 * FIELDS :]
    last = out.shape[1] - ROWS
    for g in range(groups):
        part = sums[:, g * CAP : (g + 1) * CAP]
        out[g, pl.ds(last, ROWS), 0:CAP] = part[0:ROWS]
        out[g, pl.ds(last, ROWS), CAP : 2 * CAP] = part[ROWS:FIELDS]


def prep_kernel(groups, levels, tiles, got_hbm, idx_ref, w_ref, vr_ref, got, scr, columns, sem):
    last = got_hbm.shape[1] - ROWS
    load = pltpu.make_async_copy(got_hbm.at[:, pl.ds(last, ROWS), :], got, sem)
    load.start()
    scr[...] = jnp.zeros_like(scr)
    load.wait()
    lon = tiles * LANES
    for g in range(groups):
        part = pl.ds(g * CAP, CAP)
        ints = got[g, :, 0:CAP].astype(I32)
        cell = ints[0:4]
        time = ints[4:5]
        lev = cell // (ROWS * lon)
        row = (cell // lon) % ROWS
        col = cell % lon
        tile = (time * levels + lev) * tiles + col // LANES
        scr[0:4, part] = (tile * 16 + (row % 2) * 8 + row // 2).astype(F32)
        scr[8:12, part] = (col % LANES).astype(F32)
        scr[16:24, part] = got[g, :, CAP : 2 * CAP]
        scr[32:36, part] = (tile * 8 + (row % 2) * 4 + row // 2).astype(F32)
    slots = groups * CAP
    lane = lax.broadcasted_iota(I32, (LANES, LANES), 1)
    few = LANES // 8
    narrow = lax.broadcasted_iota(I32, (few, LANES), 1)
    for b in range(slots // LANES):
        rows = pl.ds(b * LANES, LANES)
        cols = jnp.transpose(scr[:, rows], (1, 0))
        for k in range(4):
            at = cols[:, 8 + k : 9 + k].astype(I32)
            w_ref[k, rows, :] = jnp.where(lane == at, cols[:, 16 + k : 17 + k], 0.0)
        vr_ref[0, rows, :] = jnp.broadcast_to(cols[:, 20:21], (LANES, LANES))
        vr_ref[1, rows, :] = jnp.broadcast_to(cols[:, 21:22], (LANES, LANES))
        columns[...] = cols
        index = jnp.zeros((few, LANES), F32)
        for j in range(8):
            here = columns[pl.ds(j, few, stride=8), :]
            index = jnp.where((narrow // 4) % 8 == j, pltpu.roll(here, 4 * j, 1) if j else here, index)
        idx_ref[pl.ds(b * few, few), :] = index.astype(I32)


NSCRATCH = 12


def cycle_kernel(
    groups,
    levels,
    tiles,
    field,
    halo,
    uw,
    vw,
    idx_ref,
    w,
    vr,
    front_ref,
    *refs,
):
    own_out, rim_out = refs[: -NSCRATCH]
    (states, f0, f1, f2, f3, scr, picked, acc, dep_ref, flux, idx, sem) = refs[
        -NSCRATCH:
    ]
    forcing = (f0, f1, f2, f3)
    slots = acc.shape[0]
    per = tiles // groups
    block = tiles * 16
    load = pltpu.make_async_copy(idx_ref, idx, sem)
    load.start()

    lane = lax.broadcasted_iota(I32, (8, LANES), 1)
    first = lane == 0
    last = lane == LANES - 1
    sub = lax.broadcasted_iota(I32, (8, LANES), 0)
    own = sub < 4
    zero = jnp.zeros((8, LANES), F32)
    east_of = lambda x: pltpu.roll(x, LANES - 1, 1)
    west_of = lambda x: pltpu.roll(x, 1, 1)

    def forward(l, carry):
        start = pl.multiple_of(l * block, block)
        for c in range(tiles):
            j, h = divmod(c, per)
            at = pl.ds(pl.multiple_of((h * levels + l) * 8, 8), 8)
            scr[pl.ds(c * 16, 8), :] = field[j, at, :]
            scr[pl.ds(c * 16 + 8, 8), :] = halo[j, at, :] * front_ref[...]
        for c in range(tiles):
            states[pl.ds(start + c * 16, 8), :] = scr[pl.ds(c * 16, 8, stride=2), :]
            states[pl.ds(start + c * 16 + 8, 8), :] = scr[pl.ds(c * 16 + 1, 8, stride=2), :]
        fstart = pl.multiple_of(l * tiles * 8, tiles * 8)
        fstep = levels * tiles * 8
        for t in range(NT):
            src = pl.multiple_of(start + t * levels * block, block)
            dst = pl.multiple_of(start + (t + 1) * levels * block, block)

            def tile(c):
                c = c % tiles
                return (
                    states[pl.ds(src + c * 16, 8), :],
                    states[pl.ds(src + c * 16 + 8, 8), :],
                )

            q_w, q, q_e = tile(-1), tile(0), tile(1)
            w_w = [west_of(x) for x in q_w]
            w_c = [west_of(x) for x in q]
            e_c = [east_of(x) for x in q]
            for c in range(tiles):
                e_e = [east_of(x) for x in q_e]
                even, odd = q
                souths = (pltpu.roll(odd, 1, 0), even)
                norths = (odd, pltpu.roll(even, 7, 0))
                for side in range(2):
                    here = q[side]
                    at = pl.ds(c * 16 + side * 8, 8)
                    u = uw[l, at, :]
                    v = vw[l, at, :]
                    west = jnp.where(first, w_w[side], w_c[side])
                    east = jnp.where(last, e_e[side], e_c[side])
                    lon = jnp.where(u > 0, west, east)
                    lat = jnp.where(v > 0, souths[side], norths[side])
                    states[pl.ds(dst + c * 16 + side * 8, 8), :] = (
                        here + jnp.abs(u) * (lon - here) + jnp.abs(v) * (lat - here)
                    )
                for f in forcing:
                    f[pl.ds(pl.multiple_of(fstart + t * fstep, 8) + c * 8, 8), :] = zero
                    if t == NT - 1:
                        f[pl.ds(pl.multiple_of(fstart + NT * fstep, 8) + c * 8, 8), :] = zero
                w_w, w_c, e_c = w_c, [west_of(x) for x in q_e], e_e
                q, q_e = q_e, tile(c + 2)
        return carry

    lax.fori_loop(0, levels, forward, 0)

    load.wait()

    def gather(i, carry):
        base = pl.multiple_of(i * 8, 8)
        for k in range(4):
            for j in range(8):
                r = idx[i, j * 4 + k]
                picked[pl.ds(k * 8 + j, 1), :] = states[pl.ds(r, 1), :]
        total = w[0, pl.ds(base, 8), :] * picked[pl.ds(0, 8), :]
        for k in range(1, 4):
            total = total + w[k, pl.ds(base, 8), :] * picked[pl.ds(k * 8, 8), :]
        acc[pl.ds(base, 8), :] = total
        return carry

    lax.fori_loop(0, slots // 8, gather, 0)

    hx = jnp.sum(acc[...], axis=1, keepdims=True)
    dep_ref[...] = vr[1] * (hx - vr[0])
    tail = pl.ds(per * levels * 8, 8)
    for b in range(slots // LANES):
        row = to_row(dep_ref[pl.ds(b * LANES, LANES), :])
        for h in range(LANES // CAP):
            own_out[b * (LANES // CAP) + h, tail, 0:CAP] = jnp.broadcast_to(
                row[:, h * CAP : (h + 1) * CAP], (8, CAP)
            )
            own_out[b * (LANES // CAP) + h, tail, CAP:LANES] = jnp.zeros((8, LANES - CAP), F32)

    def scatter(i, carry):
        base = pl.multiple_of(i * 8, 8)
        dep = dep_ref[pl.ds(base, 8), :]
        for k in range(4):
            flux[pl.ds(k * 8, 8), :] = w[k, pl.ds(base, 8), :] * dep
        for j in range(8):
            for k in range(4):
                r = idx[i, 32 + j * 4 + k]
                at = pl.ds(r, 1)
                forcing[k][at, :] = forcing[k][at, :] + flux[pl.ds(k * 8 + j, 1), :]
        return carry

    lax.fori_loop(0, slots // 8, scatter, 0)

    def backward(l, carry):
        fstart = pl.multiple_of(l * tiles * 8, tiles * 8)
        fstep = levels * tiles * 8

        def force(t, c):
            at = pl.ds(pl.multiple_of(fstart + t * fstep, 8) + c * 8, 8)
            total = (f0[at, :] + f1[at, :]) + (f2[at, :] + f3[at, :])
            return (jnp.where(own, total, 0.0), jnp.where(own, pltpu.roll(total, 4, 0), 0.0))

        def fluxes(ref, c):
            c = c % tiles
            out = []
            for side in range(2):
                at = pl.ds(c * 16 + side * 8, 8)
                a = ref[at, :]
                u = uw[l, at, :]
                v = vw[l, at, :]
                x = jnp.abs(u) * a
                y = jnp.abs(v) * a
                p = jnp.where(u > 0, x, 0.0)
                s = jnp.where(v > 0, y, 0.0)
                out.append((a - x - y, east_of(p), west_of(x - p), s, y - s))
            return out

        for c in range(tiles):
            even, odd = force(NT, c)
            scr[pl.ds(c * 16, 8), :] = even
            scr[pl.ds(c * 16 + 8, 8), :] = odd
        half = tiles * 16
        for t in range(NT - 1, -1, -1):
            src = scr.at[pl.ds(0 if t % 2 else half, half)]
            dst = scr.at[pl.ds(half if t % 2 else 0, half)]
            before, now = fluxes(src, -1), fluxes(src, 0)
            head = now
            for c in range(tiles):
                after = head if c == tiles - 1 else fluxes(src, c + 1)
                fine = force(t, c)
                (_, _, _, s_e, n_e), (_, _, _, s_o, n_o) = now
                lats = (s_o + pltpu.roll(n_o, 1, 0), pltpu.roll(s_e, 7, 0) + n_e)
                for side in range(2):
                    stay, p, m, _, _ = now[side]
                    value = (
                        stay
                        + jnp.where(last, after[side][1], p)
                        + jnp.where(first, before[side][2], m)
                        + lats[side]
                        + fine[side]
                    )
                    dst[pl.ds(c * 16 + side * 8, 8), :] = value
                before, now = now, after
        for c in range(tiles):
            even = scr[pl.ds(c * 16, 8), :]
            odd = scr[pl.ds(c * 16 + 8, 8), :]
            scr[pl.ds(half + c * 16, 8, stride=2), :] = even
            scr[pl.ds(half + c * 16 + 1, 8, stride=2), :] = odd
        for c in range(tiles):
            j, h = divmod(c, per)
            at = pl.ds(pl.multiple_of((h * levels + l) * 8, 8), 8)
            own_out[j, at, :] = scr[pl.ds(half + c * 16, 8), :]
            rim_out[j, at, :] = scr[pl.ds(half + c * 16 + 8, 8), :]
        return carry

    lax.fori_loop(0, levels, backward, 0)


def per_device(
    control,
    spread,
    vert_root,
    wind_lon,
    wind_lat,
    obs_dest,
    obs_cells,
    obs_time,
    obs_value,
    obs_weight,
    obs_rinv,
):
    levels_all, _, width = control.shape
    groups = lax.axis_size("horiz")
    levels, _, lon = wind_lon.shape
    tiles = lon // LANES
    slots = groups * CAP
    count = obs_value.shape[0]
    halves = width // LANES
    rows = halves * levels * ROWS
    front, back = halo_masks()
    flat = (levels_all * ROWS, width)
    payload = jax.ShapeDtypeStruct((groups, rows + ROWS, LANES), F32)
    vmem = lambda *shape: pltpu.VMEM(shape, F32)
    ivmem = lambda *shape: pltpu.VMEM(shape, I32)

    outgoing, placed = call(
        functools.partial(start_kernel, groups),
        (payload, jax.ShapeDtypeStruct((count // LANES, LANES), F32)),
        [ANY] * 9,
        (ANY, VM),
        [
            vmem(*vert_root.shape),
            vmem(halves, flat[0], LANES),
            vmem(halves, flat[0], LANES),
            ivmem(1, count),
            ivmem(4, count),
            ivmem(1, count),
            vmem(1, count),
            vmem(4, count),
            vmem(1, count),
            vmem(*payload.shape),
            vmem(FIELDS, count),
            pltpu.VMEM((count, slots), jnp.bfloat16),
            pltpu.SemaphoreType.DMA((7,)),
            pltpu.SemaphoreType.DMA((2, halves)),
            pltpu.SemaphoreType.DMA((halves,)),
        ],
        limit=56,
        cost=(4e8, 4e6),
    )(
        vert_root,
        control.reshape(flat),
        spread.reshape(flat),
        obs_dest.reshape(1, count),
        obs_cells,
        obs_time[None],
        obs_value[None],
        obs_weight,
        obs_rinv[None],
    )
    field = lax.all_to_all(outgoing, "horiz", split_axis=0, concat_axis=0, tiled=True)

    ring = jax.ShapeDtypeStruct((levels, tiles * 16, LANES), F32)
    uw, vw = call(
        functools.partial(wind_kernel, tiles),
        (ring, ring),
        [VM] * 5,
        (VM, VM),
        [vmem(tiles * 16, LANES)],
        limit=14,
        cost=(1e6, 8e6),
    )(wind_lon, exchange(wind_lon, True), wind_lat, exchange(wind_lat, True), front)
    field, uw, vw, front, back = lax.optimization_barrier((field, uw, vw, front, back))

    halo = exchange(field, True)
    idx, weights, pair = call(
        functools.partial(prep_kernel, groups, levels, tiles),
        (
            jax.ShapeDtypeStruct((slots // 8, LANES), I32),
            jax.ShapeDtypeStruct((4, slots, LANES), F32),
            jax.ShapeDtypeStruct((2, slots, LANES), F32),
        ),
        [ANY],
        (VM, VM, VM),
        [
            vmem(groups, ROWS, LANES),
            vmem(LANES, slots),
            vmem(LANES, LANES),
            pltpu.SemaphoreType.DMA,
        ],
        limit=8,
        cost=(1e6, 6e6),
    )(field)

    forcing = vmem((NT + 1) * levels * tiles * 8, LANES)
    adjoint, rim = call(
        functools.partial(cycle_kernel, groups, levels, tiles),
        (payload, jax.ShapeDtypeStruct((groups, rows, LANES), F32)),
        [VM] * 8,
        (VM, VM),
        [
            vmem((NT + 1) * levels * tiles * 16, LANES),
            forcing,
            forcing,
            forcing,
            forcing,
            vmem(2 * tiles * 16, LANES),
            vmem(32, LANES),
            vmem(slots, LANES),
            vmem(slots, LANES),
            vmem(32, LANES),
            pltpu.SMEM((slots // 8, LANES), I32),
            pltpu.SemaphoreType.DMA,
        ],
        limit=34,
        cost=(1e8, 16e6),
    )(field, halo, uw, vw, idx, weights, pair, front)

    part = groups // 4
    total = call(
        rim_kernel,
        payload,
        [
            pl.BlockSpec((part, rows + ROWS, LANES), lambda i: (i, 0, 0)),
            pl.BlockSpec((part, rows, LANES), lambda i: (i, 0, 0)),
            pl.BlockSpec((ROWS, LANES), lambda i: (0, 0)),
        ],
        pl.BlockSpec((part, rows + ROWS, LANES), lambda i: (i, 0, 0)),
        limit=8,
        cost=(1e6, 3e6),
        grid=(4,),
    )(adjoint, exchange(rim, False), back)
    column = lax.all_to_all(total, "horiz", split_axis=0, concat_axis=0, tiled=True)

    gradient, departure = call(
        functools.partial(end_kernel, groups),
        (
            jax.ShapeDtypeStruct(flat, F32),
            jax.ShapeDtypeStruct((count // LANES, LANES), F32),
        ),
        [VM] * 5,
        (ANY, VM),
        [vmem(halves, flat[0], LANES)] * 3 + [vmem(8, slots), pltpu.SemaphoreType.DMA((halves,))],
        limit=14,
        cost=(4e8, 4e6),
    )(vert_root.T, control.reshape(flat), spread.reshape(flat), column, placed)
    return (gradient.reshape(control.shape), departure.reshape(count))


def solution(mesh):
    in_specs = (
        P(None, "obs", "horiz"),
        P(None, "obs", "horiz"),
        P(),
        P("horiz", "obs", None),
        P("horiz", "obs", None),
        P(("obs", "horiz"), None),
        P(None, ("obs", "horiz")),
        P(("obs", "horiz")),
        P(("obs", "horiz")),
        P(None, ("obs", "horiz")),
        P(("obs", "horiz")),
    )
    out_specs = (P(None, "obs", "horiz"), P(("obs", "horiz")))
    return jax.shard_map(
        per_device, mesh=mesh, in_specs=in_specs, out_specs=out_specs, check_vma=False
    )
```

```python
import functools

import jax
import jax.numpy as jnp
from jax import lax
from jax.experimental import pallas as pl
from jax.experimental.pallas import tpu as pltpu
from jax.sharding import PartitionSpec as P

NT = 4
CAP = 64
ROWS = 8
LANES = 128
FIELDS = 16
F32 = jnp.float32
I32 = jnp.int32
ANY = pl.BlockSpec(memory_space=pl.ANY)
VM = pl.BlockSpec(memory_space=pltpu.VMEM)


def call(body, out_shape, in_specs, out_specs, scratch=(), limit=40, cost=(1e6, 1e6), grid=()):
    return pl.pallas_call(
        body,
        out_shape=out_shape,
        grid=grid,
        in_specs=in_specs,
        out_specs=out_specs,
        scratch_shapes=list(scratch),
        compiler_params=pltpu.CompilerParams(vmem_limit_bytes=limit * 2**20),
        cost_estimate=pl.CostEstimate(
            flops=int(cost[0]), bytes_accessed=int(cost[1]), transcendentals=0
        ),
    )


def split2(x):
    a = x.astype(jnp.bfloat16)
    return a, (x - a.astype(F32)).astype(jnp.bfloat16)


def wide_root(root):
    high, low = split2(root)
    return jnp.concatenate([high, high, low], axis=1)


def apply_root(wide, columns):
    high, low = split2(columns)
    return jnp.dot(wide, jnp.concatenate([high, low, high], axis=0), preferred_element_type=F32)


def level_rows(r, levels):
    return pl.ds(r, levels, stride=ROWS)


def start_kernel(
    groups,
    root_hbm,
    control_hbm,
    spread_hbm,
    dest_hbm,
    cells_hbm,
    time_hbm,
    value_hbm,
    weight_hbm,
    rinv_hbm,
    out_hbm,
    placed_ref,
    root,
    control,
    spread,
    dest,
    cells,
    time,
    value,
    weight,
    rinv,
    out,
    data,
    hit,
    small_sems,
    sems,
    out_sems,
):
    levels_all = root.shape[0]
    levels = levels_all // groups
    halves = control.shape[0]
    smalls = [
        pltpu.make_async_copy(a, b, small_sems.at[i])
        for i, (a, b) in enumerate(
            (
                (dest_hbm, dest),
                (cells_hbm, cells),
                (time_hbm, time),
                (value_hbm, value),
                (weight_hbm, weight),
                (rinv_hbm, rinv),
                (root_hbm, root),
            )
        )
    ]
    for copy in smalls:
        copy.start()

    def part(h):
        cols = pl.ds(h * LANES, LANES)
        return (
            pltpu.make_async_copy(control_hbm.at[:, cols], control.at[h], sems.at[0, h]),
            pltpu.make_async_copy(spread_hbm.at[:, cols], spread.at[h], sems.at[1, h]),
        )

    parts = [part(h) for h in range(halves)]
    for i in range(2):
        for h in range(halves):
            parts[h][i].start()
    for copy in smalls:
        copy.wait()
    bin_observations(groups, dest, cells, time, value, weight, rinv, placed_ref, out, data, hit)
    wide = wide_root(root[...])
    block = levels * ROWS
    outs = []
    pairs = halves % 2 == 0
    for h in range(halves):
        parts[h][0].wait()
    for h in range(halves):
        parts[h][1].wait()
    for m in range(0, halves, 2 if pairs else 1):
        for r in range(ROWS):
            at = level_rows(r, levels_all)
            if pairs:
                both = apply_root(
                    wide, jnp.concatenate([control[m, at, :], control[m + 1, at, :]], axis=1)
                )
                both = both * jnp.concatenate([spread[m, at, :], spread[m + 1, at, :]], axis=1)
                both = reorder(both, even_odd(), split2)
                values = [both[:, 0:LANES], both[:, LANES:]]
            else:
                values = [spread[m, at, :] * apply_root(wide, control[m, at, :])]
            for i, value_r in enumerate(values):
                for g in range(groups):
                    out[g, pl.ds((m + i) * block + r, levels, stride=ROWS), :] = value_r[
                        g * levels : (g + 1) * levels
                    ]
    outs.append(pltpu.make_async_copy(out, out_hbm, out_sems.at[0]))
    outs[-1].start()
    for copy in outs:
        copy.wait()


def end_kernel(groups, root_ref, control_ref, spread_ref, got_ref, placed_ref, out_hbm, dep_ref, control, spread, out, row, sems):
    levels_all = root_ref.shape[0]
    levels = levels_all // groups
    halves = out.shape[0]
    block = levels * ROWS
    wide = wide_root(root_ref[...])
    outs = []
    pairs = halves % 2 == 0
    for h in range(halves):
        cols = pl.ds(h * LANES, LANES)
        control[h] = control_ref[:, cols]
        spread[h] = spread_ref[:, cols]
    for m in range(0, halves, 2 if pairs else 1):
        for r in range(ROWS):
            at = level_rows(r, levels_all)
            half = [
                jnp.concatenate(
                    [
                        got_ref[g, pl.ds(h * block + r, levels, stride=ROWS), :]
                        for g in range(groups)
                    ],
                    axis=0,
                )
                for h in range(m, m + (2 if pairs else 1))
            ]
            if pairs:
                adjoint = reorder(jnp.concatenate(half, axis=1), even_odd(back=True), split2)
                both = apply_root(
                    wide, jnp.concatenate([spread[m, at, :], spread[m + 1, at, :]], axis=1) * adjoint
                )
                values = [both[:, 0:LANES], both[:, LANES:]]
            else:
                values = [apply_root(wide, spread[m, at, :] * half[0])]
            for i, value in enumerate(values):
                out[m + i, at, :] = control[m + i, at, :] + value
        for h in range(m, m + (2 if pairs else 1)):
            cols = pl.ds(h * LANES, LANES)
            outs.append(pltpu.make_async_copy(out.at[h], out_hbm.at[:, cols], sems.at[h]))
            outs[-1].start()
    for r in range(groups):
        row[0:1, r * CAP : (r + 1) * CAP] = got_ref[r, pl.ds(halves * block, 1), 0:CAP]
    lane = lax.broadcasted_iota(I32, (LANES, LANES), 1)
    for b in range(dep_ref.shape[0]):
        placed = to_column(placed_ref[pl.ds(b, 1), :]).astype(I32)
        total = jnp.zeros((LANES, LANES), F32)
        for c in range(groups * CAP // LANES):
            value = row[0:1, c * LANES : (c + 1) * LANES]
            total = total + jnp.where(lane + c * LANES == placed, value, 0.0)
        dep_ref[pl.ds(b, 1), :] = to_row(
            jnp.broadcast_to(jnp.sum(total, axis=1, keepdims=True), (LANES, LANES))
        )
    for copy in outs:
        copy.wait()


def rim_kernel(own_ref, rim_ref, mask_ref, out_ref):
    mask = mask_ref[...]
    rows = rim_ref.shape[1]
    for c in range(rows // ROWS):
        at = pl.ds(c * ROWS, ROWS)
        out_ref[:, at, :] = own_ref[:, at, :] + rim_ref[:, at, :] * mask[None]
    rest = pl.ds(rows, ROWS)
    out_ref[:, rest, :] = own_ref[:, rest, :]


def even_odd(back=False):
    row = lax.broadcasted_iota(I32, (2 * LANES, 2 * LANES), 0)
    col = lax.broadcasted_iota(I32, (2 * LANES, 2 * LANES), 1)
    if back:
        row, col = col, row
    return jnp.where(row == 2 * (col % LANES) + col // LANES, 1.0, 0.0).astype(jnp.bfloat16)


def reorder(x, order, split):
    parts = split(x)
    count = x.shape[0]
    got = jnp.dot(jnp.concatenate(parts, axis=0), order, preferred_element_type=F32)
    total = got[0:count]
    for i in range(1, len(parts)):
        total = total + got[i * count : (i + 1) * count]
    return total


def neighbours(value, pairs, first, last):
    made = {}

    def rolled(c, side, amount):
        key = (c, side, amount)
        if key not in made:
            made[key] = pltpu.roll(value(c, side), amount, 1)
        return made[key]

    def east(c, side):
        if pairs and c % 2 == 0:
            return value(c + 1, side)
        same, after = (c - 1, c + 1) if pairs else (c, c + 1)
        return jnp.where(last, rolled(after, side, LANES - 1), rolled(same, side, LANES - 1))

    def west(c, side):
        if pairs and c % 2:
            return value(c - 1, side)
        same, before = (c + 1, c - 1) if pairs else (c, c - 1)
        return jnp.where(first, rolled(before, side, 1), rolled(same, side, 1))

    return east, west


def exchange(tile_rows, toward):
    count = lax.axis_size("obs")
    if count == 2:
        return lax.ppermute(tile_rows, "obs", [(0, 1), (1, 0)])
    below = lax.ppermute(tile_rows, "obs", [(i, i + 1) for i in range(count - 1)])
    above = lax.ppermute(tile_rows, "obs", [(i + 1, i) for i in range(count - 1)])
    first = (jnp.arange(tile_rows.shape[1]) % ROWS < ROWS // 2)[None, :, None]
    return jnp.where(first, above, below) if toward else jnp.where(first, below, above)


def halo_masks():
    first = (jnp.arange(ROWS) < ROWS // 2)[:, None]
    if lax.axis_size("obs") == 2:
        lower = lax.axis_index("obs") == 0
        front = jnp.where(lower, first, ~first)
        back = ~front
    else:
        front = back = jnp.ones_like(first)
    wide = lambda m: jnp.broadcast_to(m, (ROWS, LANES)).astype(F32)
    return wide(front), wide(back)


def wind_kernel(tiles, pairs, u_ref, uh_ref, v_ref, vh_ref, mask_ref, uo_ref, vo_ref, scr):
    levels = u_ref.shape[0]

    def level(l, carry):
        for src, rim, dst in ((u_ref, uh_ref, uo_ref), (v_ref, vh_ref, vo_ref)):
            step = 2 if pairs else 1
            for c in range(0, tiles, step):
                cols = pl.ds(c * LANES, step * LANES)
                both = jnp.concatenate([src[l, :, cols], rim[l, :, cols]], axis=0)
                if pairs:
                    both = reorder(both, even_odd(), split3)
                for i in range(step):
                    lanes = slice(i * LANES, (i + 1) * LANES)
                    scr[pl.ds((c + i) * 16, 8), :] = both[0:8, lanes]
                    scr[pl.ds((c + i) * 16 + 8, 8), :] = both[8:16, lanes] * mask_ref[...]
            for c in range(tiles):
                dst[l, pl.ds(c * 16, 8), :] = scr[pl.ds(c * 16, 8, stride=2), :]
                dst[l, pl.ds(c * 16 + 8, 8), :] = scr[pl.ds(c * 16 + 1, 8, stride=2), :]
        return carry

    lax.fori_loop(0, levels, level, 0)


def split3(x):
    a = x.astype(jnp.bfloat16)
    r = x - a.astype(F32)
    b = r.astype(jnp.bfloat16)
    return a, b, (r - b.astype(F32)).astype(jnp.bfloat16)


def to_row(wide):
    at = lax.broadcasted_iota(I32, (LANES, LANES), 0) == lax.broadcasted_iota(I32, (LANES, LANES), 1)
    return jnp.sum(jnp.where(at, wide, 0.0), axis=0, keepdims=True)


def to_column(row):
    at = lax.broadcasted_iota(I32, (LANES, LANES), 0) == lax.broadcasted_iota(I32, (LANES, LANES), 1)
    return jnp.sum(jnp.where(at, row, 0.0), axis=1, keepdims=True)


def bin_observations(
    groups, dest_ref, cells_ref, time_ref, value_ref, weight_ref, rinv_ref, placed_ref, out, data, hit
):
    count = dest_ref.shape[1]
    slots = groups * CAP
    width = -(-groups // LANES) * LANES
    below = (
        lax.broadcasted_iota(I32, (LANES, LANES), 0) > lax.broadcasted_iota(I32, (LANES, LANES), 1)
    ).astype(jnp.bfloat16)
    lane = lax.broadcasted_iota(I32, (LANES, width), 1)
    slot_lane = lax.broadcasted_iota(I32, (LANES, slots), 1)
    seen = jnp.zeros((1, width), F32)
    target = dest_ref[...].astype(F32)
    for b in range(count // LANES):
        rows = pl.ds(b * LANES, LANES)
        owner = to_column(target[:, b * LANES : (b + 1) * LANES]).astype(I32)
        mine = (lane == owner).astype(F32)
        before = (
            jnp.dot(below, mine.astype(jnp.bfloat16), preferred_element_type=F32) + seen
        )
        rank = jnp.sum(before * mine, axis=1, keepdims=True)
        seen = seen + jnp.sum(mine, axis=0, keepdims=True)
        placed = owner * CAP + rank.astype(I32)
        placed_ref[pl.ds(b, 1), :] = to_row(
            jnp.broadcast_to(placed.astype(F32), (LANES, LANES))
        )
        hit[rows, :] = jnp.where(slot_lane == placed, 1.0, 0.0).astype(jnp.bfloat16)
    data[0:4, :] = cells_ref[...].astype(F32)
    data[4:5, :] = time_ref[...].astype(F32)
    data[5:8, :] = jnp.zeros((3, count), F32)
    data[8:12, :] = weight_ref[...]
    data[12:13, :] = value_ref[...]
    data[13:14, :] = rinv_ref[...]
    data[14:16, :] = jnp.zeros((2, count), F32)
    parts = jnp.concatenate(split3(data[...]), axis=0)
    got = jnp.dot(parts, hit[...], preferred_element_type=F32)
    sums = got[:FIELDS] + got[FIELDS : 2 * FIELDS] + got[2 * FIELDS :]
    last = out.shape[1] - ROWS
    for g in range(groups):
        part = sums[:, g * CAP : (g + 1) * CAP]
        out[g, pl.ds(last, ROWS), 0:CAP] = part[0:ROWS]
        out[g, pl.ds(last, ROWS), CAP : 2 * CAP] = part[ROWS:FIELDS]


def prep_kernel(groups, levels, tiles, pairs, got_hbm, idx_ref, w_ref, vr_ref, got, scr, columns, sem):
    last = got_hbm.shape[1] - ROWS
    load = pltpu.make_async_copy(got_hbm.at[:, pl.ds(last, ROWS), :], got, sem)
    load.start()
    scr[...] = jnp.zeros_like(scr)
    load.wait()
    lon = tiles * LANES
    for g in range(groups):
        part = pl.ds(g * CAP, CAP)
        ints = got[g, :, 0:CAP].astype(I32)
        cell = ints[0:4]
        time = ints[4:5]
        lev = cell // (ROWS * lon)
        row = (cell // lon) % ROWS
        col = cell % lon
        if pairs:
            side, lane_at = col // (2 * LANES) * 2 + col % 2, col % (2 * LANES) // 2
        else:
            side, lane_at = col // LANES, col % LANES
        tile = (time * levels + lev) * tiles + side
        scr[0:4, part] = (tile * 16 + (row % 2) * 8 + row // 2).astype(F32)
        scr[8:12, part] = lane_at.astype(F32)
        scr[16:24, part] = got[g, :, CAP : 2 * CAP]
        scr[32:36, part] = (tile * 8 + (row % 2) * 4 + row // 2).astype(F32)
    slots = groups * CAP
    lane = lax.broadcasted_iota(I32, (LANES, LANES), 1)
    few = LANES // 8
    narrow = lax.broadcasted_iota(I32, (few, LANES), 1)
    for b in range(slots // LANES):
        rows = pl.ds(b * LANES, LANES)
        cols = jnp.transpose(scr[:, rows], (1, 0))
        for k in range(4):
            at = cols[:, 8 + k : 9 + k].astype(I32)
            w_ref[k, rows, :] = jnp.where(lane == at, cols[:, 16 + k : 17 + k], 0.0)
        vr_ref[0, rows, :] = jnp.broadcast_to(cols[:, 20:21], (LANES, LANES))
        vr_ref[1, rows, :] = jnp.broadcast_to(cols[:, 21:22], (LANES, LANES))
        columns[...] = cols
        index = jnp.zeros((few, LANES), F32)
        for j in range(8):
            here = columns[pl.ds(j, few, stride=8), :]
            index = jnp.where((narrow // 4) % 8 == j, pltpu.roll(here, 4 * j, 1) if j else here, index)
        idx_ref[pl.ds(b * few, few), :] = index.astype(I32)


NSCRATCH = 13


def cycle_kernel(
    groups,
    levels,
    tiles,
    field,
    halo,
    uw_hbm,
    vw_hbm,
    idx_ref,
    w,
    vr,
    front_ref,
    *refs,
):
    own_out, rim_out = refs[: -NSCRATCH]
    (uw, vw, states, f0, f1, f2, f3, scr, acc, dep_ref, idx, sem, lsems) = refs[
        -NSCRATCH:
    ]
    forcing = (f0, f1, f2, f3)
    slots = acc.shape[0]
    per = tiles // groups
    pairs = per % 2 == 0
    block = tiles * 16
    def wind_loads(l):
        return (
            pltpu.make_async_copy(uw_hbm.at[l], uw.at[l], lsems.at[0, l]),
            pltpu.make_async_copy(vw_hbm.at[l], vw.at[l], lsems.at[1, l]),
        )

    for l in range(levels):
        for copy in wind_loads(l):
            copy.start()
    load = pltpu.make_async_copy(idx_ref, idx, sem)
    load.start()

    lane = lax.broadcasted_iota(I32, (8, LANES), 1)
    first = lane == 0
    last = lane == LANES - 1
    sub = lax.broadcasted_iota(I32, (8, LANES), 0)
    own = sub < 4
    zero = jnp.zeros((8, LANES), F32)

    def forward(l, carry):
        for copy in wind_loads(l):
            copy.wait()
        start = pl.multiple_of(l * block, block)
        for c in range(tiles):
            j, h = divmod(c, per)
            at = pl.ds(pl.multiple_of((h * levels + l) * 8, 8), 8)
            scr[pl.ds(c * 16, 8), :] = field[j, at, :]
            scr[pl.ds(c * 16 + 8, 8), :] = halo[j, at, :] * front_ref[...]
        for c in range(tiles):
            states[pl.ds(start + c * 16, 8), :] = scr[pl.ds(c * 16, 8, stride=2), :]
            states[pl.ds(start + c * 16 + 8, 8), :] = scr[pl.ds(c * 16 + 1, 8, stride=2), :]
        fstart = pl.multiple_of(l * tiles * 8, tiles * 8)
        fstep = levels * tiles * 8
        for t in range(NT):
            src = pl.multiple_of(start + t * levels * block, block)
            dst = pl.multiple_of(start + (t + 1) * levels * block, block)

            held = {}

            def tile(c, side):
                if (c, side) not in held:
                    held[c, side] = states[pl.ds(src + c % tiles * 16 + side * 8, 8), :]
                return held[c, side]

            east, west = neighbours(tile, pairs, first, last)
            for c in range(tiles):
                even, odd = tile(c, 0), tile(c, 1)
                souths = (pltpu.roll(odd, 1, 0), even)
                norths = (odd, pltpu.roll(even, 7, 0))
                for side in range(2):
                    here = tile(c, side)
                    at = pl.ds(c * 16 + side * 8, 8)
                    u = uw[l, at, :]
                    v = vw[l, at, :]
                    lon = jnp.where(u > 0, west(c, side), east(c, side))
                    lat = jnp.where(v > 0, souths[side], norths[side])
                    states[pl.ds(dst + c * 16 + side * 8, 8), :] = (
                        here + jnp.abs(u) * (lon - here) + jnp.abs(v) * (lat - here)
                    )
                for f in forcing:
                    f[pl.ds(pl.multiple_of(fstart + t * fstep, 8) + c * 8, 8), :] = zero
                    if t == NT - 1:
                        f[pl.ds(pl.multiple_of(fstart + NT * fstep, 8) + c * 8, 8), :] = zero
        return carry

    lax.fori_loop(0, levels, forward, 0)

    load.wait()

    def gather(i, carry):
        base = pl.multiple_of(i * 8, 8)
        for j in range(8):
            total = None
            for k in range(4):
                term = w[k, pl.ds(base + j, 1), :] * states[pl.ds(idx[i, j * 4 + k], 1), :]
                total = term if total is None else total + term
            acc[pl.ds(base + j, 1), :] = total
        return carry

    lax.fori_loop(0, slots // 8, gather, 0, unroll=4)

    hx = jnp.sum(acc[...], axis=1, keepdims=True)
    dep_ref[...] = vr[1] * (hx - vr[0])
    tail = pl.ds(per * levels * 8, 8)
    for b in range(slots // LANES):
        row = to_row(dep_ref[pl.ds(b * LANES, LANES), :])
        for h in range(LANES // CAP):
            own_out[b * (LANES // CAP) + h, tail, 0:CAP] = jnp.broadcast_to(
                row[:, h * CAP : (h + 1) * CAP], (8, CAP)
            )
            own_out[b * (LANES // CAP) + h, tail, CAP:LANES] = jnp.zeros((8, LANES - CAP), F32)

    def scatter(i, carry):
        base = pl.multiple_of(i * 8, 8)
        for j in range(8):
            dep = dep_ref[pl.ds(base + j, 1), :]
            for k in range(4):
                at = pl.ds(idx[i, 32 + j * 4 + k], 1)
                forcing[k][at, :] = forcing[k][at, :] + w[k, pl.ds(base + j, 1), :] * dep
        return carry

    lax.fori_loop(0, slots // 8, scatter, 0, unroll=2)

    def backward(l, carry):
        fstart = pl.multiple_of(l * tiles * 8, tiles * 8)
        fstep = levels * tiles * 8

        def force(t, c):
            at = pl.ds(pl.multiple_of(fstart + t * fstep, 8) + c * 8, 8)
            total = (f0[at, :] + f1[at, :]) + (f2[at, :] + f3[at, :])
            return (jnp.where(own, total, 0.0), jnp.where(own, pltpu.roll(total, 4, 0), 0.0))

        def fluxes(ref):
            held = {}

            def flux(c, side):
                if (c, side) not in held:
                    at = pl.ds(c % tiles * 16 + side * 8, 8)
                    a = ref[at, :]
                    u = uw[l, at, :]
                    v = vw[l, at, :]
                    x = jnp.abs(u) * a
                    y = jnp.abs(v) * a
                    p = jnp.where(u > 0, x, 0.0)
                    s = jnp.where(v > 0, y, 0.0)
                    held[c, side] = (a - x - y, p, x - p, s, y - s)
                return held[c, side]

            return flux

        for c in range(tiles):
            even, odd = force(NT, c)
            scr[pl.ds(c * 16, 8), :] = even
            scr[pl.ds(c * 16 + 8, 8), :] = odd
        half = tiles * 16
        for t in range(NT - 1, -1, -1):
            src = scr.at[pl.ds(0 if t % 2 else half, half)]
            dst = scr.at[pl.ds(half if t % 2 else 0, half)]
            flux = fluxes(src)
            east, _ = neighbours(lambda c, side: flux(c, side)[1], pairs, first, last)
            _, west = neighbours(lambda c, side: flux(c, side)[2], pairs, first, last)
            for c in range(tiles):
                fine = force(t, c)
                (_, _, _, s_e, n_e), (_, _, _, s_o, n_o) = flux(c, 0), flux(c, 1)
                lats = (s_o + pltpu.roll(n_o, 1, 0), pltpu.roll(s_e, 7, 0) + n_e)
                for side in range(2):
                    value = (
                        (flux(c, side)[0] + east(c, side))
                        + (west(c, side) + lats[side])
                        + fine[side]
                    )
                    dst[pl.ds(c * 16 + side * 8, 8), :] = value
        for c in range(tiles):
            even = scr[pl.ds(c * 16, 8), :]
            odd = scr[pl.ds(c * 16 + 8, 8), :]
            scr[pl.ds(half + c * 16, 8, stride=2), :] = even
            scr[pl.ds(half + c * 16 + 1, 8, stride=2), :] = odd
        for c in range(tiles):
            j, h = divmod(c, per)
            at = pl.ds(pl.multiple_of((h * levels + l) * 8, 8), 8)
            own_out[j, at, :] = scr[pl.ds(half + c * 16, 8), :]
            rim_out[j, at, :] = scr[pl.ds(half + c * 16 + 8, 8), :]
        return carry

    lax.fori_loop(0, levels, backward, 0)


def per_device(
    control,
    spread,
    vert_root,
    wind_lon,
    wind_lat,
    obs_dest,
    obs_cells,
    obs_time,
    obs_value,
    obs_weight,
    obs_rinv,
):
    levels_all, _, width = control.shape
    groups = lax.axis_size("horiz")
    levels, _, lon = wind_lon.shape
    tiles = lon // LANES
    slots = groups * CAP
    count = obs_value.shape[0]
    halves = width // LANES
    rows = halves * levels * ROWS
    front, back = halo_masks()
    flat = (levels_all * ROWS, width)
    payload = jax.ShapeDtypeStruct((groups, rows + ROWS, LANES), F32)
    vmem = lambda *shape: pltpu.VMEM(shape, F32)
    ivmem = lambda *shape: pltpu.VMEM(shape, I32)

    outgoing, placed = call(
        functools.partial(start_kernel, groups),
        (payload, jax.ShapeDtypeStruct((count // LANES, LANES), F32)),
        [ANY] * 9,
        (ANY, VM),
        [
            vmem(*vert_root.shape),
            vmem(halves, flat[0], LANES),
            vmem(halves, flat[0], LANES),
            ivmem(1, count),
            ivmem(4, count),
            ivmem(1, count),
            vmem(1, count),
            vmem(4, count),
            vmem(1, count),
            vmem(*payload.shape),
            vmem(FIELDS, count),
            pltpu.VMEM((count, slots), jnp.bfloat16),
            pltpu.SemaphoreType.DMA((7,)),
            pltpu.SemaphoreType.DMA((2, halves)),
            pltpu.SemaphoreType.DMA((halves,)),
        ],
        limit=56,
        cost=(4e8, 4e6),
    )(
        vert_root,
        control.reshape(flat),
        spread.reshape(flat),
        obs_dest.reshape(1, count),
        obs_cells,
        obs_time[None],
        obs_value[None],
        obs_weight,
        obs_rinv[None],
    )
    field = lax.all_to_all(outgoing, "horiz", split_axis=0, concat_axis=0, tiled=True)

    ring = jax.ShapeDtypeStruct((levels, tiles * 16, LANES), F32)
    uw, vw = call(
        functools.partial(wind_kernel, tiles, halves % 2 == 0),
        (ring, ring),
        [VM] * 5,
        (VM, VM),
        [vmem(tiles * 16, LANES)],
        limit=14,
        cost=(1e6, 8e6),
    )(wind_lon, exchange(wind_lon, True), wind_lat, exchange(wind_lat, True), front)
    field, uw, vw, front, back = lax.optimization_barrier((field, uw, vw, front, back))

    halo = exchange(field, True)
    idx, weights, pair = call(
        functools.partial(prep_kernel, groups, levels, tiles, halves % 2 == 0),
        (
            jax.ShapeDtypeStruct((slots // 8, LANES), I32),
            jax.ShapeDtypeStruct((4, slots, LANES), F32),
            jax.ShapeDtypeStruct((2, slots, LANES), F32),
        ),
        [ANY],
        (VM, VM, VM),
        [
            vmem(groups, ROWS, LANES),
            vmem(LANES, slots),
            vmem(LANES, LANES),
            pltpu.SemaphoreType.DMA,
        ],
        limit=8,
        cost=(1e6, 6e6),
    )(field)

    forcing = vmem((NT + 1) * levels * tiles * 8, LANES)
    adjoint, rim = call(
        functools.partial(cycle_kernel, groups, levels, tiles),
        (payload, jax.ShapeDtypeStruct((groups, rows, LANES), F32)),
        [VM, VM, ANY, ANY] + [VM] * 4,
        (VM, VM),
        [
            vmem(levels, tiles * 16, LANES),
            vmem(levels, tiles * 16, LANES),
            vmem((NT + 1) * levels * tiles * 16, LANES),
            forcing,
            forcing,
            forcing,
            forcing,
            vmem(2 * tiles * 16, LANES),
            vmem(slots, LANES),
            vmem(slots, LANES),
            pltpu.SMEM((slots // 8, LANES), I32),
            pltpu.SemaphoreType.DMA,
            pltpu.SemaphoreType.DMA((2, levels)),
        ],
        limit=38,
        cost=(1e8, 16e6),
    )(field, halo, uw, vw, idx, weights, pair, front)

    part = groups // 4
    total = call(
        rim_kernel,
        payload,
        [
            pl.BlockSpec((part, rows + ROWS, LANES), lambda i: (i, 0, 0)),
            pl.BlockSpec((part, rows, LANES), lambda i: (i, 0, 0)),
            pl.BlockSpec((ROWS, LANES), lambda i: (0, 0)),
        ],
        pl.BlockSpec((part, rows + ROWS, LANES), lambda i: (i, 0, 0)),
        limit=8,
        cost=(1e6, 3e6),
        grid=(4,),
    )(adjoint, exchange(rim, False), back)
    column = lax.all_to_all(total, "horiz", split_axis=0, concat_axis=0, tiled=True)

    gradient, departure = call(
        functools.partial(end_kernel, groups),
        (
            jax.ShapeDtypeStruct(flat, F32),
            jax.ShapeDtypeStruct((count // LANES, LANES), F32),
        ),
        [VM] * 5,
        (ANY, VM),
        [vmem(halves, flat[0], LANES)] * 3 + [vmem(8, slots), pltpu.SemaphoreType.DMA((halves,))],
        limit=14,
        cost=(4e8, 4e6),
    )(vert_root.T, control.reshape(flat), spread.reshape(flat), column, placed)
    return (gradient.reshape(control.shape), departure.reshape(count))


def solution(mesh):
    in_specs = (
        P(None, "obs", "horiz"),
        P(None, "obs", "horiz"),
        P(),
        P("horiz", "obs", None),
        P("horiz", "obs", None),
        P(("obs", "horiz"), None),
        P(None, ("obs", "horiz")),
        P(("obs", "horiz")),
        P(("obs", "horiz")),
        P(None, ("obs", "horiz")),
        P(("obs", "horiz")),
    )
    out_specs = (P(None, "obs", "horiz"), P(("obs", "horiz")))
    return jax.shard_map(
        per_device, mesh=mesh, in_specs=in_specs, out_specs=out_specs, check_vma=False
    )
```

```python
import functools

import jax
import jax.numpy as jnp
from jax import lax
from jax.experimental import pallas as pl
from jax.experimental.pallas import tpu as pltpu
from jax.sharding import PartitionSpec as P

NT = 4
CAP = 64
ROWS = 8
LANES = 128
FIELDS = 16
F32 = jnp.float32
I32 = jnp.int32
ANY = pl.BlockSpec(memory_space=pl.ANY)
VM = pl.BlockSpec(memory_space=pltpu.VMEM)


def call(body, out_shape, in_specs, out_specs, scratch=(), limit=40, cost=(1e6, 1e6), grid=()):
    return pl.pallas_call(
        body,
        out_shape=out_shape,
        grid=grid,
        in_specs=in_specs,
        out_specs=out_specs,
        scratch_shapes=list(scratch),
        compiler_params=pltpu.CompilerParams(vmem_limit_bytes=limit * 2**20),
        cost_estimate=pl.CostEstimate(
            flops=int(cost[0]), bytes_accessed=int(cost[1]), transcendentals=0
        ),
    )


def split2(x):
    a = x.astype(jnp.bfloat16)
    return a, (x - a.astype(F32)).astype(jnp.bfloat16)


def wide_root(root):
    high, low = split2(root)
    return jnp.concatenate([high, high, low], axis=1)


def apply_root(wide, columns):
    high, low = split2(columns)
    return jnp.dot(wide, jnp.concatenate([high, low, high], axis=0), preferred_element_type=F32)


def level_rows(r, levels):
    return pl.ds(r, levels, stride=ROWS)


def start_kernel(
    groups,
    root_hbm,
    control_hbm,
    spread_hbm,
    dest_hbm,
    cells_hbm,
    time_hbm,
    value_hbm,
    weight_hbm,
    rinv_hbm,
    out_hbm,
    placed_ref,
    root,
    control,
    spread,
    dest,
    cells,
    time,
    value,
    weight,
    rinv,
    out,
    data,
    hit,
    small_sems,
    sems,
    out_sems,
):
    levels_all = root.shape[0]
    levels = levels_all // groups
    halves = control.shape[0]
    smalls = [
        pltpu.make_async_copy(a, b, small_sems.at[i])
        for i, (a, b) in enumerate(
            (
                (dest_hbm, dest),
                (cells_hbm, cells),
                (time_hbm, time),
                (value_hbm, value),
                (weight_hbm, weight),
                (rinv_hbm, rinv),
                (root_hbm, root),
            )
        )
    ]
    for copy in smalls:
        copy.start()

    def part(h):
        cols = pl.ds(h * LANES, LANES)
        return (
            pltpu.make_async_copy(control_hbm.at[:, cols], control.at[h], sems.at[0, h]),
            pltpu.make_async_copy(spread_hbm.at[:, cols], spread.at[h], sems.at[1, h]),
        )

    parts = [part(h) for h in range(halves)]
    for i in range(2):
        for h in range(halves):
            parts[h][i].start()
    for copy in smalls:
        copy.wait()
    bin_observations(groups, dest, cells, time, value, weight, rinv, placed_ref, out, data, hit)
    wide = wide_root(root[...])
    block = levels * ROWS
    outs = []
    pairs = halves % 2 == 0
    for h in range(halves):
        parts[h][0].wait()
    for h in range(halves):
        parts[h][1].wait()
    for m in range(0, halves, 2 if pairs else 1):
        for r in range(ROWS):
            at = level_rows(r, levels_all)
            if pairs:
                both = apply_root(
                    wide, jnp.concatenate([control[m, at, :], control[m + 1, at, :]], axis=1)
                )
                both = both * jnp.concatenate([spread[m, at, :], spread[m + 1, at, :]], axis=1)
                both = reorder(both, even_odd(), split2)
                values = [both[:, 0:LANES], both[:, LANES:]]
            else:
                values = [spread[m, at, :] * apply_root(wide, control[m, at, :])]
            for i, value_r in enumerate(values):
                for g in range(groups):
                    out[g, pl.ds((m + i) * block + r, levels, stride=ROWS), :] = value_r[
                        g * levels : (g + 1) * levels
                    ]
    outs.append(pltpu.make_async_copy(out, out_hbm, out_sems.at[0]))
    outs[-1].start()
    for copy in outs:
        copy.wait()


def end_kernel(groups, root_ref, control_ref, spread_ref, got_ref, placed_ref, out_hbm, dep_ref, control, spread, out, row, sems):
    levels_all = root_ref.shape[0]
    levels = levels_all // groups
    halves = out.shape[0]
    block = levels * ROWS
    wide = wide_root(root_ref[...])
    outs = []
    pairs = halves % 2 == 0
    for h in range(halves):
        cols = pl.ds(h * LANES, LANES)
        control[h] = control_ref[:, cols]
        spread[h] = spread_ref[:, cols]
    for m in range(0, halves, 2 if pairs else 1):
        for r in range(ROWS):
            at = level_rows(r, levels_all)
            half = [
                jnp.concatenate(
                    [
                        got_ref[g, pl.ds(h * block + r, levels, stride=ROWS), :]
                        for g in range(groups)
                    ],
                    axis=0,
                )
                for h in range(m, m + (2 if pairs else 1))
            ]
            if pairs:
                adjoint = reorder(jnp.concatenate(half, axis=1), even_odd(back=True), split2)
                both = apply_root(
                    wide, jnp.concatenate([spread[m, at, :], spread[m + 1, at, :]], axis=1) * adjoint
                )
                values = [both[:, 0:LANES], both[:, LANES:]]
            else:
                values = [apply_root(wide, spread[m, at, :] * half[0])]
            for i, value in enumerate(values):
                out[m + i, at, :] = control[m + i, at, :] + value
        for h in range(m, m + (2 if pairs else 1)):
            cols = pl.ds(h * LANES, LANES)
            outs.append(pltpu.make_async_copy(out.at[h], out_hbm.at[:, cols], sems.at[h]))
            outs[-1].start()
    for r in range(groups):
        row[0:1, r * CAP : (r + 1) * CAP] = got_ref[r, pl.ds(halves * block, 1), 0:CAP]
    lane = lax.broadcasted_iota(I32, (LANES, LANES), 1)
    for b in range(dep_ref.shape[0]):
        placed = to_column(placed_ref[pl.ds(b, 1), :]).astype(I32)
        total = jnp.zeros((LANES, LANES), F32)
        for c in range(groups * CAP // LANES):
            value = row[0:1, c * LANES : (c + 1) * LANES]
            total = total + jnp.where(lane + c * LANES == placed, value, 0.0)
        dep_ref[pl.ds(b, 1), :] = to_row(
            jnp.broadcast_to(jnp.sum(total, axis=1, keepdims=True), (LANES, LANES))
        )
    for copy in outs:
        copy.wait()


def rim_kernel(own_ref, rim_ref, mask_ref, out_ref):
    mask = mask_ref[...]
    rows = rim_ref.shape[1]
    for c in range(rows // ROWS):
        at = pl.ds(c * ROWS, ROWS)
        out_ref[:, at, :] = own_ref[:, at, :] + rim_ref[:, at, :] * mask[None]
    rest = pl.ds(rows, ROWS)
    out_ref[:, rest, :] = own_ref[:, rest, :]


def even_odd(back=False):
    row = lax.broadcasted_iota(I32, (2 * LANES, 2 * LANES), 0)
    col = lax.broadcasted_iota(I32, (2 * LANES, 2 * LANES), 1)
    if back:
        row, col = col, row
    return jnp.where(row == 2 * (col % LANES) + col // LANES, 1.0, 0.0).astype(jnp.bfloat16)


def reorder(x, order, split):
    parts = split(x)
    count = x.shape[0]
    got = jnp.dot(jnp.concatenate(parts, axis=0), order, preferred_element_type=F32)
    total = got[0:count]
    for i in range(1, len(parts)):
        total = total + got[i * count : (i + 1) * count]
    return total


def neighbours(value, pairs, first, last):
    made = {}

    def rolled(c, side, amount):
        key = (c, side, amount)
        if key not in made:
            made[key] = pltpu.roll(value(c, side), amount, 1)
        return made[key]

    def east(c, side):
        if pairs and c % 2 == 0:
            return value(c + 1, side)
        same, after = (c - 1, c + 1) if pairs else (c, c + 1)
        return jnp.where(last, rolled(after, side, LANES - 1), rolled(same, side, LANES - 1))

    def west(c, side):
        if pairs and c % 2:
            return value(c - 1, side)
        same, before = (c + 1, c - 1) if pairs else (c, c - 1)
        return jnp.where(first, rolled(before, side, 1), rolled(same, side, 1))

    return east, west


def exchange(tile_rows, toward):
    count = lax.axis_size("obs")
    if count == 2:
        return lax.ppermute(tile_rows, "obs", [(0, 1), (1, 0)])
    below = lax.ppermute(tile_rows, "obs", [(i, i + 1) for i in range(count - 1)])
    above = lax.ppermute(tile_rows, "obs", [(i + 1, i) for i in range(count - 1)])
    first = (jnp.arange(tile_rows.shape[1]) % ROWS < ROWS // 2)[None, :, None]
    return jnp.where(first, above, below) if toward else jnp.where(first, below, above)


def halo_masks():
    first = (jnp.arange(ROWS) < ROWS // 2)[:, None]
    if lax.axis_size("obs") == 2:
        lower = lax.axis_index("obs") == 0
        front = jnp.where(lower, first, ~first)
        back = ~front
    else:
        front = back = jnp.ones_like(first)
    wide = lambda m: jnp.broadcast_to(m, (ROWS, LANES)).astype(F32)
    return wide(front), wide(back)


def wind_kernel(tiles, pairs, u_ref, uh_ref, v_ref, vh_ref, mask_ref, uo_ref, vo_ref, scr):
    levels = u_ref.shape[0]

    def level(l, carry):
        for src, rim, dst in ((u_ref, uh_ref, uo_ref), (v_ref, vh_ref, vo_ref)):
            step = 2 if pairs else 1
            for c in range(0, tiles, step):
                cols = pl.ds(c * LANES, step * LANES)
                both = jnp.concatenate([src[l, :, cols], rim[l, :, cols]], axis=0)
                if pairs:
                    both = reorder(both, even_odd(), split3)
                for i in range(step):
                    lanes = slice(i * LANES, (i + 1) * LANES)
                    scr[pl.ds((c + i) * 16, 8), :] = both[0:8, lanes]
                    scr[pl.ds((c + i) * 16 + 8, 8), :] = both[8:16, lanes] * mask_ref[...]
            for c in range(tiles):
                dst[l, pl.ds(c * 16, 8), :] = scr[pl.ds(c * 16, 8, stride=2), :]
                dst[l, pl.ds(c * 16 + 8, 8), :] = scr[pl.ds(c * 16 + 1, 8, stride=2), :]
        return carry

    lax.fori_loop(0, levels, level, 0)


def split3(x):
    a = x.astype(jnp.bfloat16)
    r = x - a.astype(F32)
    b = r.astype(jnp.bfloat16)
    return a, b, (r - b.astype(F32)).astype(jnp.bfloat16)


def to_row(wide):
    at = lax.broadcasted_iota(I32, (LANES, LANES), 0) == lax.broadcasted_iota(I32, (LANES, LANES), 1)
    return jnp.sum(jnp.where(at, wide, 0.0), axis=0, keepdims=True)


def to_column(row):
    at = lax.broadcasted_iota(I32, (LANES, LANES), 0) == lax.broadcasted_iota(I32, (LANES, LANES), 1)
    return jnp.sum(jnp.where(at, row, 0.0), axis=1, keepdims=True)


def bin_observations(
    groups, dest_ref, cells_ref, time_ref, value_ref, weight_ref, rinv_ref, placed_ref, out, data, hit
):
    count = dest_ref.shape[1]
    slots = groups * CAP
    width = -(-groups // LANES) * LANES
    below = (
        lax.broadcasted_iota(I32, (LANES, LANES), 0) > lax.broadcasted_iota(I32, (LANES, LANES), 1)
    ).astype(jnp.bfloat16)
    lane = lax.broadcasted_iota(I32, (LANES, width), 1)
    slot_lane = lax.broadcasted_iota(I32, (LANES, slots), 1)
    seen = jnp.zeros((1, width), F32)
    target = dest_ref[...].astype(F32)
    for b in range(count // LANES):
        rows = pl.ds(b * LANES, LANES)
        owner = to_column(target[:, b * LANES : (b + 1) * LANES]).astype(I32)
        mine = (lane == owner).astype(F32)
        before = (
            jnp.dot(below, mine.astype(jnp.bfloat16), preferred_element_type=F32) + seen
        )
        rank = jnp.sum(before * mine, axis=1, keepdims=True)
        seen = seen + jnp.sum(mine, axis=0, keepdims=True)
        placed = owner * CAP + rank.astype(I32)
        placed_ref[pl.ds(b, 1), :] = to_row(
            jnp.broadcast_to(placed.astype(F32), (LANES, LANES))
        )
        hit[rows, :] = jnp.where(slot_lane == placed, 1.0, 0.0).astype(jnp.bfloat16)
    data[0:4, :] = cells_ref[...].astype(F32)
    data[4:5, :] = time_ref[...].astype(F32)
    data[5:8, :] = jnp.zeros((3, count), F32)
    data[8:12, :] = weight_ref[...]
    data[12:13, :] = value_ref[...]
    data[13:14, :] = rinv_ref[...]
    data[14:16, :] = jnp.zeros((2, count), F32)
    parts = jnp.concatenate(split3(data[...]), axis=0)
    got = jnp.dot(parts, hit[...], preferred_element_type=F32)
    sums = got[:FIELDS] + got[FIELDS : 2 * FIELDS] + got[2 * FIELDS :]
    last = out.shape[1] - ROWS
    for g in range(groups):
        part = sums[:, g * CAP : (g + 1) * CAP]
        out[g, pl.ds(last, ROWS), 0:CAP] = part[0:ROWS]
        out[g, pl.ds(last, ROWS), CAP : 2 * CAP] = part[ROWS:FIELDS]


def prep_kernel(
    groups,
    levels,
    tiles,
    pairs,
    got_hbm,
    uw_hbm,
    vw_hbm,
    idx_ref,
    w_ref,
    vr_ref,
    uw_ref,
    vw_ref,
    got,
    scr,
    columns,
    sem,
    wind_sems,
):
    last = got_hbm.shape[1] - ROWS
    load = pltpu.make_async_copy(got_hbm.at[:, pl.ds(last, ROWS), :], got, sem)
    load.start()
    winds = [
        pltpu.make_async_copy(uw_hbm, uw_ref, wind_sems.at[0]),
        pltpu.make_async_copy(vw_hbm, vw_ref, wind_sems.at[1]),
    ]
    for copy in winds:
        copy.start()
    scr[...] = jnp.zeros_like(scr)
    load.wait()
    lon = tiles * LANES
    for g in range(groups):
        part = pl.ds(g * CAP, CAP)
        ints = got[g, :, 0:CAP].astype(I32)
        cell = ints[0:4]
        time = ints[4:5]
        lev = cell // (ROWS * lon)
        row = (cell // lon) % ROWS
        col = cell % lon
        if pairs:
            side, lane_at = col // (2 * LANES) * 2 + col % 2, col % (2 * LANES) // 2
        else:
            side, lane_at = col // LANES, col % LANES
        tile = (time * levels + lev) * tiles + side
        scr[0:4, part] = (tile * 16 + (row % 2) * 8 + row // 2).astype(F32)
        scr[8:12, part] = lane_at.astype(F32)
        scr[16:24, part] = got[g, :, CAP : 2 * CAP]
        scr[32:36, part] = (tile * 8 + (row % 2) * 4 + row // 2).astype(F32)
    slots = groups * CAP
    lane = lax.broadcasted_iota(I32, (LANES, LANES), 1)
    few = LANES // 8
    narrow = lax.broadcasted_iota(I32, (few, LANES), 1)
    for b in range(slots // LANES):
        rows = pl.ds(b * LANES, LANES)
        cols = jnp.transpose(scr[:, rows], (1, 0))
        for k in range(4):
            at = cols[:, 8 + k : 9 + k].astype(I32)
            w_ref[k, rows, :] = jnp.where(lane == at, cols[:, 16 + k : 17 + k], 0.0)
        vr_ref[0, rows, :] = jnp.broadcast_to(cols[:, 20:21], (LANES, LANES))
        vr_ref[1, rows, :] = jnp.broadcast_to(cols[:, 21:22], (LANES, LANES))
        columns[...] = cols
        index = jnp.zeros((few, LANES), F32)
        for j in range(8):
            here = columns[pl.ds(j, few, stride=8), :]
            index = jnp.where((narrow // 4) % 8 == j, pltpu.roll(here, 4 * j, 1) if j else here, index)
        idx_ref[pl.ds(b * few, few), :] = index.astype(I32)
    for copy in winds:
        copy.wait()


NSCRATCH = 10


def cycle_kernel(
    groups,
    levels,
    tiles,
    field,
    halo,
    uw,
    vw,
    idx_ref,
    w,
    vr,
    front_ref,
    *refs,
):
    own_out, rim_out = refs[: -NSCRATCH]
    (states, f0, f1, f2, f3, scr, acc, dep_ref, idx, sem) = refs[
        -NSCRATCH:
    ]
    forcing = (f0, f1, f2, f3)
    slots = acc.shape[0]
    per = tiles // groups
    pairs = per % 2 == 0
    block = tiles * 16
    load = pltpu.make_async_copy(idx_ref, idx, sem)
    load.start()

    lane = lax.broadcasted_iota(I32, (8, LANES), 1)
    first = lane == 0
    last = lane == LANES - 1
    sub = lax.broadcasted_iota(I32, (8, LANES), 0)
    own = sub < 4
    zero = jnp.zeros((8, LANES), F32)

    def forward(l, carry):
        start = pl.multiple_of(l * block, block)
        for c in range(tiles):
            j, h = divmod(c, per)
            at = pl.ds(pl.multiple_of((h * levels + l) * 8, 8), 8)
            scr[pl.ds(c * 16, 8), :] = field[j, at, :]
            scr[pl.ds(c * 16 + 8, 8), :] = halo[j, at, :] * front_ref[...]
        for c in range(tiles):
            states[pl.ds(start + c * 16, 8), :] = scr[pl.ds(c * 16, 8, stride=2), :]
            states[pl.ds(start + c * 16 + 8, 8), :] = scr[pl.ds(c * 16 + 1, 8, stride=2), :]
        for t in range(NT):
            src = pl.multiple_of(start + t * levels * block, block)
            dst = pl.multiple_of(start + (t + 1) * levels * block, block)

            held = {}

            def tile(c, side):
                if (c, side) not in held:
                    held[c, side] = states[pl.ds(src + c % tiles * 16 + side * 8, 8), :]
                return held[c, side]

            east, west = neighbours(tile, pairs, first, last)
            for c in range(tiles):
                even, odd = tile(c, 0), tile(c, 1)
                souths = (pltpu.roll(odd, 1, 0), even)
                norths = (odd, pltpu.roll(even, 7, 0))
                for side in range(2):
                    here = tile(c, side)
                    at = pl.ds(c * 16 + side * 8, 8)
                    u = uw[l, at, :]
                    v = vw[l, at, :]
                    lon = jnp.where(u > 0, west(c, side), east(c, side))
                    lat = jnp.where(v > 0, souths[side], norths[side])
                    states[pl.ds(dst + c * 16 + side * 8, 8), :] = (
                        here + jnp.abs(u) * (lon - here) + jnp.abs(v) * (lat - here)
                    )
        return carry

    lax.fori_loop(0, levels, forward, 0)

    load.wait()

    share = f0.shape[0] // (slots // 16)

    def gather(i, carry):
        start = pl.multiple_of(i * share, 8)
        for f in forcing:
            for c in range(share // 8):
                f[pl.ds(start + c * 8, 8), :] = zero
        for half in range(2):
            group = i * 2 + half
            base = pl.multiple_of(group * 8, 8)
            for j in range(8):
                total = None
                for k in range(4):
                    term = (
                        w[k, pl.ds(base + j, 1), :] * states[pl.ds(idx[group, j * 4 + k], 1), :]
                    )
                    total = term if total is None else total + term
                acc[pl.ds(base + j, 1), :] = total
        return carry

    lax.fori_loop(0, slots // 16, gather, 0, unroll=2)

    hx = jnp.sum(acc[...], axis=1, keepdims=True)
    dep_ref[...] = vr[1] * (hx - vr[0])
    tail = pl.ds(per * levels * 8, 8)
    for b in range(slots // LANES):
        row = to_row(dep_ref[pl.ds(b * LANES, LANES), :])
        for h in range(LANES // CAP):
            own_out[b * (LANES // CAP) + h, tail, 0:CAP] = jnp.broadcast_to(
                row[:, h * CAP : (h + 1) * CAP], (8, CAP)
            )
            own_out[b * (LANES // CAP) + h, tail, CAP:LANES] = jnp.zeros((8, LANES - CAP), F32)

    def scatter(i, carry):
        base = pl.multiple_of(i * 8, 8)
        for j in range(8):
            dep = dep_ref[pl.ds(base + j, 1), :]
            for k in range(4):
                at = pl.ds(idx[i, 32 + j * 4 + k], 1)
                forcing[k][at, :] = forcing[k][at, :] + w[k, pl.ds(base + j, 1), :] * dep
        return carry

    lax.fori_loop(0, slots // 8, scatter, 0, unroll=2)

    def backward(l, carry):
        fstart = pl.multiple_of(l * tiles * 8, tiles * 8)
        fstep = levels * tiles * 8

        def force(t, c):
            at = pl.ds(pl.multiple_of(fstart + t * fstep, 8) + c * 8, 8)
            total = (f0[at, :] + f1[at, :]) + (f2[at, :] + f3[at, :])
            return (jnp.where(own, total, 0.0), jnp.where(own, pltpu.roll(total, 4, 0), 0.0))

        def fluxes(ref):
            held = {}

            def flux(c, side):
                if (c, side) not in held:
                    at = pl.ds(c % tiles * 16 + side * 8, 8)
                    a = ref[at, :]
                    u = uw[l, at, :]
                    v = vw[l, at, :]
                    x = jnp.abs(u) * a
                    y = jnp.abs(v) * a
                    p = jnp.where(u > 0, x, 0.0)
                    s = jnp.where(v > 0, y, 0.0)
                    held[c, side] = (a - x - y, p, x - p, s, y - s)
                return held[c, side]

            return flux

        for c in range(tiles):
            even, odd = force(NT, c)
            scr[pl.ds(c * 16, 8), :] = even
            scr[pl.ds(c * 16 + 8, 8), :] = odd
        half = tiles * 16
        for t in range(NT - 1, -1, -1):
            src = scr.at[pl.ds(0 if t % 2 else half, half)]
            dst = scr.at[pl.ds(half if t % 2 else 0, half)]
            flux = fluxes(src)
            east, _ = neighbours(lambda c, side: flux(c, side)[1], pairs, first, last)
            _, west = neighbours(lambda c, side: flux(c, side)[2], pairs, first, last)
            for c in range(tiles):
                fine = force(t, c)
                (_, _, _, s_e, n_e), (_, _, _, s_o, n_o) = flux(c, 0), flux(c, 1)
                lats = (s_o + pltpu.roll(n_o, 1, 0), pltpu.roll(s_e, 7, 0) + n_e)
                for side in range(2):
                    value = (
                        (flux(c, side)[0] + east(c, side))
                        + (west(c, side) + lats[side])
                        + fine[side]
                    )
                    dst[pl.ds(c * 16 + side * 8, 8), :] = value
        for c in range(tiles):
            even = scr[pl.ds(c * 16, 8), :]
            odd = scr[pl.ds(c * 16 + 8, 8), :]
            scr[pl.ds(half + c * 16, 8, stride=2), :] = even
            scr[pl.ds(half + c * 16 + 1, 8, stride=2), :] = odd
        for c in range(tiles):
            j, h = divmod(c, per)
            at = pl.ds(pl.multiple_of((h * levels + l) * 8, 8), 8)
            own_out[j, at, :] = scr[pl.ds(half + c * 16, 8), :]
            rim_out[j, at, :] = scr[pl.ds(half + c * 16 + 8, 8), :]
        return carry

    lax.fori_loop(0, levels, backward, 0)


def per_device(
    control,
    spread,
    vert_root,
    wind_lon,
    wind_lat,
    obs_dest,
    obs_cells,
    obs_time,
    obs_value,
    obs_weight,
    obs_rinv,
):
    levels_all, _, width = control.shape
    groups = lax.axis_size("horiz")
    levels, _, lon = wind_lon.shape
    tiles = lon // LANES
    slots = groups * CAP
    count = obs_value.shape[0]
    halves = width // LANES
    rows = halves * levels * ROWS
    front, back = halo_masks()
    flat = (levels_all * ROWS, width)
    payload = jax.ShapeDtypeStruct((groups, rows + ROWS, LANES), F32)
    vmem = lambda *shape: pltpu.VMEM(shape, F32)
    ivmem = lambda *shape: pltpu.VMEM(shape, I32)

    outgoing, placed = call(
        functools.partial(start_kernel, groups),
        (payload, jax.ShapeDtypeStruct((count // LANES, LANES), F32)),
        [ANY] * 9,
        (ANY, VM),
        [
            vmem(*vert_root.shape),
            vmem(halves, flat[0], LANES),
            vmem(halves, flat[0], LANES),
            ivmem(1, count),
            ivmem(4, count),
            ivmem(1, count),
            vmem(1, count),
            vmem(4, count),
            vmem(1, count),
            vmem(*payload.shape),
            vmem(FIELDS, count),
            pltpu.VMEM((count, slots), jnp.bfloat16),
            pltpu.SemaphoreType.DMA((7,)),
            pltpu.SemaphoreType.DMA((2, halves)),
            pltpu.SemaphoreType.DMA((halves,)),
        ],
        limit=56,
        cost=(4e8, 4e6),
    )(
        vert_root,
        control.reshape(flat),
        spread.reshape(flat),
        obs_dest.reshape(1, count),
        obs_cells,
        obs_time[None],
        obs_value[None],
        obs_weight,
        obs_rinv[None],
    )
    field = lax.all_to_all(outgoing, "horiz", split_axis=0, concat_axis=0, tiled=True)

    ring = jax.ShapeDtypeStruct((levels, tiles * 16, LANES), F32)
    uw, vw = call(
        functools.partial(wind_kernel, tiles, halves % 2 == 0),
        (ring, ring),
        [VM] * 5,
        (VM, VM),
        [vmem(tiles * 16, LANES)],
        limit=14,
        cost=(1e6, 8e6),
    )(wind_lon, exchange(wind_lon, True), wind_lat, exchange(wind_lat, True), front)
    field, uw, vw, front, back = lax.optimization_barrier((field, uw, vw, front, back))

    halo = exchange(field, True)
    idx, weights, pair, uw, vw = call(
        functools.partial(prep_kernel, groups, levels, tiles, halves % 2 == 0),
        (
            jax.ShapeDtypeStruct((slots // 8, LANES), I32),
            jax.ShapeDtypeStruct((4, slots, LANES), F32),
            jax.ShapeDtypeStruct((2, slots, LANES), F32),
            ring,
            ring,
        ),
        [ANY] * 3,
        (VM,) * 5,
        [
            vmem(groups, ROWS, LANES),
            vmem(LANES, slots),
            vmem(LANES, LANES),
            pltpu.SemaphoreType.DMA,
            pltpu.SemaphoreType.DMA((2,)),
        ],
        limit=44,
        cost=(1e6, 6e6),
    )(field, uw, vw)

    forcing = vmem((NT + 1) * levels * tiles * 8, LANES)
    adjoint, rim = call(
        functools.partial(cycle_kernel, groups, levels, tiles),
        (payload, jax.ShapeDtypeStruct((groups, rows, LANES), F32)),
        [VM] * 8,
        (VM, VM),
        [
            vmem((NT + 1) * levels * tiles * 16, LANES),
            forcing,
            forcing,
            forcing,
            forcing,
            vmem(2 * tiles * 16, LANES),
            vmem(slots, LANES),
            vmem(slots, LANES),
            pltpu.SMEM((slots // 8, LANES), I32),
            pltpu.SemaphoreType.DMA,
        ],
        limit=34,
        cost=(1e8, 16e6),
    )(field, halo, uw, vw, idx, weights, pair, front)

    part = groups // 4
    total = call(
        rim_kernel,
        payload,
        [
            pl.BlockSpec((part, rows + ROWS, LANES), lambda i: (i, 0, 0)),
            pl.BlockSpec((part, rows, LANES), lambda i: (i, 0, 0)),
            pl.BlockSpec((ROWS, LANES), lambda i: (0, 0)),
        ],
        pl.BlockSpec((part, rows + ROWS, LANES), lambda i: (i, 0, 0)),
        limit=8,
        cost=(1e6, 3e6),
        grid=(4,),
    )(adjoint, exchange(rim, False), back)
    column = lax.all_to_all(total, "horiz", split_axis=0, concat_axis=0, tiled=True)

    gradient, departure = call(
        functools.partial(end_kernel, groups),
        (
            jax.ShapeDtypeStruct(flat, F32),
            jax.ShapeDtypeStruct((count // LANES, LANES), F32),
        ),
        [VM] * 5,
        (ANY, VM),
        [vmem(halves, flat[0], LANES)] * 3 + [vmem(8, slots), pltpu.SemaphoreType.DMA((halves,))],
        limit=14,
        cost=(4e8, 4e6),
    )(vert_root.T, control.reshape(flat), spread.reshape(flat), column, placed)
    return (gradient.reshape(control.shape), departure.reshape(count))


def solution(mesh):
    in_specs = (
        P(None, "obs", "horiz"),
        P(None, "obs", "horiz"),
        P(),
        P("horiz", "obs", None),
        P("horiz", "obs", None),
        P(("obs", "horiz"), None),
        P(None, ("obs", "horiz")),
        P(("obs", "horiz")),
        P(("obs", "horiz")),
        P(None, ("obs", "horiz")),
        P(("obs", "horiz")),
    )
    out_specs = (P(None, "obs", "horiz"), P(("obs", "horiz")))
    return jax.shard_map(
        per_device, mesh=mesh, in_specs=in_specs, out_specs=out_specs, check_vma=False
    )
```

```python
import functools

import jax
import jax.numpy as jnp
from jax import lax
from jax.experimental import pallas as pl
from jax.experimental.pallas import tpu as pltpu
from jax.sharding import PartitionSpec as P

NT = 4
CAP = 64
ROWS = 8
LANES = 128
FIELDS = 16
F32 = jnp.float32
I32 = jnp.int32
ANY = pl.BlockSpec(memory_space=pl.ANY)
VM = pl.BlockSpec(memory_space=pltpu.VMEM)


def call(body, out_shape, in_specs, out_specs, scratch=(), limit=40, cost=(1e6, 1e6), grid=()):
    return pl.pallas_call(
        body,
        out_shape=out_shape,
        grid=grid,
        in_specs=in_specs,
        out_specs=out_specs,
        scratch_shapes=list(scratch),
        compiler_params=pltpu.CompilerParams(vmem_limit_bytes=limit * 2**20),
        cost_estimate=pl.CostEstimate(
            flops=int(cost[0]), bytes_accessed=int(cost[1]), transcendentals=0
        ),
    )


def split2(x):
    a = x.astype(jnp.bfloat16)
    return a, (x - a.astype(F32)).astype(jnp.bfloat16)


def wide_root(root):
    high, low = split2(root)
    return jnp.concatenate([high, high, low], axis=1)


def apply_root(wide, columns):
    high, low = split2(columns)
    return jnp.dot(wide, jnp.concatenate([high, low, high], axis=0), preferred_element_type=F32)


def level_rows(r, levels):
    return pl.ds(r, levels, stride=ROWS)


def start_kernel(
    groups,
    root_hbm,
    control_hbm,
    spread_hbm,
    dest_hbm,
    cells_hbm,
    time_hbm,
    value_hbm,
    weight_hbm,
    rinv_hbm,
    out_hbm,
    placed_ref,
    root,
    control,
    spread,
    dest,
    cells,
    time,
    value,
    weight,
    rinv,
    out,
    mid,
    data,
    hit,
    small_sems,
    sems,
    out_sems,
):
    levels_all = root.shape[0]
    levels = levels_all // groups
    halves = control.shape[0]
    smalls = [
        pltpu.make_async_copy(a, b, small_sems.at[i])
        for i, (a, b) in enumerate(
            (
                (dest_hbm, dest),
                (cells_hbm, cells),
                (time_hbm, time),
                (value_hbm, value),
                (weight_hbm, weight),
                (rinv_hbm, rinv),
                (root_hbm, root),
            )
        )
    ]
    for copy in smalls:
        copy.start()

    def part(h):
        cols = pl.ds(h * LANES, LANES)
        return (
            pltpu.make_async_copy(control_hbm.at[:, cols], control.at[h], sems.at[0, h]),
            pltpu.make_async_copy(spread_hbm.at[:, cols], spread.at[h], sems.at[1, h]),
        )

    parts = [part(h) for h in range(halves)]
    for i in range(2):
        for h in range(halves):
            parts[h][i].start()
    for copy in smalls:
        copy.wait()
    bin_observations(groups, dest, cells, time, value, weight, rinv, placed_ref, out, data, hit)
    wide = wide_root(root[...])
    block = levels * ROWS
    outs = []
    pairs = halves % 2 == 0
    step = 2 if pairs else 1
    for h in range(halves):
        parts[h][0].wait()
    for m in range(0, halves, step):
        for r in range(ROWS):
            at = level_rows(r, levels_all)
            columns = jnp.concatenate([control[m + i, at, :] for i in range(step)], axis=1)
            mid[m // step, r] = apply_root(wide, columns)
    for h in range(halves):
        parts[h][1].wait()
    share = groups // 2
    count = share * levels
    for p in range(2):
        for m in range(0, halves, step):
            for r in range(ROWS):
                at = pl.ds(p * count * ROWS + r, count, stride=ROWS)
                both = mid[m // step, r, pl.ds(p * count, count), :] * jnp.concatenate(
                    [spread[m + i, at, :] for i in range(step)], axis=1
                )
                if pairs:
                    both = reorder(both, even_odd(), split2)
                for i in range(step):
                    for g in range(share):
                        out[p * share + g, pl.ds((m + i) * block + r, levels, stride=ROWS), :] = both[
                            g * levels : (g + 1) * levels, i * LANES : (i + 1) * LANES
                        ]
        part_groups = pl.ds(p * share, share)
        outs.append(
            pltpu.make_async_copy(out.at[part_groups], out_hbm.at[part_groups], out_sems.at[p])
        )
        outs[-1].start()
    for copy in outs:
        copy.wait()


def end_kernel(groups, root_ref, control_ref, spread_ref, got_ref, placed_ref, out_hbm, dep_ref, control, spread, out, row, sems):
    levels_all = root_ref.shape[0]
    levels = levels_all // groups
    halves = out.shape[0]
    block = levels * ROWS
    wide = wide_root(root_ref[...])
    outs = []
    pairs = halves % 2 == 0
    for h in range(halves):
        cols = pl.ds(h * LANES, LANES)
        control[h] = control_ref[:, cols]
        spread[h] = spread_ref[:, cols]
    for m in range(0, halves, 2 if pairs else 1):
        for r in range(ROWS):
            at = level_rows(r, levels_all)
            half = [
                jnp.concatenate(
                    [
                        got_ref[g, pl.ds(h * block + r, levels, stride=ROWS), :]
                        for g in range(groups)
                    ],
                    axis=0,
                )
                for h in range(m, m + (2 if pairs else 1))
            ]
            if pairs:
                adjoint = reorder(jnp.concatenate(half, axis=1), even_odd(back=True), split2)
                both = apply_root(
                    wide, jnp.concatenate([spread[m, at, :], spread[m + 1, at, :]], axis=1) * adjoint
                )
                values = [both[:, 0:LANES], both[:, LANES:]]
            else:
                values = [apply_root(wide, spread[m, at, :] * half[0])]
            for i, value in enumerate(values):
                out[m + i, at, :] = control[m + i, at, :] + value
        for h in range(m, m + (2 if pairs else 1)):
            cols = pl.ds(h * LANES, LANES)
            outs.append(pltpu.make_async_copy(out.at[h], out_hbm.at[:, cols], sems.at[h]))
            outs[-1].start()
    for r in range(groups):
        row[0:1, r * CAP : (r + 1) * CAP] = got_ref[r, pl.ds(halves * block, 1), 0:CAP]
    lane = lax.broadcasted_iota(I32, (LANES, LANES), 1)
    for b in range(dep_ref.shape[0]):
        placed = to_column(placed_ref[pl.ds(b, 1), :]).astype(I32)
        total = jnp.zeros((LANES, LANES), F32)
        for c in range(groups * CAP // LANES):
            value = row[0:1, c * LANES : (c + 1) * LANES]
            total = total + jnp.where(lane + c * LANES == placed, value, 0.0)
        dep_ref[pl.ds(b, 1), :] = to_row(
            jnp.broadcast_to(jnp.sum(total, axis=1, keepdims=True), (LANES, LANES))
        )
    for copy in outs:
        copy.wait()


def rim_kernel(levels, packed, own_ref, rim_ref, mask_ref, out_ref):
    mask = mask_ref[...]
    rows = own_ref.shape[1] - ROWS
    for c in range(rows // ROWS):
        at = pl.ds(c * ROWS, ROWS)
        h, l = divmod(c, levels)
        for g in range(own_ref.shape[0]):
            if packed:
                rim = rim_ref[g, pl.ds((h // 2 * levels + l) * ROWS, ROWS), :]
                rim = pltpu.roll(rim, 4, 0) if h % 2 else rim
            else:
                rim = rim_ref[g, at, :]
            out_ref[g, at, :] = own_ref[g, at, :] + rim * mask
    rest = pl.ds(rows, ROWS)
    out_ref[:, rest, :] = own_ref[:, rest, :]


def even_odd(back=False):
    row = lax.broadcasted_iota(I32, (2 * LANES, 2 * LANES), 0)
    col = lax.broadcasted_iota(I32, (2 * LANES, 2 * LANES), 1)
    if back:
        row, col = col, row
    return jnp.where(row == 2 * (col % LANES) + col // LANES, 1.0, 0.0).astype(jnp.bfloat16)


def reorder(x, order, split):
    parts = split(x)
    count = x.shape[0]
    got = jnp.dot(jnp.concatenate(parts, axis=0), order, preferred_element_type=F32)
    total = got[0:count]
    for i in range(1, len(parts)):
        total = total + got[i * count : (i + 1) * count]
    return total


def neighbours(value, pairs, first, last):
    made = {}

    def rolled(c, side, amount):
        key = (c, side, amount)
        if key not in made:
            made[key] = pltpu.roll(value(c, side), amount, 1)
        return made[key]

    def east(c, side):
        if pairs and c % 2 == 0:
            return value(c + 1, side)
        same, after = (c - 1, c + 1) if pairs else (c, c + 1)
        return jnp.where(last, rolled(after, side, LANES - 1), rolled(same, side, LANES - 1))

    def west(c, side):
        if pairs and c % 2:
            return value(c - 1, side)
        same, before = (c + 1, c - 1) if pairs else (c, c - 1)
        return jnp.where(first, rolled(before, side, 1), rolled(same, side, 1))

    return east, west


def exchange(tile_rows, toward):
    count = lax.axis_size("obs")
    if count == 2:
        return lax.ppermute(tile_rows, "obs", [(0, 1), (1, 0)])
    below = lax.ppermute(tile_rows, "obs", [(i, i + 1) for i in range(count - 1)])
    above = lax.ppermute(tile_rows, "obs", [(i + 1, i) for i in range(count - 1)])
    first = (jnp.arange(tile_rows.shape[1]) % ROWS < ROWS // 2)[None, :, None]
    return jnp.where(first, above, below) if toward else jnp.where(first, below, above)


def halo_masks():
    first = (jnp.arange(ROWS) < ROWS // 2)[:, None]
    if lax.axis_size("obs") == 2:
        lower = lax.axis_index("obs") == 0
        front = jnp.where(lower, first, ~first)
        back = ~front
    else:
        front = back = jnp.ones_like(first)
    wide = lambda m: jnp.broadcast_to(m, (ROWS, LANES)).astype(F32)
    return wide(front), wide(back)


def wind_kernel(tiles, pairs, u_ref, uh_ref, v_ref, vh_ref, mask_ref, uo_ref, vo_ref, scr):
    levels = u_ref.shape[0]

    def level(l, carry):
        for src, rim, dst in ((u_ref, uh_ref, uo_ref), (v_ref, vh_ref, vo_ref)):
            step = 2 if pairs else 1
            for c in range(0, tiles, step):
                cols = pl.ds(c * LANES, step * LANES)
                both = jnp.concatenate([src[l, :, cols], rim[l, :, cols]], axis=0)
                if pairs:
                    both = reorder(both, even_odd(), split3)
                for i in range(step):
                    lanes = slice(i * LANES, (i + 1) * LANES)
                    scr[pl.ds((c + i) * 16, 8), :] = both[0:8, lanes]
                    scr[pl.ds((c + i) * 16 + 8, 8), :] = both[8:16, lanes] * mask_ref[...]
            for c in range(tiles):
                dst[l, pl.ds(c * 16, 8), :] = scr[pl.ds(c * 16, 8, stride=2), :]
                dst[l, pl.ds(c * 16 + 8, 8), :] = scr[pl.ds(c * 16 + 1, 8, stride=2), :]
        return carry

    lax.fori_loop(0, levels, level, 0)


def split3(x):
    a = x.astype(jnp.bfloat16)
    r = x - a.astype(F32)
    b = r.astype(jnp.bfloat16)
    return a, b, (r - b.astype(F32)).astype(jnp.bfloat16)


def to_row(wide):
    at = lax.broadcasted_iota(I32, (LANES, LANES), 0) == lax.broadcasted_iota(I32, (LANES, LANES), 1)
    return jnp.sum(jnp.where(at, wide, 0.0), axis=0, keepdims=True)


def to_column(row):
    at = lax.broadcasted_iota(I32, (LANES, LANES), 0) == lax.broadcasted_iota(I32, (LANES, LANES), 1)
    return jnp.sum(jnp.where(at, row, 0.0), axis=1, keepdims=True)


def bin_observations(
    groups, dest_ref, cells_ref, time_ref, value_ref, weight_ref, rinv_ref, placed_ref, out, data, hit
):
    count = dest_ref.shape[1]
    slots = groups * CAP
    width = -(-groups // LANES) * LANES
    below = (
        lax.broadcasted_iota(I32, (LANES, LANES), 0) > lax.broadcasted_iota(I32, (LANES, LANES), 1)
    ).astype(jnp.bfloat16)
    lane = lax.broadcasted_iota(I32, (LANES, width), 1)
    slot_lane = lax.broadcasted_iota(I32, (LANES, slots), 1)
    seen = jnp.zeros((1, width), F32)
    target = dest_ref[...].astype(F32)
    for b in range(count // LANES):
        rows = pl.ds(b * LANES, LANES)
        owner = to_column(target[:, b * LANES : (b + 1) * LANES]).astype(I32)
        mine = (lane == owner).astype(F32)
        before = (
            jnp.dot(below, mine.astype(jnp.bfloat16), preferred_element_type=F32) + seen
        )
        rank = jnp.sum(before * mine, axis=1, keepdims=True)
        seen = seen + jnp.sum(mine, axis=0, keepdims=True)
        placed = owner * CAP + rank.astype(I32)
        placed_ref[pl.ds(b, 1), :] = to_row(
            jnp.broadcast_to(placed.astype(F32), (LANES, LANES))
        )
        hit[rows, :] = jnp.where(slot_lane == placed, 1.0, 0.0).astype(jnp.bfloat16)
    data[0:4, :] = cells_ref[...].astype(F32)
    data[4:5, :] = time_ref[...].astype(F32)
    data[5:8, :] = jnp.zeros((3, count), F32)
    data[8:12, :] = weight_ref[...]
    data[12:13, :] = value_ref[...]
    data[13:14, :] = rinv_ref[...]
    data[14:16, :] = jnp.zeros((2, count), F32)
    parts = jnp.concatenate(split3(data[...]), axis=0)
    got = jnp.dot(parts, hit[...], preferred_element_type=F32)
    sums = got[:FIELDS] + got[FIELDS : 2 * FIELDS] + got[2 * FIELDS :]
    last = out.shape[1] - ROWS
    for g in range(groups):
        part = sums[:, g * CAP : (g + 1) * CAP]
        out[g, pl.ds(last, ROWS), 0:CAP] = part[0:ROWS]
        out[g, pl.ds(last, ROWS), CAP : 2 * CAP] = part[ROWS:FIELDS]


def prep_kernel(
    groups,
    levels,
    tiles,
    pairs,
    got_hbm,
    uw_hbm,
    vw_hbm,
    idx_ref,
    w_ref,
    vr_ref,
    uw_ref,
    vw_ref,
    got,
    scr,
    columns,
    sem,
    wind_sems,
):
    last = got_hbm.shape[1] - ROWS
    load = pltpu.make_async_copy(got_hbm.at[:, pl.ds(last, ROWS), :], got, sem)
    load.start()
    winds = [
        pltpu.make_async_copy(uw_hbm, uw_ref, wind_sems.at[0]),
        pltpu.make_async_copy(vw_hbm, vw_ref, wind_sems.at[1]),
    ]
    for copy in winds:
        copy.start()
    scr[...] = jnp.zeros_like(scr)
    load.wait()
    lon = tiles * LANES
    for g in range(groups):
        part = pl.ds(g * CAP, CAP)
        ints = got[g, :, 0:CAP].astype(I32)
        cell = ints[0:4]
        time = ints[4:5]
        lev = cell // (ROWS * lon)
        row = (cell // lon) % ROWS
        col = cell % lon
        if pairs:
            side, lane_at = col // (2 * LANES) * 2 + col % 2, col % (2 * LANES) // 2
        else:
            side, lane_at = col // LANES, col % LANES
        tile = (time * levels + lev) * tiles + side
        scr[0:4, part] = (tile * 16 + (row % 2) * 8 + row // 2).astype(F32)
        scr[8:12, part] = lane_at.astype(F32)
        scr[16:24, part] = got[g, :, CAP : 2 * CAP]
        scr[32:36, part] = (tile * 8 + (row % 2) * 4 + row // 2).astype(F32)
    slots = groups * CAP
    lane = lax.broadcasted_iota(I32, (LANES, LANES), 1)
    few = LANES // 8
    narrow = lax.broadcasted_iota(I32, (few, LANES), 1)
    for b in range(slots // LANES):
        rows = pl.ds(b * LANES, LANES)
        cols = jnp.transpose(scr[:, rows], (1, 0))
        for k in range(4):
            at = cols[:, 8 + k : 9 + k].astype(I32)
            w_ref[k, rows, :] = jnp.where(lane == at, cols[:, 16 + k : 17 + k], 0.0)
        vr_ref[0, rows, :] = jnp.broadcast_to(cols[:, 20:21], (LANES, LANES))
        vr_ref[1, rows, :] = jnp.broadcast_to(cols[:, 21:22], (LANES, LANES))
        columns[...] = cols
        index = jnp.zeros((few, LANES), F32)
        for j in range(8):
            here = columns[pl.ds(j, few, stride=8), :]
            index = jnp.where((narrow // 4) % 8 == j, pltpu.roll(here, 4 * j, 1) if j else here, index)
        idx_ref[pl.ds(b * few, few), :] = index.astype(I32)
    for copy in winds:
        copy.wait()


NSCRATCH = 10


def cycle_kernel(
    groups,
    levels,
    tiles,
    packed,
    field,
    halo,
    uw,
    vw,
    idx_ref,
    w,
    vr,
    front_ref,
    *refs,
):
    own_out, rim_out = refs[: -NSCRATCH]
    (states, f0, f1, f2, f3, scr, acc, dep_ref, idx, sem) = refs[
        -NSCRATCH:
    ]
    forcing = (f0, f1, f2, f3)
    slots = acc.shape[0]
    per = tiles // groups
    pairs = per % 2 == 0
    block = tiles * 16
    load = pltpu.make_async_copy(idx_ref, idx, sem)
    load.start()

    lane = lax.broadcasted_iota(I32, (8, LANES), 1)
    first = lane == 0
    last = lane == LANES - 1
    sub = lax.broadcasted_iota(I32, (8, LANES), 0)
    own = sub < 4
    zero = jnp.zeros((8, LANES), F32)

    def forward(l, carry):
        start = pl.multiple_of(l * block, block)
        for c in range(tiles):
            j, h = divmod(c, per)
            at = pl.ds(pl.multiple_of((h * levels + l) * 8, 8), 8)
            scr[pl.ds(c * 16, 8), :] = field[j, at, :]
            scr[pl.ds(c * 16 + 8, 8), :] = halo[j, at, :] * front_ref[...]
        for c in range(tiles):
            states[pl.ds(start + c * 16, 8), :] = scr[pl.ds(c * 16, 8, stride=2), :]
            states[pl.ds(start + c * 16 + 8, 8), :] = scr[pl.ds(c * 16 + 1, 8, stride=2), :]
        for t in range(NT):
            src = pl.multiple_of(start + t * levels * block, block)
            dst = pl.multiple_of(start + (t + 1) * levels * block, block)

            held = {}

            def tile(c, side):
                if (c, side) not in held:
                    held[c, side] = states[pl.ds(src + c % tiles * 16 + side * 8, 8), :]
                return held[c, side]

            east, west = neighbours(tile, pairs, first, last)
            for c in range(tiles):
                even, odd = tile(c, 0), tile(c, 1)
                souths = (pltpu.roll(odd, 1, 0), even)
                norths = (odd, pltpu.roll(even, 7, 0))
                for side in range(2):
                    here = tile(c, side)
                    at = pl.ds(c * 16 + side * 8, 8)
                    u = uw[l, at, :]
                    v = vw[l, at, :]
                    lon = jnp.where(u > 0, west(c, side), east(c, side))
                    lat = jnp.where(v > 0, souths[side], norths[side])
                    states[pl.ds(dst + c * 16 + side * 8, 8), :] = (
                        here + jnp.abs(u) * (lon - here) + jnp.abs(v) * (lat - here)
                    )
        return carry

    lax.fori_loop(0, levels, forward, 0)

    load.wait()

    share = f0.shape[0] // (slots // 16)

    def gather(i, carry):
        start = pl.multiple_of(i * share, 8)
        for f in forcing:
            for c in range(share // 8):
                f[pl.ds(start + c * 8, 8), :] = zero
        for half in range(2):
            group = i * 2 + half
            base = pl.multiple_of(group * 8, 8)
            for j in range(8):
                total = None
                for k in range(4):
                    term = (
                        w[k, pl.ds(base + j, 1), :] * states[pl.ds(idx[group, j * 4 + k], 1), :]
                    )
                    total = term if total is None else total + term
                acc[pl.ds(base + j, 1), :] = total
        return carry

    lax.fori_loop(0, slots // 16, gather, 0, unroll=2)

    hx = jnp.sum(acc[...], axis=1, keepdims=True)
    dep_ref[...] = vr[1] * (hx - vr[0])
    tail = pl.ds(per * levels * 8, 8)
    for b in range(slots // LANES):
        row = to_row(dep_ref[pl.ds(b * LANES, LANES), :])
        for h in range(LANES // CAP):
            own_out[b * (LANES // CAP) + h, tail, 0:CAP] = jnp.broadcast_to(
                row[:, h * CAP : (h + 1) * CAP], (8, CAP)
            )
            own_out[b * (LANES // CAP) + h, tail, CAP:LANES] = jnp.zeros((8, LANES - CAP), F32)

    def scatter(i, carry):
        base = pl.multiple_of(i * 8, 8)
        for j in range(8):
            dep = dep_ref[pl.ds(base + j, 1), :]
            for k in range(4):
                at = pl.ds(idx[i, 32 + j * 4 + k], 1)
                forcing[k][at, :] = forcing[k][at, :] + w[k, pl.ds(base + j, 1), :] * dep
        return carry

    lax.fori_loop(0, slots // 8, scatter, 0, unroll=2)

    def backward(l, carry):
        fstart = pl.multiple_of(l * tiles * 8, tiles * 8)
        fstep = levels * tiles * 8

        def force(t, c):
            at = pl.ds(pl.multiple_of(fstart + t * fstep, 8) + c * 8, 8)
            total = (f0[at, :] + f1[at, :]) + (f2[at, :] + f3[at, :])
            return (jnp.where(own, total, 0.0), jnp.where(own, pltpu.roll(total, 4, 0), 0.0))

        def fluxes(ref):
            held = {}

            def flux(c, side):
                if (c, side) not in held:
                    at = pl.ds(c % tiles * 16 + side * 8, 8)
                    a = ref[at, :]
                    u = uw[l, at, :]
                    v = vw[l, at, :]
                    x = jnp.abs(u) * a
                    y = jnp.abs(v) * a
                    p = jnp.where(u > 0, x, 0.0)
                    s = jnp.where(v > 0, y, 0.0)
                    held[c, side] = (a - x - y, p, x - p, s, y - s)
                return held[c, side]

            return flux

        for c in range(tiles):
            even, odd = force(NT, c)
            scr[pl.ds(c * 16, 8), :] = even
            scr[pl.ds(c * 16 + 8, 8), :] = odd
        half = tiles * 16
        for t in range(NT - 1, -1, -1):
            src = scr.at[pl.ds(0 if t % 2 else half, half)]
            dst = scr.at[pl.ds(half if t % 2 else 0, half)]
            flux = fluxes(src)
            east, _ = neighbours(lambda c, side: flux(c, side)[1], pairs, first, last)
            _, west = neighbours(lambda c, side: flux(c, side)[2], pairs, first, last)
            for c in range(tiles):
                fine = force(t, c)
                (_, _, _, s_e, n_e), (_, _, _, s_o, n_o) = flux(c, 0), flux(c, 1)
                lats = (s_o + pltpu.roll(n_o, 1, 0), pltpu.roll(s_e, 7, 0) + n_e)
                for side in range(2):
                    value = (
                        (flux(c, side)[0] + east(c, side))
                        + (west(c, side) + lats[side])
                        + fine[side]
                    )
                    dst[pl.ds(c * 16 + side * 8, 8), :] = value
        for c in range(tiles):
            even = scr[pl.ds(c * 16, 8), :]
            odd = scr[pl.ds(c * 16 + 8, 8), :]
            scr[pl.ds(half + c * 16, 8, stride=2), :] = even
            scr[pl.ds(half + c * 16 + 1, 8, stride=2), :] = odd
        for c in range(tiles):
            j, h = divmod(c, per)
            at = pl.ds(pl.multiple_of((h * levels + l) * 8, 8), 8)
            own_out[j, at, :] = scr[pl.ds(half + c * 16, 8), :]
            rim = scr[pl.ds(half + c * 16 + 8, 8), :]
            if not packed:
                rim_out[j, at, :] = rim
            elif h % 2:
                earlier = scr[pl.ds(half + (c - 1) * 16 + 8, 8), :]
                at = pl.ds(pl.multiple_of((h // 2 * levels + l) * 8, 8), 8)
                rim_out[j, at, :] = jnp.where(front_ref[...] > 0, earlier, pltpu.roll(rim, 4, 0))
        return carry

    lax.fori_loop(0, levels, backward, 0)


def per_device(
    control,
    spread,
    vert_root,
    wind_lon,
    wind_lat,
    obs_dest,
    obs_cells,
    obs_time,
    obs_value,
    obs_weight,
    obs_rinv,
):
    levels_all, _, width = control.shape
    groups = lax.axis_size("horiz")
    levels, _, lon = wind_lon.shape
    tiles = lon // LANES
    slots = groups * CAP
    count = obs_value.shape[0]
    halves = width // LANES
    rows = halves * levels * ROWS
    pair_step = 2 if halves % 2 == 0 else 1
    packed = lax.axis_size("obs") == 2 and pair_step == 2
    rim_rows = rows // 2 if packed else rows
    front, back = halo_masks()
    flat = (levels_all * ROWS, width)
    payload = jax.ShapeDtypeStruct((groups, rows + ROWS, LANES), F32)
    vmem = lambda *shape: pltpu.VMEM(shape, F32)
    ivmem = lambda *shape: pltpu.VMEM(shape, I32)

    outgoing, placed = call(
        functools.partial(start_kernel, groups),
        (payload, jax.ShapeDtypeStruct((count // LANES, LANES), F32)),
        [ANY] * 9,
        (ANY, VM),
        [
            vmem(*vert_root.shape),
            vmem(halves, flat[0], LANES),
            vmem(halves, flat[0], LANES),
            ivmem(1, count),
            ivmem(4, count),
            ivmem(1, count),
            vmem(1, count),
            vmem(4, count),
            vmem(1, count),
            vmem(*payload.shape),
            vmem(halves // pair_step, ROWS, levels_all, pair_step * LANES),
            vmem(FIELDS, count),
            pltpu.VMEM((count, slots), jnp.bfloat16),
            pltpu.SemaphoreType.DMA((7,)),
            pltpu.SemaphoreType.DMA((2, halves)),
            pltpu.SemaphoreType.DMA((2,)),
        ],
        limit=56,
        cost=(4e8, 4e6),
    )(
        vert_root,
        control.reshape(flat),
        spread.reshape(flat),
        obs_dest.reshape(1, count),
        obs_cells,
        obs_time[None],
        obs_value[None],
        obs_weight,
        obs_rinv[None],
    )
    field = lax.all_to_all(outgoing, "horiz", split_axis=0, concat_axis=0, tiled=True)

    ring = jax.ShapeDtypeStruct((levels, tiles * 16, LANES), F32)
    uw, vw = call(
        functools.partial(wind_kernel, tiles, halves % 2 == 0),
        (ring, ring),
        [VM] * 5,
        (VM, VM),
        [vmem(tiles * 16, LANES)],
        limit=14,
        cost=(1e6, 8e6),
    )(wind_lon, exchange(wind_lon, True), wind_lat, exchange(wind_lat, True), front)
    field, uw, vw, front, back = lax.optimization_barrier((field, uw, vw, front, back))

    halo = exchange(field, True)
    idx, weights, pair, uw, vw = call(
        functools.partial(prep_kernel, groups, levels, tiles, halves % 2 == 0),
        (
            jax.ShapeDtypeStruct((slots // 8, LANES), I32),
            jax.ShapeDtypeStruct((4, slots, LANES), F32),
            jax.ShapeDtypeStruct((2, slots, LANES), F32),
            ring,
            ring,
        ),
        [ANY] * 3,
        (VM,) * 5,
        [
            vmem(groups, ROWS, LANES),
            vmem(LANES, slots),
            vmem(LANES, LANES),
            pltpu.SemaphoreType.DMA,
            pltpu.SemaphoreType.DMA((2,)),
        ],
        limit=44,
        cost=(1e6, 6e6),
    )(field, uw, vw)

    forcing = vmem((NT + 1) * levels * tiles * 8, LANES)
    adjoint, rim = call(
        functools.partial(cycle_kernel, groups, levels, tiles, packed),
        (payload, jax.ShapeDtypeStruct((groups, rim_rows, LANES), F32)),
        [VM] * 8,
        (VM, VM),
        [
            vmem((NT + 1) * levels * tiles * 16, LANES),
            forcing,
            forcing,
            forcing,
            forcing,
            vmem(2 * tiles * 16, LANES),
            vmem(slots, LANES),
            vmem(slots, LANES),
            pltpu.SMEM((slots // 8, LANES), I32),
            pltpu.SemaphoreType.DMA,
        ],
        limit=34,
        cost=(1e8, 16e6),
    )(field, halo, uw, vw, idx, weights, pair, front)

    part = groups // 4
    total = call(
        functools.partial(rim_kernel, levels, packed),
        payload,
        [
            pl.BlockSpec((part, rows + ROWS, LANES), lambda i: (i, 0, 0)),
            pl.BlockSpec((part, rim_rows, LANES), lambda i: (i, 0, 0)),
            pl.BlockSpec((ROWS, LANES), lambda i: (0, 0)),
        ],
        pl.BlockSpec((part, rows + ROWS, LANES), lambda i: (i, 0, 0)),
        limit=8,
        cost=(1e6, 3e6),
        grid=(4,),
    )(adjoint, exchange(rim, False), back)
    column = lax.all_to_all(total, "horiz", split_axis=0, concat_axis=0, tiled=True)

    gradient, departure = call(
        functools.partial(end_kernel, groups),
        (
            jax.ShapeDtypeStruct(flat, F32),
            jax.ShapeDtypeStruct((count // LANES, LANES), F32),
        ),
        [VM] * 5,
        (ANY, VM),
        [vmem(halves, flat[0], LANES)] * 3 + [vmem(8, slots), pltpu.SemaphoreType.DMA((halves,))],
        limit=14,
        cost=(4e8, 4e6),
    )(vert_root.T, control.reshape(flat), spread.reshape(flat), column, placed)
    return (gradient.reshape(control.shape), departure.reshape(count))


def solution(mesh):
    in_specs = (
        P(None, "obs", "horiz"),
        P(None, "obs", "horiz"),
        P(),
        P("horiz", "obs", None),
        P("horiz", "obs", None),
        P(("obs", "horiz"), None),
        P(None, ("obs", "horiz")),
        P(("obs", "horiz")),
        P(("obs", "horiz")),
        P(None, ("obs", "horiz")),
        P(("obs", "horiz")),
    )
    out_specs = (P(None, "obs", "horiz"), P(("obs", "horiz")))
    return jax.shard_map(
        per_device, mesh=mesh, in_specs=in_specs, out_specs=out_specs, check_vma=False
    )
```

```python
import functools

import jax
import jax.numpy as jnp
from jax import lax
from jax.experimental import pallas as pl
from jax.experimental.pallas import tpu as pltpu
from jax.sharding import PartitionSpec as P

NT = 4
CAP = 64
ROWS = 8
LANES = 128
FIELDS = 16
F32 = jnp.float32
I32 = jnp.int32
ANY = pl.BlockSpec(memory_space=pl.ANY)
VM = pl.BlockSpec(memory_space=pltpu.VMEM)


def call(body, out_shape, in_specs, out_specs, scratch=(), limit=40, cost=(1e6, 1e6), grid=()):
    return pl.pallas_call(
        body,
        out_shape=out_shape,
        grid=grid,
        in_specs=in_specs,
        out_specs=out_specs,
        scratch_shapes=list(scratch),
        compiler_params=pltpu.CompilerParams(vmem_limit_bytes=limit * 2**20),
        cost_estimate=pl.CostEstimate(
            flops=int(cost[0]), bytes_accessed=int(cost[1]), transcendentals=0
        ),
    )


def split2(x):
    a = x.astype(jnp.bfloat16)
    return a, (x - a.astype(F32)).astype(jnp.bfloat16)


def wide_root(root):
    high, low = split2(root)
    return jnp.concatenate([high, high, low], axis=1)


def apply_root(wide, columns):
    high, low = split2(columns)
    return jnp.dot(wide, jnp.concatenate([high, low, high], axis=0), preferred_element_type=F32)


def level_rows(r, levels):
    return pl.ds(r, levels, stride=ROWS)


def start_kernel(
    groups,
    root_hbm,
    control_hbm,
    spread_hbm,
    dest_hbm,
    cells_hbm,
    time_hbm,
    value_hbm,
    weight_hbm,
    rinv_hbm,
    out_hbm,
    placed_ref,
    root,
    control,
    spread,
    dest,
    cells,
    time,
    value,
    weight,
    rinv,
    out,
    mid,
    data,
    hit,
    small_sems,
    sems,
    out_sems,
):
    levels_all = root.shape[0]
    levels = levels_all // groups
    halves = control.shape[0]
    smalls = [
        pltpu.make_async_copy(a, b, small_sems.at[i])
        for i, (a, b) in enumerate(
            (
                (dest_hbm, dest),
                (cells_hbm, cells),
                (time_hbm, time),
                (value_hbm, value),
                (weight_hbm, weight),
                (rinv_hbm, rinv),
                (root_hbm, root),
            )
        )
    ]
    for copy in smalls:
        copy.start()

    def part(h):
        cols = pl.ds(h * LANES, LANES)
        return (
            pltpu.make_async_copy(control_hbm.at[:, cols], control.at[h], sems.at[0, h]),
            pltpu.make_async_copy(spread_hbm.at[:, cols], spread.at[h], sems.at[1, h]),
        )

    parts = [part(h) for h in range(halves)]
    for i in range(2):
        for h in range(halves):
            parts[h][i].start()
    for copy in smalls:
        copy.wait()
    bin_observations(groups, dest, cells, time, value, weight, rinv, placed_ref, out, data, hit)
    wide = wide_root(root[...])
    block = levels * ROWS
    outs = []
    pairs = halves % 2 == 0
    step = 2 if pairs else 1
    for h in range(halves):
        parts[h][0].wait()
    for m in range(0, halves, step):
        for r in range(ROWS):
            at = level_rows(r, levels_all)
            columns = jnp.concatenate([control[m + i, at, :] for i in range(step)], axis=1)
            mid[m // step, r] = apply_root(wide, columns)
    for h in range(halves):
        parts[h][1].wait()
    share = groups // 2
    count = share * levels
    for p in range(2):
        for m in range(0, halves, step):
            for r in range(ROWS):
                at = pl.ds(p * count * ROWS + r, count, stride=ROWS)
                both = mid[m // step, r, pl.ds(p * count, count), :] * jnp.concatenate(
                    [spread[m + i, at, :] for i in range(step)], axis=1
                )
                if pairs:
                    both = reorder(both, even_odd(), split2)
                for i in range(step):
                    for g in range(share):
                        out[p * share + g, pl.ds((m + i) * block + r, levels, stride=ROWS), :] = both[
                            g * levels : (g + 1) * levels, i * LANES : (i + 1) * LANES
                        ]
        part_groups = pl.ds(p * share, share)
        outs.append(
            pltpu.make_async_copy(out.at[part_groups], out_hbm.at[part_groups], out_sems.at[p])
        )
        outs[-1].start()
    for copy in outs:
        copy.wait()


def end_kernel(groups, root_ref, control_ref, spread_ref, got_ref, placed_ref, out_hbm, dep_ref, control, spread, out, row, sems):
    levels_all = root_ref.shape[0]
    levels = levels_all // groups
    halves = out.shape[0]
    block = levels * ROWS
    share = halves * block + 1
    wide = wide_root(root_ref[...])
    outs = []
    pairs = halves % 2 == 0
    for h in range(halves):
        cols = pl.ds(h * LANES, LANES)
        control[h] = control_ref[:, cols]
        spread[h] = spread_ref[:, cols]
    for m in range(0, halves, 2 if pairs else 1):
        for r in range(ROWS):
            at = level_rows(r, levels_all)
            half = [
                jnp.concatenate(
                    [
                        got_ref[pl.ds(g * share + h * block + r, levels, stride=ROWS), :]
                        for g in range(groups)
                    ],
                    axis=0,
                )
                for h in range(m, m + (2 if pairs else 1))
            ]
            if pairs:
                adjoint = reorder(jnp.concatenate(half, axis=1), even_odd(back=True), split2)
                both = apply_root(
                    wide, jnp.concatenate([spread[m, at, :], spread[m + 1, at, :]], axis=1) * adjoint
                )
                values = [both[:, 0:LANES], both[:, LANES:]]
            else:
                values = [apply_root(wide, spread[m, at, :] * half[0])]
            for i, value in enumerate(values):
                out[m + i, at, :] = control[m + i, at, :] + value
        for h in range(m, m + (2 if pairs else 1)):
            cols = pl.ds(h * LANES, LANES)
            outs.append(pltpu.make_async_copy(out.at[h], out_hbm.at[:, cols], sems.at[h]))
            outs[-1].start()
    for r in range(groups):
        row[0:1, r * CAP : (r + 1) * CAP] = got_ref[pl.ds(r * share + halves * block, 1), 0:CAP]
    lane = lax.broadcasted_iota(I32, (LANES, LANES), 1)
    for b in range(dep_ref.shape[0]):
        placed = to_column(placed_ref[pl.ds(b, 1), :]).astype(I32)
        total = jnp.zeros((LANES, LANES), F32)
        for c in range(groups * CAP // LANES):
            value = row[0:1, c * LANES : (c + 1) * LANES]
            total = total + jnp.where(lane + c * LANES == placed, value, 0.0)
        dep_ref[pl.ds(b, 1), :] = to_row(
            jnp.broadcast_to(jnp.sum(total, axis=1, keepdims=True), (LANES, LANES))
        )
    for copy in outs:
        copy.wait()


def rim_kernel(levels, packed, own_ref, rim_ref, mask_ref, out_hbm, out, sems):
    mask = mask_ref[...]
    groups, rows = own_ref.shape[0], own_ref.shape[1] - ROWS
    share = groups // 2
    copies = []
    for p in range(2):
        for g in range(p * share, (p + 1) * share):
            for c in range(rows // ROWS):
                at = pl.ds(c * ROWS, ROWS)
                h, l = divmod(c, levels)
                if packed:
                    rim = rim_ref[g, pl.ds((h // 2 * levels + l) * ROWS, ROWS), :]
                    rim = pltpu.roll(rim, 4, 0) if h % 2 else rim
                else:
                    rim = rim_ref[g, at, :]
                out[pl.ds(g * (rows + 1) + c * ROWS, ROWS), :] = own_ref[g, at, :] + rim * mask
            out[pl.ds(g * (rows + 1) + rows, 1), :] = own_ref[g, pl.ds(rows, 1), :]
        part = pl.ds(p * share * (rows + 1), share * (rows + 1))
        copies.append(pltpu.make_async_copy(out.at[part], out_hbm.at[part], sems.at[p]))
        copies[-1].start()
    for copy in copies:
        copy.wait()


def even_odd(back=False):
    row = lax.broadcasted_iota(I32, (2 * LANES, 2 * LANES), 0)
    col = lax.broadcasted_iota(I32, (2 * LANES, 2 * LANES), 1)
    if back:
        row, col = col, row
    return jnp.where(row == 2 * (col % LANES) + col // LANES, 1.0, 0.0).astype(jnp.bfloat16)


def reorder(x, order, split):
    parts = split(x)
    count = x.shape[0]
    got = jnp.dot(jnp.concatenate(parts, axis=0), order, preferred_element_type=F32)
    total = got[0:count]
    for i in range(1, len(parts)):
        total = total + got[i * count : (i + 1) * count]
    return total


def neighbours(value, pairs, first, last):
    made = {}

    def rolled(c, side, amount):
        key = (c, side, amount)
        if key not in made:
            made[key] = pltpu.roll(value(c, side), amount, 1)
        return made[key]

    def east(c, side):
        if pairs and c % 2 == 0:
            return value(c + 1, side)
        same, after = (c - 1, c + 1) if pairs else (c, c + 1)
        return jnp.where(last, rolled(after, side, LANES - 1), rolled(same, side, LANES - 1))

    def west(c, side):
        if pairs and c % 2:
            return value(c - 1, side)
        same, before = (c + 1, c - 1) if pairs else (c, c - 1)
        return jnp.where(first, rolled(before, side, 1), rolled(same, side, 1))

    return east, west


def exchange(tile_rows, toward):
    count = lax.axis_size("obs")
    if count == 2:
        return lax.ppermute(tile_rows, "obs", [(0, 1), (1, 0)])
    below = lax.ppermute(tile_rows, "obs", [(i, i + 1) for i in range(count - 1)])
    above = lax.ppermute(tile_rows, "obs", [(i + 1, i) for i in range(count - 1)])
    first = (jnp.arange(tile_rows.shape[1]) % ROWS < ROWS // 2)[None, :, None]
    return jnp.where(first, above, below) if toward else jnp.where(first, below, above)


def halo_masks():
    first = (jnp.arange(ROWS) < ROWS // 2)[:, None]
    if lax.axis_size("obs") == 2:
        lower = lax.axis_index("obs") == 0
        front = jnp.where(lower, first, ~first)
        back = ~front
    else:
        front = back = jnp.ones_like(first)
    wide = lambda m: jnp.broadcast_to(m, (ROWS, LANES)).astype(F32)
    return wide(front), wide(back)


def wind_kernel(tiles, pairs, u_ref, uh_ref, v_ref, vh_ref, mask_ref, uo_ref, vo_ref, scr):
    levels = u_ref.shape[0]

    def level(l, carry):
        for src, rim, dst in ((u_ref, uh_ref, uo_ref), (v_ref, vh_ref, vo_ref)):
            step = 2 if pairs else 1
            for c in range(0, tiles, step):
                cols = pl.ds(c * LANES, step * LANES)
                both = jnp.concatenate([src[l, :, cols], rim[l, :, cols]], axis=0)
                if pairs:
                    both = reorder(both, even_odd(), split3)
                for i in range(step):
                    lanes = slice(i * LANES, (i + 1) * LANES)
                    scr[pl.ds((c + i) * 16, 8), :] = both[0:8, lanes]
                    scr[pl.ds((c + i) * 16 + 8, 8), :] = both[8:16, lanes] * mask_ref[...]
            for c in range(tiles):
                dst[l, pl.ds(c * 16, 8), :] = scr[pl.ds(c * 16, 8, stride=2), :]
                dst[l, pl.ds(c * 16 + 8, 8), :] = scr[pl.ds(c * 16 + 1, 8, stride=2), :]
        return carry

    lax.fori_loop(0, levels, level, 0)


def split3(x):
    a = x.astype(jnp.bfloat16)
    r = x - a.astype(F32)
    b = r.astype(jnp.bfloat16)
    return a, b, (r - b.astype(F32)).astype(jnp.bfloat16)


def to_row(wide):
    at = lax.broadcasted_iota(I32, (LANES, LANES), 0) == lax.broadcasted_iota(I32, (LANES, LANES), 1)
    return jnp.sum(jnp.where(at, wide, 0.0), axis=0, keepdims=True)


def to_column(row):
    at = lax.broadcasted_iota(I32, (LANES, LANES), 0) == lax.broadcasted_iota(I32, (LANES, LANES), 1)
    return jnp.sum(jnp.where(at, row, 0.0), axis=1, keepdims=True)


def bin_observations(
    groups, dest_ref, cells_ref, time_ref, value_ref, weight_ref, rinv_ref, placed_ref, out, data, hit
):
    count = dest_ref.shape[1]
    slots = groups * CAP
    width = -(-groups // LANES) * LANES
    below = (
        lax.broadcasted_iota(I32, (LANES, LANES), 0) > lax.broadcasted_iota(I32, (LANES, LANES), 1)
    ).astype(jnp.bfloat16)
    lane = lax.broadcasted_iota(I32, (LANES, width), 1)
    slot_lane = lax.broadcasted_iota(I32, (LANES, slots), 1)
    seen = jnp.zeros((1, width), F32)
    target = dest_ref[...].astype(F32)
    for b in range(count // LANES):
        rows = pl.ds(b * LANES, LANES)
        owner = to_column(target[:, b * LANES : (b + 1) * LANES]).astype(I32)
        mine = (lane == owner).astype(F32)
        before = (
            jnp.dot(below, mine.astype(jnp.bfloat16), preferred_element_type=F32) + seen
        )
        rank = jnp.sum(before * mine, axis=1, keepdims=True)
        seen = seen + jnp.sum(mine, axis=0, keepdims=True)
        placed = owner * CAP + rank.astype(I32)
        placed_ref[pl.ds(b, 1), :] = to_row(
            jnp.broadcast_to(placed.astype(F32), (LANES, LANES))
        )
        hit[rows, :] = jnp.where(slot_lane == placed, 1.0, 0.0).astype(jnp.bfloat16)
    data[0:4, :] = cells_ref[...].astype(F32)
    data[4:5, :] = time_ref[...].astype(F32)
    data[5:8, :] = jnp.zeros((3, count), F32)
    data[8:12, :] = weight_ref[...]
    data[12:13, :] = value_ref[...]
    data[13:14, :] = rinv_ref[...]
    data[14:16, :] = jnp.zeros((2, count), F32)
    parts = jnp.concatenate(split3(data[...]), axis=0)
    got = jnp.dot(parts, hit[...], preferred_element_type=F32)
    sums = got[:FIELDS] + got[FIELDS : 2 * FIELDS] + got[2 * FIELDS :]
    last = out.shape[1] - ROWS
    for g in range(groups):
        part = sums[:, g * CAP : (g + 1) * CAP]
        out[g, pl.ds(last, ROWS), 0:CAP] = part[0:ROWS]
        out[g, pl.ds(last, ROWS), CAP : 2 * CAP] = part[ROWS:FIELDS]


def prep_kernel(
    groups,
    levels,
    tiles,
    pairs,
    got_hbm,
    uw_hbm,
    vw_hbm,
    idx_ref,
    w_ref,
    vr_ref,
    uw_ref,
    vw_ref,
    got,
    scr,
    columns,
    sem,
    wind_sems,
):
    last = got_hbm.shape[1] - ROWS
    load = pltpu.make_async_copy(got_hbm.at[:, pl.ds(last, ROWS), :], got, sem)
    load.start()
    winds = [
        pltpu.make_async_copy(uw_hbm, uw_ref, wind_sems.at[0]),
        pltpu.make_async_copy(vw_hbm, vw_ref, wind_sems.at[1]),
    ]
    for copy in winds:
        copy.start()
    scr[...] = jnp.zeros_like(scr)
    load.wait()
    lon = tiles * LANES
    for g in range(groups):
        part = pl.ds(g * CAP, CAP)
        ints = got[g, :, 0:CAP].astype(I32)
        cell = ints[0:4]
        time = ints[4:5]
        lev = cell // (ROWS * lon)
        row = (cell // lon) % ROWS
        col = cell % lon
        if pairs:
            side, lane_at = col // (2 * LANES) * 2 + col % 2, col % (2 * LANES) // 2
        else:
            side, lane_at = col // LANES, col % LANES
        tile = (time * levels + lev) * tiles + side
        scr[0:4, part] = (tile * 16 + (row % 2) * 8 + row // 2).astype(F32)
        scr[8:12, part] = lane_at.astype(F32)
        scr[16:24, part] = got[g, :, CAP : 2 * CAP]
        scr[32:36, part] = (tile * 8 + (row % 2) * 4 + row // 2).astype(F32)
    slots = groups * CAP
    lane = lax.broadcasted_iota(I32, (LANES, LANES), 1)
    few = LANES // 8
    narrow = lax.broadcasted_iota(I32, (few, LANES), 1)
    for b in range(slots // LANES):
        rows = pl.ds(b * LANES, LANES)
        cols = jnp.transpose(scr[:, rows], (1, 0))
        for k in range(4):
            at = cols[:, 8 + k : 9 + k].astype(I32)
            w_ref[k, rows, :] = jnp.where(lane == at, cols[:, 16 + k : 17 + k], 0.0)
        vr_ref[0, rows, :] = jnp.broadcast_to(cols[:, 20:21], (LANES, LANES))
        vr_ref[1, rows, :] = jnp.broadcast_to(cols[:, 21:22], (LANES, LANES))
        columns[...] = cols
        index = jnp.zeros((few, LANES), F32)
        for j in range(8):
            here = columns[pl.ds(j, few, stride=8), :]
            index = jnp.where((narrow // 4) % 8 == j, pltpu.roll(here, 4 * j, 1) if j else here, index)
        idx_ref[pl.ds(b * few, few), :] = index.astype(I32)
    for copy in winds:
        copy.wait()


NSCRATCH = 10


def cycle_kernel(
    groups,
    levels,
    tiles,
    packed,
    field,
    halo,
    uw,
    vw,
    idx_ref,
    w,
    vr,
    front_ref,
    *refs,
):
    own_out, rim_out = refs[: -NSCRATCH]
    (states, f0, f1, f2, f3, scr, acc, dep_ref, idx, sem) = refs[
        -NSCRATCH:
    ]
    forcing = (f0, f1, f2, f3)
    slots = acc.shape[0]
    per = tiles // groups
    pairs = per % 2 == 0
    block = tiles * 16
    load = pltpu.make_async_copy(idx_ref, idx, sem)
    load.start()

    lane = lax.broadcasted_iota(I32, (8, LANES), 1)
    first = lane == 0
    last = lane == LANES - 1
    sub = lax.broadcasted_iota(I32, (8, LANES), 0)
    own = sub < 4
    zero = jnp.zeros((8, LANES), F32)

    def forward(l, carry):
        start = pl.multiple_of(l * block, block)
        for c in range(tiles):
            j, h = divmod(c, per)
            at = pl.ds(pl.multiple_of((h * levels + l) * 8, 8), 8)
            scr[pl.ds(c * 16, 8), :] = field[j, at, :]
            scr[pl.ds(c * 16 + 8, 8), :] = halo[j, at, :] * front_ref[...]
        for c in range(tiles):
            states[pl.ds(start + c * 16, 8), :] = scr[pl.ds(c * 16, 8, stride=2), :]
            states[pl.ds(start + c * 16 + 8, 8), :] = scr[pl.ds(c * 16 + 1, 8, stride=2), :]
        for t in range(NT):
            src = pl.multiple_of(start + t * levels * block, block)
            dst = pl.multiple_of(start + (t + 1) * levels * block, block)

            held = {}

            def tile(c, side):
                if (c, side) not in held:
                    held[c, side] = states[pl.ds(src + c % tiles * 16 + side * 8, 8), :]
                return held[c, side]

            east, west = neighbours(tile, pairs, first, last)
            for c in range(tiles):
                even, odd = tile(c, 0), tile(c, 1)
                souths = (pltpu.roll(odd, 1, 0), even)
                norths = (odd, pltpu.roll(even, 7, 0))
                for side in range(2):
                    here = tile(c, side)
                    at = pl.ds(c * 16 + side * 8, 8)
                    u = uw[l, at, :]
                    v = vw[l, at, :]
                    lon = jnp.where(u > 0, west(c, side), east(c, side))
                    lat = jnp.where(v > 0, souths[side], norths[side])
                    states[pl.ds(dst + c * 16 + side * 8, 8), :] = (
                        here + jnp.abs(u) * (lon - here) + jnp.abs(v) * (lat - here)
                    )
        return carry

    lax.fori_loop(0, levels, forward, 0)

    load.wait()

    share = f0.shape[0] // (slots // 16)

    def gather(i, carry):
        start = pl.multiple_of(i * share, 8)
        for f in forcing:
            for c in range(share // 8):
                f[pl.ds(start + c * 8, 8), :] = zero
        for half in range(2):
            group = i * 2 + half
            base = pl.multiple_of(group * 8, 8)
            for j in range(8):
                total = None
                for k in range(4):
                    term = (
                        w[k, pl.ds(base + j, 1), :] * states[pl.ds(idx[group, j * 4 + k], 1), :]
                    )
                    total = term if total is None else total + term
                acc[pl.ds(base + j, 1), :] = total
        return carry

    lax.fori_loop(0, slots // 16, gather, 0, unroll=2)

    hx = jnp.sum(acc[...], axis=1, keepdims=True)
    dep_ref[...] = vr[1] * (hx - vr[0])
    tail = pl.ds(per * levels * 8, 8)
    for b in range(slots // LANES):
        row = to_row(dep_ref[pl.ds(b * LANES, LANES), :])
        for h in range(LANES // CAP):
            own_out[b * (LANES // CAP) + h, tail, 0:CAP] = jnp.broadcast_to(
                row[:, h * CAP : (h + 1) * CAP], (8, CAP)
            )
            own_out[b * (LANES // CAP) + h, tail, CAP:LANES] = jnp.zeros((8, LANES - CAP), F32)

    def scatter(i, carry):
        base = pl.multiple_of(i * 8, 8)
        for j in range(8):
            dep = dep_ref[pl.ds(base + j, 1), :]
            for k in range(4):
                at = pl.ds(idx[i, 32 + j * 4 + k], 1)
                forcing[k][at, :] = forcing[k][at, :] + w[k, pl.ds(base + j, 1), :] * dep
        return carry

    lax.fori_loop(0, slots // 8, scatter, 0, unroll=2)

    def backward(l, carry):
        fstart = pl.multiple_of(l * tiles * 8, tiles * 8)
        fstep = levels * tiles * 8

        def force(t, c):
            at = pl.ds(pl.multiple_of(fstart + t * fstep, 8) + c * 8, 8)
            total = (f0[at, :] + f1[at, :]) + (f2[at, :] + f3[at, :])
            return (jnp.where(own, total, 0.0), jnp.where(own, pltpu.roll(total, 4, 0), 0.0))

        def fluxes(ref):
            held = {}

            def flux(c, side):
                if (c, side) not in held:
                    at = pl.ds(c % tiles * 16 + side * 8, 8)
                    a = ref[at, :]
                    u = uw[l, at, :]
                    v = vw[l, at, :]
                    x = jnp.abs(u) * a
                    y = jnp.abs(v) * a
                    p = jnp.where(u > 0, x, 0.0)
                    s = jnp.where(v > 0, y, 0.0)
                    held[c, side] = (a - x - y, p, x - p, s, y - s)
                return held[c, side]

            return flux

        for c in range(tiles):
            even, odd = force(NT, c)
            scr[pl.ds(c * 16, 8), :] = even
            scr[pl.ds(c * 16 + 8, 8), :] = odd
        half = tiles * 16
        for t in range(NT - 1, -1, -1):
            src = scr.at[pl.ds(0 if t % 2 else half, half)]
            dst = scr.at[pl.ds(half if t % 2 else 0, half)]
            flux = fluxes(src)
            east, _ = neighbours(lambda c, side: flux(c, side)[1], pairs, first, last)
            _, west = neighbours(lambda c, side: flux(c, side)[2], pairs, first, last)
            for c in range(tiles):
                fine = force(t, c)
                (_, _, _, s_e, n_e), (_, _, _, s_o, n_o) = flux(c, 0), flux(c, 1)
                lats = (s_o + pltpu.roll(n_o, 1, 0), pltpu.roll(s_e, 7, 0) + n_e)
                for side in range(2):
                    value = (
                        (flux(c, side)[0] + east(c, side))
                        + (west(c, side) + lats[side])
                        + fine[side]
                    )
                    dst[pl.ds(c * 16 + side * 8, 8), :] = value
        for c in range(tiles):
            even = scr[pl.ds(c * 16, 8), :]
            odd = scr[pl.ds(c * 16 + 8, 8), :]
            scr[pl.ds(half + c * 16, 8, stride=2), :] = even
            scr[pl.ds(half + c * 16 + 1, 8, stride=2), :] = odd
        for c in range(tiles):
            j, h = divmod(c, per)
            at = pl.ds(pl.multiple_of((h * levels + l) * 8, 8), 8)
            own_out[j, at, :] = scr[pl.ds(half + c * 16, 8), :]
            rim = scr[pl.ds(half + c * 16 + 8, 8), :]
            if not packed:
                rim_out[j, at, :] = rim
            elif h % 2:
                earlier = scr[pl.ds(half + (c - 1) * 16 + 8, 8), :]
                at = pl.ds(pl.multiple_of((h // 2 * levels + l) * 8, 8), 8)
                rim_out[j, at, :] = jnp.where(front_ref[...] > 0, earlier, pltpu.roll(rim, 4, 0))
        return carry

    lax.fori_loop(0, levels, backward, 0)


def per_device(
    control,
    spread,
    vert_root,
    wind_lon,
    wind_lat,
    obs_dest,
    obs_cells,
    obs_time,
    obs_value,
    obs_weight,
    obs_rinv,
):
    levels_all, _, width = control.shape
    groups = lax.axis_size("horiz")
    levels, _, lon = wind_lon.shape
    tiles = lon // LANES
    slots = groups * CAP
    count = obs_value.shape[0]
    halves = width // LANES
    rows = halves * levels * ROWS
    pair_step = 2 if halves % 2 == 0 else 1
    packed = lax.axis_size("obs") == 2 and pair_step == 2
    rim_rows = rows // 2 if packed else rows
    front, back = halo_masks()
    flat = (levels_all * ROWS, width)
    payload = jax.ShapeDtypeStruct((groups, rows + ROWS, LANES), F32)
    vmem = lambda *shape: pltpu.VMEM(shape, F32)
    ivmem = lambda *shape: pltpu.VMEM(shape, I32)

    outgoing, placed = call(
        functools.partial(start_kernel, groups),
        (payload, jax.ShapeDtypeStruct((count // LANES, LANES), F32)),
        [ANY] * 9,
        (ANY, VM),
        [
            vmem(*vert_root.shape),
            vmem(halves, flat[0], LANES),
            vmem(halves, flat[0], LANES),
            ivmem(1, count),
            ivmem(4, count),
            ivmem(1, count),
            vmem(1, count),
            vmem(4, count),
            vmem(1, count),
            vmem(*payload.shape),
            vmem(halves // pair_step, ROWS, levels_all, pair_step * LANES),
            vmem(FIELDS, count),
            pltpu.VMEM((count, slots), jnp.bfloat16),
            pltpu.SemaphoreType.DMA((7,)),
            pltpu.SemaphoreType.DMA((2, halves)),
            pltpu.SemaphoreType.DMA((2,)),
        ],
        limit=56,
        cost=(4e8, 4e6),
    )(
        vert_root,
        control.reshape(flat),
        spread.reshape(flat),
        obs_dest.reshape(1, count),
        obs_cells,
        obs_time[None],
        obs_value[None],
        obs_weight,
        obs_rinv[None],
    )
    field = lax.all_to_all(outgoing, "horiz", split_axis=0, concat_axis=0, tiled=True)

    ring = jax.ShapeDtypeStruct((levels, tiles * 16, LANES), F32)
    uw, vw = call(
        functools.partial(wind_kernel, tiles, halves % 2 == 0),
        (ring, ring),
        [VM] * 5,
        (VM, VM),
        [vmem(tiles * 16, LANES)],
        limit=14,
        cost=(1e6, 8e6),
    )(wind_lon, exchange(wind_lon, True), wind_lat, exchange(wind_lat, True), front)
    field, uw, vw, front, back = lax.optimization_barrier((field, uw, vw, front, back))

    halo = exchange(field, True)
    idx, weights, pair, uw, vw = call(
        functools.partial(prep_kernel, groups, levels, tiles, halves % 2 == 0),
        (
            jax.ShapeDtypeStruct((slots // 8, LANES), I32),
            jax.ShapeDtypeStruct((4, slots, LANES), F32),
            jax.ShapeDtypeStruct((2, slots, LANES), F32),
            ring,
            ring,
        ),
        [ANY] * 3,
        (VM,) * 5,
        [
            vmem(groups, ROWS, LANES),
            vmem(LANES, slots),
            vmem(LANES, LANES),
            pltpu.SemaphoreType.DMA,
            pltpu.SemaphoreType.DMA((2,)),
        ],
        limit=44,
        cost=(1e6, 6e6),
    )(field, uw, vw)

    forcing = vmem((NT + 1) * levels * tiles * 8, LANES)
    adjoint, rim = call(
        functools.partial(cycle_kernel, groups, levels, tiles, packed),
        (payload, jax.ShapeDtypeStruct((groups, rim_rows, LANES), F32)),
        [VM] * 8,
        (VM, VM),
        [
            vmem((NT + 1) * levels * tiles * 16, LANES),
            forcing,
            forcing,
            forcing,
            forcing,
            vmem(2 * tiles * 16, LANES),
            vmem(slots, LANES),
            vmem(slots, LANES),
            pltpu.SMEM((slots // 8, LANES), I32),
            pltpu.SemaphoreType.DMA,
        ],
        limit=34,
        cost=(1e8, 16e6),
    )(field, halo, uw, vw, idx, weights, pair, front)

    back_shape = (groups * (rows + 1), LANES)
    total = call(
        functools.partial(rim_kernel, levels, packed),
        jax.ShapeDtypeStruct(back_shape, F32),
        [VM] * 3,
        ANY,
        [vmem(*back_shape), pltpu.SemaphoreType.DMA((2,))],
        limit=8,
        cost=(1e6, 3e6),
    )(adjoint, exchange(rim, False), back)
    column = lax.all_to_all(
        total.reshape(back_shape[0], 1, LANES), "horiz", split_axis=0, concat_axis=0, tiled=True
    ).reshape(back_shape)

    gradient, departure = call(
        functools.partial(end_kernel, groups),
        (
            jax.ShapeDtypeStruct(flat, F32),
            jax.ShapeDtypeStruct((count // LANES, LANES), F32),
        ),
        [VM] * 5,
        (ANY, VM),
        [vmem(halves, flat[0], LANES)] * 3 + [vmem(8, slots), pltpu.SemaphoreType.DMA((halves,))],
        limit=14,
        cost=(4e8, 4e6),
    )(vert_root.T, control.reshape(flat), spread.reshape(flat), column, placed)
    return (gradient.reshape(control.shape), departure.reshape(count))


def solution(mesh):
    in_specs = (
        P(None, "obs", "horiz"),
        P(None, "obs", "horiz"),
        P(),
        P("horiz", "obs", None),
        P("horiz", "obs", None),
        P(("obs", "horiz"), None),
        P(None, ("obs", "horiz")),
        P(("obs", "horiz")),
        P(("obs", "horiz")),
        P(None, ("obs", "horiz")),
        P(("obs", "horiz")),
    )
    out_specs = (P(None, "obs", "horiz"), P(("obs", "horiz")))
    return jax.shard_map(
        per_device, mesh=mesh, in_specs=in_specs, out_specs=out_specs, check_vma=False
    )
```

```python
import functools

import jax
import jax.numpy as jnp
from jax import lax
from jax.experimental import pallas as pl
from jax.experimental.pallas import tpu as pltpu
from jax.sharding import PartitionSpec as P

NT = 4
CAP = 64
ROWS = 8
LANES = 128
FIELDS = 16
F32 = jnp.float32
I32 = jnp.int32
ANY = pl.BlockSpec(memory_space=pl.ANY)
VM = pl.BlockSpec(memory_space=pltpu.VMEM)


def call(body, out_shape, in_specs, out_specs, scratch=(), limit=40, cost=(1e6, 1e6), grid=()):
    return pl.pallas_call(
        body,
        out_shape=out_shape,
        grid=grid,
        in_specs=in_specs,
        out_specs=out_specs,
        scratch_shapes=list(scratch),
        compiler_params=pltpu.CompilerParams(vmem_limit_bytes=limit * 2**20),
        cost_estimate=pl.CostEstimate(
            flops=int(cost[0]), bytes_accessed=int(cost[1]), transcendentals=0
        ),
    )


def split2(x):
    a = x.astype(jnp.bfloat16)
    return a, (x - a.astype(F32)).astype(jnp.bfloat16)


def wide_root(root):
    high, low = split2(root)
    return jnp.concatenate([high, high, low], axis=1)


def apply_root(wide, columns):
    high, low = split2(columns)
    return jnp.dot(wide, jnp.concatenate([high, low, high], axis=0), preferred_element_type=F32)


def level_rows(r, levels):
    return pl.ds(r, levels, stride=ROWS)


def start_kernel(
    groups,
    root_hbm,
    control_hbm,
    spread_hbm,
    dest_hbm,
    cells_hbm,
    time_hbm,
    value_hbm,
    weight_hbm,
    rinv_hbm,
    out_hbm,
    placed_ref,
    root,
    control,
    spread,
    dest,
    cells,
    time,
    value,
    weight,
    rinv,
    out,
    mid,
    data,
    hit,
    small_sems,
    sems,
    out_sems,
):
    levels_all = root.shape[0]
    levels = levels_all // groups
    halves = control.shape[0]
    smalls = [
        pltpu.make_async_copy(a, b, small_sems.at[i])
        for i, (a, b) in enumerate(
            (
                (dest_hbm, dest),
                (cells_hbm, cells),
                (time_hbm, time),
                (value_hbm, value),
                (weight_hbm, weight),
                (rinv_hbm, rinv),
                (root_hbm, root),
            )
        )
    ]
    for copy in smalls:
        copy.start()

    def part(h):
        cols = pl.ds(h * LANES, LANES)
        return (
            pltpu.make_async_copy(control_hbm.at[:, cols], control.at[h], sems.at[0, h]),
            pltpu.make_async_copy(spread_hbm.at[:, cols], spread.at[h], sems.at[1, h]),
        )

    parts = [part(h) for h in range(halves)]
    for i in range(2):
        for h in range(halves):
            parts[h][i].start()
    for copy in smalls:
        copy.wait()
    bin_observations(groups, dest, cells, time, value, weight, rinv, placed_ref, out, data, hit)
    wide = wide_root(root[...])
    block = levels * ROWS
    outs = []
    pairs = halves % 2 == 0
    step = 2 if pairs else 1
    for h in range(halves):
        parts[h][0].wait()
    for m in range(0, halves, step):
        for r in range(ROWS):
            at = level_rows(r, levels_all)
            columns = jnp.concatenate([control[m + i, at, :] for i in range(step)], axis=1)
            mid[m // step, r] = apply_root(wide, columns)
    for h in range(halves):
        parts[h][1].wait()
    share = groups // 2
    count = share * levels
    for p in range(2):
        for m in range(0, halves, step):
            for r in range(ROWS):
                at = pl.ds(p * count * ROWS + r, count, stride=ROWS)
                both = mid[m // step, r, pl.ds(p * count, count), :] * jnp.concatenate(
                    [spread[m + i, at, :] for i in range(step)], axis=1
                )
                if pairs:
                    both = reorder(both, even_odd(), split2)
                for i in range(step):
                    for g in range(share):
                        out[p * share + g, pl.ds((m + i) * block + r, levels, stride=ROWS), :] = both[
                            g * levels : (g + 1) * levels, i * LANES : (i + 1) * LANES
                        ]
        part_groups = pl.ds(p * share, share)
        outs.append(
            pltpu.make_async_copy(out.at[part_groups], out_hbm.at[part_groups], out_sems.at[p])
        )
        outs[-1].start()
    for copy in outs:
        copy.wait()


def end_kernel(groups, root_ref, control_ref, spread_ref, got_ref, placed_ref, out_hbm, dep_ref, control, spread, out, row, sems):
    levels_all = root_ref.shape[0]
    levels = levels_all // groups
    halves = out.shape[0]
    block = levels * ROWS
    share = halves * block + 1
    wide = wide_root(root_ref[...])
    outs = []
    pairs = halves % 2 == 0
    for h in range(halves):
        cols = pl.ds(h * LANES, LANES)
        control[h] = control_ref[:, cols]
        spread[h] = spread_ref[:, cols]
    for m in range(0, halves, 2 if pairs else 1):
        for r in range(ROWS):
            at = level_rows(r, levels_all)
            half = [
                jnp.concatenate(
                    [
                        got_ref[pl.ds(g * share + h * block + r, levels, stride=ROWS), :]
                        for g in range(groups)
                    ],
                    axis=0,
                )
                for h in range(m, m + (2 if pairs else 1))
            ]
            if pairs:
                adjoint = reorder(jnp.concatenate(half, axis=1), even_odd(back=True), split2)
                both = apply_root(
                    wide, jnp.concatenate([spread[m, at, :], spread[m + 1, at, :]], axis=1) * adjoint
                )
                values = [both[:, 0:LANES], both[:, LANES:]]
            else:
                values = [apply_root(wide, spread[m, at, :] * half[0])]
            for i, value in enumerate(values):
                out[m + i, at, :] = control[m + i, at, :] + value
        for h in range(m, m + (2 if pairs else 1)):
            cols = pl.ds(h * LANES, LANES)
            outs.append(pltpu.make_async_copy(out.at[h], out_hbm.at[:, cols], sems.at[h]))
            outs[-1].start()
    for r in range(groups):
        row[0:1, r * CAP : (r + 1) * CAP] = got_ref[pl.ds(r * share + halves * block, 1), 0:CAP]
    lane = lax.broadcasted_iota(I32, (LANES, LANES), 1)
    for b in range(dep_ref.shape[0]):
        placed = to_column(placed_ref[pl.ds(b, 1), :]).astype(I32)
        total = jnp.zeros((LANES, LANES), F32)
        for c in range(groups * CAP // LANES):
            value = row[0:1, c * LANES : (c + 1) * LANES]
            total = total + jnp.where(lane + c * LANES == placed, value, 0.0)
        dep_ref[pl.ds(b, 1), :] = to_row(
            jnp.broadcast_to(jnp.sum(total, axis=1, keepdims=True), (LANES, LANES))
        )
    for copy in outs:
        copy.wait()


def rim_kernel(levels, packed, own_ref, rim_ref, mask_ref, out_hbm, out, sems):
    mask = mask_ref[...]
    groups, rows = own_ref.shape[0], own_ref.shape[1] - ROWS
    share = groups // 2
    copies = []
    for p in range(2):
        for g in range(p * share, (p + 1) * share):
            for c in range(rows // ROWS):
                at = pl.ds(c * ROWS, ROWS)
                h, l = divmod(c, levels)
                if packed:
                    rim = rim_ref[g, pl.ds((h // 2 * levels + l) * ROWS, ROWS), :]
                    rim = pltpu.roll(rim, 4, 0) if h % 2 else rim
                else:
                    rim = rim_ref[g, at, :]
                out[pl.ds(g * (rows + 1) + c * ROWS, ROWS), :] = own_ref[g, at, :] + rim * mask
            out[pl.ds(g * (rows + 1) + rows, 1), :] = own_ref[g, pl.ds(rows, 1), :]
        part = pl.ds(p * share * (rows + 1), share * (rows + 1))
        copies.append(pltpu.make_async_copy(out.at[part], out_hbm.at[part], sems.at[p]))
        copies[-1].start()
    for copy in copies:
        copy.wait()


def even_odd(back=False):
    row = lax.broadcasted_iota(I32, (2 * LANES, 2 * LANES), 0)
    col = lax.broadcasted_iota(I32, (2 * LANES, 2 * LANES), 1)
    if back:
        row, col = col, row
    return jnp.where(row == 2 * (col % LANES) + col // LANES, 1.0, 0.0).astype(jnp.bfloat16)


def reorder(x, order, split):
    parts = split(x)
    count = x.shape[0]
    got = jnp.dot(jnp.concatenate(parts, axis=0), order, preferred_element_type=F32)
    total = got[0:count]
    for i in range(1, len(parts)):
        total = total + got[i * count : (i + 1) * count]
    return total


def neighbours(value, pairs, first, last):
    made = {}

    def rolled(c, side, amount):
        key = (c, side, amount)
        if key not in made:
            made[key] = pltpu.roll(value(c, side), amount, 1)
        return made[key]

    def east(c, side):
        if pairs and c % 2 == 0:
            return value(c + 1, side)
        same, after = (c - 1, c + 1) if pairs else (c, c + 1)
        return jnp.where(last, rolled(after, side, LANES - 1), rolled(same, side, LANES - 1))

    def west(c, side):
        if pairs and c % 2:
            return value(c - 1, side)
        same, before = (c + 1, c - 1) if pairs else (c, c - 1)
        return jnp.where(first, rolled(before, side, 1), rolled(same, side, 1))

    return east, west


def exchange(tile_rows, toward):
    count = lax.axis_size("obs")
    if count == 2:
        return lax.ppermute(tile_rows, "obs", [(0, 1), (1, 0)])
    below = lax.ppermute(tile_rows, "obs", [(i, i + 1) for i in range(count - 1)])
    above = lax.ppermute(tile_rows, "obs", [(i + 1, i) for i in range(count - 1)])
    first = (jnp.arange(tile_rows.shape[1]) % ROWS < ROWS // 2)[None, :, None]
    return jnp.where(first, above, below) if toward else jnp.where(first, below, above)


def halo_masks():
    first = (jnp.arange(ROWS) < ROWS // 2)[:, None]
    if lax.axis_size("obs") == 2:
        lower = lax.axis_index("obs") == 0
        front = jnp.where(lower, first, ~first)
        back = ~front
    else:
        front = back = jnp.ones_like(first)
    wide = lambda m: jnp.broadcast_to(m, (ROWS, LANES)).astype(F32)
    return wide(front), wide(back)


def wind_kernel(tiles, pairs, u_ref, uh_ref, v_ref, vh_ref, mask_ref, uo_ref, vo_ref, scr):
    levels = u_ref.shape[0]

    def level(l, carry):
        for src, rim, dst in ((u_ref, uh_ref, uo_ref), (v_ref, vh_ref, vo_ref)):
            step = 2 if pairs else 1
            for c in range(0, tiles, step):
                cols = pl.ds(c * LANES, step * LANES)
                both = jnp.concatenate([src[l, :, cols], rim[l, :, cols]], axis=0)
                if pairs:
                    both = reorder(both, even_odd(), split3)
                for i in range(step):
                    lanes = slice(i * LANES, (i + 1) * LANES)
                    scr[pl.ds((c + i) * 16, 8), :] = both[0:8, lanes]
                    scr[pl.ds((c + i) * 16 + 8, 8), :] = both[8:16, lanes] * mask_ref[...]
            for c in range(tiles):
                dst[l, pl.ds(c * 16, 8), :] = scr[pl.ds(c * 16, 8, stride=2), :]
                dst[l, pl.ds(c * 16 + 8, 8), :] = scr[pl.ds(c * 16 + 1, 8, stride=2), :]
        return carry

    lax.fori_loop(0, levels, level, 0)


def split3(x):
    a = x.astype(jnp.bfloat16)
    r = x - a.astype(F32)
    b = r.astype(jnp.bfloat16)
    return a, b, (r - b.astype(F32)).astype(jnp.bfloat16)


def to_row(wide):
    at = lax.broadcasted_iota(I32, (LANES, LANES), 0) == lax.broadcasted_iota(I32, (LANES, LANES), 1)
    return jnp.sum(jnp.where(at, wide, 0.0), axis=0, keepdims=True)


def to_column(row):
    at = lax.broadcasted_iota(I32, (LANES, LANES), 0) == lax.broadcasted_iota(I32, (LANES, LANES), 1)
    return jnp.sum(jnp.where(at, row, 0.0), axis=1, keepdims=True)


def bin_observations(
    groups, dest_ref, cells_ref, time_ref, value_ref, weight_ref, rinv_ref, placed_ref, out, data, hit
):
    count = dest_ref.shape[1]
    slots = groups * CAP
    width = -(-groups // LANES) * LANES
    below = (
        lax.broadcasted_iota(I32, (LANES, LANES), 0) > lax.broadcasted_iota(I32, (LANES, LANES), 1)
    ).astype(jnp.bfloat16)
    lane = lax.broadcasted_iota(I32, (LANES, width), 1)
    slot_lane = lax.broadcasted_iota(I32, (LANES, slots), 1)
    seen = jnp.zeros((1, width), F32)
    target = dest_ref[...].astype(F32)
    for b in range(count // LANES):
        rows = pl.ds(b * LANES, LANES)
        owner = to_column(target[:, b * LANES : (b + 1) * LANES]).astype(I32)
        mine = (lane == owner).astype(F32)
        before = (
            jnp.dot(below, mine.astype(jnp.bfloat16), preferred_element_type=F32) + seen
        )
        rank = jnp.sum(before * mine, axis=1, keepdims=True)
        seen = seen + jnp.sum(mine, axis=0, keepdims=True)
        placed = owner * CAP + rank.astype(I32)
        placed_ref[pl.ds(b, 1), :] = to_row(
            jnp.broadcast_to(placed.astype(F32), (LANES, LANES))
        )
        hit[rows, :] = jnp.where(slot_lane == placed, 1.0, 0.0).astype(jnp.bfloat16)
    data[0:4, :] = cells_ref[...].astype(F32)
    data[4:5, :] = time_ref[...].astype(F32)
    data[5:8, :] = jnp.zeros((3, count), F32)
    data[8:12, :] = weight_ref[...]
    data[12:13, :] = value_ref[...]
    data[13:14, :] = rinv_ref[...]
    data[14:16, :] = jnp.zeros((2, count), F32)
    parts = jnp.concatenate(split3(data[...]), axis=0)
    got = jnp.dot(parts, hit[...], preferred_element_type=F32)
    sums = got[:FIELDS] + got[FIELDS : 2 * FIELDS] + got[2 * FIELDS :]
    last = out.shape[1] - ROWS
    for g in range(groups):
        part = sums[:, g * CAP : (g + 1) * CAP]
        out[g, pl.ds(last, ROWS), 0:CAP] = part[0:ROWS]
        out[g, pl.ds(last, ROWS), CAP : 2 * CAP] = part[ROWS:FIELDS]


def prep_kernel(
    groups,
    levels,
    tiles,
    pairs,
    got_hbm,
    uw_hbm,
    vw_hbm,
    idx_ref,
    w_ref,
    vr_ref,
    uw_ref,
    vw_ref,
    got,
    scr,
    columns,
    sem,
    wind_sems,
):
    last = got_hbm.shape[1] - ROWS
    load = pltpu.make_async_copy(got_hbm.at[:, pl.ds(last, ROWS), :], got, sem)
    load.start()
    winds = [
        pltpu.make_async_copy(uw_hbm, uw_ref, wind_sems.at[0]),
        pltpu.make_async_copy(vw_hbm, vw_ref, wind_sems.at[1]),
    ]
    for copy in winds:
        copy.start()
    scr[...] = jnp.zeros_like(scr)
    load.wait()
    lon = tiles * LANES
    for g in range(groups):
        part = pl.ds(g * CAP, CAP)
        ints = got[g, :, 0:CAP].astype(I32)
        cell = ints[0:4]
        time = ints[4:5]
        lev = cell // (ROWS * lon)
        row = (cell // lon) % ROWS
        col = cell % lon
        if pairs:
            side, lane_at = col // (2 * LANES) * 2 + col % 2, col % (2 * LANES) // 2
        else:
            side, lane_at = col // LANES, col % LANES
        tile = (time * levels + lev) * tiles + side
        scr[0:4, part] = (tile * 16 + (row % 2) * 8 + row // 2).astype(F32)
        scr[8:12, part] = lane_at.astype(F32)
        scr[16:24, part] = got[g, :, CAP : 2 * CAP]
        scr[32:36, part] = (tile * 8 + (row % 2) * 4 + row // 2).astype(F32)
    slots = groups * CAP
    lane = lax.broadcasted_iota(I32, (LANES, LANES), 1)
    few = LANES // 8
    narrow = lax.broadcasted_iota(I32, (few, LANES), 1)
    for b in range(slots // LANES):
        rows = pl.ds(b * LANES, LANES)
        cols = jnp.transpose(scr[:, rows], (1, 0))
        for k in range(4):
            at = cols[:, 8 + k : 9 + k].astype(I32)
            w_ref[k, rows, :] = jnp.where(lane == at, cols[:, 16 + k : 17 + k], 0.0)
        vr_ref[0, rows, :] = jnp.broadcast_to(cols[:, 20:21], (LANES, LANES))
        vr_ref[1, rows, :] = jnp.broadcast_to(cols[:, 21:22], (LANES, LANES))
        columns[...] = cols
        index = jnp.zeros((few, LANES), F32)
        for j in range(8):
            here = columns[pl.ds(j, few, stride=8), :]
            index = jnp.where((narrow // 4) % 8 == j, pltpu.roll(here, 4 * j, 1) if j else here, index)
        idx_ref[pl.ds(b * few, few), :] = index.astype(I32)
    for copy in winds:
        copy.wait()


NSCRATCH = 10


def cycle_kernel(
    groups,
    levels,
    tiles,
    packed,
    field,
    halo,
    uw,
    vw,
    idx_ref,
    w,
    vr,
    front_ref,
    *refs,
):
    own_out, rim_out = refs[: -NSCRATCH]
    (states, f0, f1, f2, f3, scr, acc, dep_ref, idx, sem) = refs[
        -NSCRATCH:
    ]
    forcing = (f0, f1, f2, f3)
    slots = acc.shape[0]
    per = tiles // groups
    pairs = per % 2 == 0
    block = tiles * 16
    load = pltpu.make_async_copy(idx_ref, idx, sem)
    load.start()

    lane = lax.broadcasted_iota(I32, (8, LANES), 1)
    first = lane == 0
    last = lane == LANES - 1
    sub = lax.broadcasted_iota(I32, (8, LANES), 0)
    own = sub < 4
    zero = jnp.zeros((8, LANES), F32)

    def forward(l, carry):
        start = pl.multiple_of(l * block, block)
        for c in range(tiles):
            j, h = divmod(c, per)
            at = pl.ds(pl.multiple_of((h * levels + l) * 8, 8), 8)
            scr[pl.ds(c * 16, 8), :] = field[j, at, :]
            scr[pl.ds(c * 16 + 8, 8), :] = halo[j, at, :] * front_ref[...]
        for c in range(tiles):
            states[pl.ds(start + c * 16, 8), :] = scr[pl.ds(c * 16, 8, stride=2), :]
            states[pl.ds(start + c * 16 + 8, 8), :] = scr[pl.ds(c * 16 + 1, 8, stride=2), :]
        for t in range(NT):
            src = pl.multiple_of(start + t * levels * block, block)
            dst = pl.multiple_of(start + (t + 1) * levels * block, block)

            held = {}

            def tile(c, side):
                if (c, side) not in held:
                    held[c, side] = states[pl.ds(src + c % tiles * 16 + side * 8, 8), :]
                return held[c, side]

            east, west = neighbours(tile, pairs, first, last)
            for c in range(tiles):
                even, odd = tile(c, 0), tile(c, 1)
                souths = (pltpu.roll(odd, 1, 0), even)
                norths = (odd, pltpu.roll(even, 7, 0))
                for side in range(2):
                    here = tile(c, side)
                    at = pl.ds(c * 16 + side * 8, 8)
                    u = uw[l, at, :]
                    v = vw[l, at, :]
                    lon = jnp.where(u > 0, west(c, side), east(c, side))
                    lat = jnp.where(v > 0, souths[side], norths[side])
                    states[pl.ds(dst + c * 16 + side * 8, 8), :] = (
                        here + jnp.abs(u) * (lon - here) + jnp.abs(v) * (lat - here)
                    )
        return carry

    lax.fori_loop(0, levels, forward, 0, unroll=2)

    load.wait()

    share = f0.shape[0] // (slots // 16)

    def gather(i, carry):
        start = pl.multiple_of(i * share, 8)
        for f in forcing:
            for c in range(share // 8):
                f[pl.ds(start + c * 8, 8), :] = zero
        for half in range(2):
            group = i * 2 + half
            base = pl.multiple_of(group * 8, 8)
            for j in range(8):
                total = None
                for k in range(4):
                    term = (
                        w[k, pl.ds(base + j, 1), :] * states[pl.ds(idx[group, j * 4 + k], 1), :]
                    )
                    total = term if total is None else total + term
                acc[pl.ds(base + j, 1), :] = total
        return carry

    lax.fori_loop(0, slots // 16, gather, 0, unroll=2)

    hx = jnp.sum(acc[...], axis=1, keepdims=True)
    dep_ref[...] = vr[1] * (hx - vr[0])
    tail = pl.ds(per * levels * 8, 8)
    for b in range(slots // LANES):
        row = to_row(dep_ref[pl.ds(b * LANES, LANES), :])
        for h in range(LANES // CAP):
            own_out[b * (LANES // CAP) + h, tail, 0:CAP] = jnp.broadcast_to(
                row[:, h * CAP : (h + 1) * CAP], (8, CAP)
            )
            own_out[b * (LANES // CAP) + h, tail, CAP:LANES] = jnp.zeros((8, LANES - CAP), F32)

    def scatter(i, carry):
        base = pl.multiple_of(i * 8, 8)
        for j in range(8):
            dep = dep_ref[pl.ds(base + j, 1), :]
            for k in range(4):
                at = pl.ds(idx[i, 32 + j * 4 + k], 1)
                forcing[k][at, :] = forcing[k][at, :] + w[k, pl.ds(base + j, 1), :] * dep
        return carry

    lax.fori_loop(0, slots // 8, scatter, 0, unroll=4)

    def backward(l, carry):
        fstart = pl.multiple_of(l * tiles * 8, tiles * 8)
        fstep = levels * tiles * 8

        def force(t, c):
            at = pl.ds(pl.multiple_of(fstart + t * fstep, 8) + c * 8, 8)
            total = (f0[at, :] + f1[at, :]) + (f2[at, :] + f3[at, :])
            return (jnp.where(own, total, 0.0), jnp.where(own, pltpu.roll(total, 4, 0), 0.0))

        def fluxes(ref):
            held = {}

            def flux(c, side):
                if (c, side) not in held:
                    at = pl.ds(c % tiles * 16 + side * 8, 8)
                    a = ref[at, :]
                    u = uw[l, at, :]
                    v = vw[l, at, :]
                    x = jnp.abs(u) * a
                    y = jnp.abs(v) * a
                    p = jnp.where(u > 0, x, 0.0)
                    s = jnp.where(v > 0, y, 0.0)
                    held[c, side] = (a - x - y, p, x - p, s, y - s)
                return held[c, side]

            return flux

        for c in range(tiles):
            even, odd = force(NT, c)
            scr[pl.ds(c * 16, 8), :] = even
            scr[pl.ds(c * 16 + 8, 8), :] = odd
        half = tiles * 16
        for t in range(NT - 1, -1, -1):
            src = scr.at[pl.ds(0 if t % 2 else half, half)]
            dst = scr.at[pl.ds(half if t % 2 else 0, half)]
            flux = fluxes(src)
            east, _ = neighbours(lambda c, side: flux(c, side)[1], pairs, first, last)
            _, west = neighbours(lambda c, side: flux(c, side)[2], pairs, first, last)
            for c in range(tiles):
                fine = force(t, c)
                (_, _, _, s_e, n_e), (_, _, _, s_o, n_o) = flux(c, 0), flux(c, 1)
                lats = (s_o + pltpu.roll(n_o, 1, 0), pltpu.roll(s_e, 7, 0) + n_e)
                for side in range(2):
                    value = (
                        (flux(c, side)[0] + east(c, side))
                        + (west(c, side) + lats[side])
                        + fine[side]
                    )
                    dst[pl.ds(c * 16 + side * 8, 8), :] = value
        for c in range(tiles):
            even = scr[pl.ds(c * 16, 8), :]
            odd = scr[pl.ds(c * 16 + 8, 8), :]
            scr[pl.ds(half + c * 16, 8, stride=2), :] = even
            scr[pl.ds(half + c * 16 + 1, 8, stride=2), :] = odd
        for c in range(tiles):
            j, h = divmod(c, per)
            at = pl.ds(pl.multiple_of((h * levels + l) * 8, 8), 8)
            own_out[j, at, :] = scr[pl.ds(half + c * 16, 8), :]
            rim = scr[pl.ds(half + c * 16 + 8, 8), :]
            if not packed:
                rim_out[j, at, :] = rim
            elif h % 2:
                earlier = scr[pl.ds(half + (c - 1) * 16 + 8, 8), :]
                at = pl.ds(pl.multiple_of((h // 2 * levels + l) * 8, 8), 8)
                rim_out[j, at, :] = jnp.where(front_ref[...] > 0, earlier, pltpu.roll(rim, 4, 0))
        return carry

    lax.fori_loop(0, levels, backward, 0)


def per_device(
    control,
    spread,
    vert_root,
    wind_lon,
    wind_lat,
    obs_dest,
    obs_cells,
    obs_time,
    obs_value,
    obs_weight,
    obs_rinv,
):
    levels_all, _, width = control.shape
    groups = lax.axis_size("horiz")
    levels, _, lon = wind_lon.shape
    tiles = lon // LANES
    slots = groups * CAP
    count = obs_value.shape[0]
    halves = width // LANES
    rows = halves * levels * ROWS
    pair_step = 2 if halves % 2 == 0 else 1
    packed = lax.axis_size("obs") == 2 and pair_step == 2
    rim_rows = rows // 2 if packed else rows
    front, back = halo_masks()
    flat = (levels_all * ROWS, width)
    payload = jax.ShapeDtypeStruct((groups, rows + ROWS, LANES), F32)
    vmem = lambda *shape: pltpu.VMEM(shape, F32)
    ivmem = lambda *shape: pltpu.VMEM(shape, I32)

    outgoing, placed = call(
        functools.partial(start_kernel, groups),
        (payload, jax.ShapeDtypeStruct((count // LANES, LANES), F32)),
        [ANY] * 9,
        (ANY, VM),
        [
            vmem(*vert_root.shape),
            vmem(halves, flat[0], LANES),
            vmem(halves, flat[0], LANES),
            ivmem(1, count),
            ivmem(4, count),
            ivmem(1, count),
            vmem(1, count),
            vmem(4, count),
            vmem(1, count),
            vmem(*payload.shape),
            vmem(halves // pair_step, ROWS, levels_all, pair_step * LANES),
            vmem(FIELDS, count),
            pltpu.VMEM((count, slots), jnp.bfloat16),
            pltpu.SemaphoreType.DMA((7,)),
            pltpu.SemaphoreType.DMA((2, halves)),
            pltpu.SemaphoreType.DMA((2,)),
        ],
        limit=56,
        cost=(4e8, 4e6),
    )(
        vert_root,
        control.reshape(flat),
        spread.reshape(flat),
        obs_dest.reshape(1, count),
        obs_cells,
        obs_time[None],
        obs_value[None],
        obs_weight,
        obs_rinv[None],
    )
    field = lax.all_to_all(outgoing, "horiz", split_axis=0, concat_axis=0, tiled=True)

    ring = jax.ShapeDtypeStruct((levels, tiles * 16, LANES), F32)
    uw, vw = call(
        functools.partial(wind_kernel, tiles, halves % 2 == 0),
        (ring, ring),
        [VM] * 5,
        (VM, VM),
        [vmem(tiles * 16, LANES)],
        limit=14,
        cost=(1e6, 8e6),
    )(wind_lon, exchange(wind_lon, True), wind_lat, exchange(wind_lat, True), front)
    field, uw, vw, front, back = lax.optimization_barrier((field, uw, vw, front, back))

    halo = exchange(field, True)
    idx, weights, pair, uw, vw = call(
        functools.partial(prep_kernel, groups, levels, tiles, halves % 2 == 0),
        (
            jax.ShapeDtypeStruct((slots // 8, LANES), I32),
            jax.ShapeDtypeStruct((4, slots, LANES), F32),
            jax.ShapeDtypeStruct((2, slots, LANES), F32),
            ring,
            ring,
        ),
        [ANY] * 3,
        (VM,) * 5,
        [
            vmem(groups, ROWS, LANES),
            vmem(LANES, slots),
            vmem(LANES, LANES),
            pltpu.SemaphoreType.DMA,
            pltpu.SemaphoreType.DMA((2,)),
        ],
        limit=44,
        cost=(1e6, 6e6),
    )(field, uw, vw)

    forcing = vmem((NT + 1) * levels * tiles * 8, LANES)
    adjoint, rim = call(
        functools.partial(cycle_kernel, groups, levels, tiles, packed),
        (payload, jax.ShapeDtypeStruct((groups, rim_rows, LANES), F32)),
        [VM] * 8,
        (VM, VM),
        [
            vmem((NT + 1) * levels * tiles * 16, LANES),
            forcing,
            forcing,
            forcing,
            forcing,
            vmem(2 * tiles * 16, LANES),
            vmem(slots, LANES),
            vmem(slots, LANES),
            pltpu.SMEM((slots // 8, LANES), I32),
            pltpu.SemaphoreType.DMA,
        ],
        limit=34,
        cost=(1e8, 16e6),
    )(field, halo, uw, vw, idx, weights, pair, front)

    back_shape = (groups * (rows + 1), LANES)
    total = call(
        functools.partial(rim_kernel, levels, packed),
        jax.ShapeDtypeStruct(back_shape, F32),
        [VM] * 3,
        ANY,
        [vmem(*back_shape), pltpu.SemaphoreType.DMA((2,))],
        limit=8,
        cost=(1e6, 3e6),
    )(adjoint, exchange(rim, False), back)
    column = lax.all_to_all(
        total.reshape(back_shape[0], 1, LANES), "horiz", split_axis=0, concat_axis=0, tiled=True
    ).reshape(back_shape)

    gradient, departure = call(
        functools.partial(end_kernel, groups),
        (
            jax.ShapeDtypeStruct(flat, F32),
            jax.ShapeDtypeStruct((count // LANES, LANES), F32),
        ),
        [VM] * 5,
        (ANY, VM),
        [vmem(halves, flat[0], LANES)] * 3 + [vmem(8, slots), pltpu.SemaphoreType.DMA((halves,))],
        limit=14,
        cost=(4e8, 4e6),
    )(vert_root.T, control.reshape(flat), spread.reshape(flat), column, placed)
    return (gradient.reshape(control.shape), departure.reshape(count))


def solution(mesh):
    in_specs = (
        P(None, "obs", "horiz"),
        P(None, "obs", "horiz"),
        P(),
        P("horiz", "obs", None),
        P("horiz", "obs", None),
        P(("obs", "horiz"), None),
        P(None, ("obs", "horiz")),
        P(("obs", "horiz")),
        P(("obs", "horiz")),
        P(None, ("obs", "horiz")),
        P(("obs", "horiz")),
    )
    out_specs = (P(None, "obs", "horiz"), P(("obs", "horiz")))
    return jax.shard_map(
        per_device, mesh=mesh, in_specs=in_specs, out_specs=out_specs, check_vma=False
    )
```
